256 devices in a mesh: gx: 64 (over z, x, core), gy: 4 (over y).
Axes of the slice: x: 4, y: 4, z: 8, core: 2. Of those that a mesh axis runs over, the one named last changes fastest.
Arguments:
- prior: float32 [128, 4096, 512], P(None, 'gx', 'gy'), may hold values from -6 to 6
- cond_x: int32 [4096, 512], P('gx', 'gy'), may hold values from 1 to 8
- cond_y: int32 [4096, 512], P('gx', 'gy'), may hold values from 1 to 8
- cap_level: int32 [4096, 512], P('gx', 'gy'), may hold values from 4 to 16
- decap: int32 [4096, 512], P('gx', 'gy'), may hold values 0 or 1
- via: int32 [4096, 512], P('gx', 'gy'), may hold values 0 or 1
- ports: int32 [64], replicated, may hold values from 0 to 2097151
Outputs:
- new_basis: float32 [64, 4096, 512], P(None, 'gx', 'gy')
- next_image: float32 [32, 4096, 512], P(None, 'gx', 'gy')
- g_columns: float32 [192, 64], replicated
- c_reduced: float32 [192, 192], replicated
- b_reduced: float32 [192, 64], replicated
The draws below stay inside these ranges and needn't reach their ends.
All inputs are finite; a program needn't handle non-finite values. No bound on the sum of `decap` or of `via` on one device may be relied on, other than what follows from the above.
Results may differ from the reference program's by a relative error of at most 0.00013.
Values sent between devices are 32-bit elements; how exact they have to be, the bound alone decides.
No kernel may reach another device: no remote copies, remote signals or barrier semaphores. Data moves between devices by JAX's collectives and lax.ppermute only.
A program may use at most 128 MiB of HBM per device.

```python
import jax
import jax.numpy as jnp
from jax import lax

B = 32
PRIOR = 128
PORTS = 64
NX = 4096
NY = 512
BASIS = 192


def draw_cap_level(key, part):
    key = jax.random.fold_in(key, 7)
    rows = lax.broadcasted_iota(jnp.int32, (NX, NY), 0)
    upper = 5 + 12 * rows // NX
    return jax.random.randint(key, (NX, NY), 4, upper + 1).astype(jnp.int32)


def with_ends(result, stream_key, low, top_value):
    index_at = [jax.random.randint(jax.random.fold_in(stream_key, axis), (), 0, length) for axis, length in enumerate(result.shape)]
    widest = result.shape.index(max(result.shape))
    beside = index_at[:widest] + [(index_at[widest] + 1) % result.shape[widest]] + index_at[widest + 1:]
    return result.at[tuple(index_at)].set(low).at[tuple(beside)].set(top_value)


def block_scale(stream_key, shape, pieces, low, top_value):
    def one(dim, blocks):
        heights = jax.random.uniform(jax.random.fold_in(jax.random.fold_in(stream_key, 6), dim), (blocks,), jnp.float32, low / len(pieces), top_value / len(pieces))
        return jnp.repeat(jnp.exp(heights), shape[dim] // blocks).reshape((-1,) + (1,) * (len(shape) - dim - 1))

    loudness = one(*pieces[0])
    for cut in pieces[1:]:
        loudness = loudness * one(*cut)
    return loudness


def bell_draw(key, shape, spread, limit, pieces=(), kind=jnp.bfloat16):
    drawn = spread * jax.random.normal(key, shape, jnp.float32)
    if pieces:
        drawn = drawn * block_scale(key, shape, pieces, -0.22, 0.18)
    return jnp.clip(drawn, -limit, limit).astype(kind)


def setup_inputs(seed: int = 0) -> dict:
    key_of = jax.random.split(jax.random.key(seed), 8)
    return {
        "prior": bell_draw(key_of[0], (PRIOR, NX, NY), 1.0, 6.0, ((1, 64), (2, 4)), jnp.float32),
        "cond_x": with_ends(jax.random.randint(key_of[1], (NX, NY), 1, 9), jax.random.fold_in(key_of[1], 1), 1, 8).astype(jnp.int32),
        "cond_y": with_ends(jax.random.randint(key_of[2], (NX, NY), 1, 9), jax.random.fold_in(key_of[2], 1), 1, 8).astype(jnp.int32),
        "cap_level": draw_cap_level(jax.random.fold_in(key_of[7], 71), 0),
        "decap": with_ends((jax.random.randint(key_of[4], (NX, NY), 0, 3) < 1).astype(jnp.int32), jax.random.fold_in(key_of[4], 1), 0, 1),
        "via": with_ends((jax.random.randint(key_of[5], (NX, NY), 0, 4) < 1).astype(jnp.int32), jax.random.fold_in(key_of[5], 1), 0, 1),
        "ports": with_ends(jax.random.randint(key_of[6], (PORTS,), 0, NX * NY), jax.random.fold_in(key_of[6], 1), 0, (NX * NY) - 1).astype(jnp.int32),
    }


def pair_products(left, right):
    left_flat = left.reshape(left.shape[0], -1)
    right_flat = right.reshape(right.shape[0], -1)
    return lax.dot_general(left_flat.astype(jnp.float32), right_flat.astype(jnp.float32), (((1,), (1,)), ((), ())), precision=lax.Precision.HIGHEST, preferred_element_type=jnp.float32)

def remove_span(work, coeffs, basis):
    basis_flat = basis.reshape(basis.shape[0], -1)
    along = lax.dot_general(coeffs.astype(jnp.float32), basis_flat.astype(jnp.float32), (((0,), (0,)), ((), ())), precision=lax.Precision.HIGHEST, preferred_element_type=jnp.float32)
    return work - along.reshape(work.shape)

def grid_apply(field, gxe, gye, gvia):
    gxw = jnp.pad(gxe, ((1, 0), (0, 0)))[:-1]
    gys = jnp.pad(gye, ((0, 0), (1, 0)))[:, :-1]
    padded = jnp.pad(field, ((0, 0), (1, 1), (1, 1)))
    east = padded[:, 2:, 1:-1]
    west = padded[:, :-2, 1:-1]
    north = padded[:, 1:-1, 2:]
    south = padded[:, 1:-1, :-2]
    center = gvia + gxe + gxw + gye + gys
    return center * field - gxe * east - gxw * west - gye * north - gys * south

def arnoldi_step(basis, block, gxe, gye, gvia, cap, scale):
    image = grid_apply(block, gxe, gye, gvia)
    work = image / cap
    first = pair_products(basis, work) * scale
    cleaned = remove_span(work, first, basis)
    second = pair_products(basis, cleaned) * scale
    cleaned = remove_span(cleaned, second, basis)
    gram = pair_products(cleaned, cleaned) * scale
    lower = jnp.linalg.cholesky(gram)
    flat = cleaned.reshape(cleaned.shape[0], -1)
    fresh = lax.linalg.triangular_solve(lower, flat, left_side=True, lower=True)
    return (fresh.reshape(cleaned.shape), image)

def reference(prior, cond_x, cond_y, cap_level, decap, via, ports):
    scale = 1.0 / (NX * NY)
    gxe = 0.125 * cond_x.astype(jnp.float32)
    gye = 0.125 * cond_y.astype(jnp.float32)
    gvia = 0.5 * via.astype(jnp.float32)
    cap = 0.25 * cap_level.astype(jnp.float32) * (1.0 + 2.0 * decap.astype(jnp.float32))
    first_block, unused = arnoldi_step(prior, prior[PRIOR - B:], gxe, gye, gvia, cap, scale)
    grown = jnp.concatenate([prior, first_block], axis=0)
    second_block, image_two = arnoldi_step(grown, first_block, gxe, gye, gvia, cap, scale)
    image_three = grid_apply(second_block, gxe, gye, gvia)
    next_image = image_three / cap
    whole = jnp.concatenate([grown, second_block], axis=0)
    g_columns = pair_products(whole, jnp.concatenate([image_two, image_three], axis=0)) * scale
    c_reduced = pair_products(whole, whole * cap) * scale
    b_reduced = jnp.take(whole.reshape(BASIS, -1), ports, axis=1)
    new_basis = jnp.concatenate([first_block, second_block], axis=0)
    return (new_basis, next_image, g_columns, c_reduced, b_reduced)
```

```python
import jax
import jax.numpy as jnp
from jax import lax
from jax.sharding import PartitionSpec as P

B = 32
PRIOR = 128
HI = lax.Precision.HIGHEST


def swap(x, axis, mask):
    return lax.ppermute(x, axis, [(i, i ^ mask) for i in range(lax.axis_size(axis))])


def quad_sum(parts):
    return (parts[0] + parts[1]) + (parts[2] + parts[3])


def sum_over_devices(x):
    rows = x.shape[0]
    core = lax.axis_index("gx") % 2
    half = rows // 2
    keep = lax.dynamic_slice_in_dim(x, core * half, half, 0)
    give = lax.dynamic_slice_in_dim(x, (1 - core) * half, half, 0)
    x = keep + swap(give, "gx", 1)
    me = lax.axis_index("gy")
    quarter = half // 4
    parts = [
        lax.dynamic_slice_in_dim(x, (me ^ m) * quarter, quarter, 0) for m in range(4)
    ]
    got = [parts[0]] + [swap(parts[m], "gy", m) for m in (1, 2, 3)]
    x = quad_sum(got)
    for m in (2, 4, 8, 16, 32):
        x = x + swap(x, "gx", m)
    whole = jnp.zeros((half, x.shape[1]), x.dtype)
    for m in range(4):
        piece = x if m == 0 else swap(x, "gy", m)
        whole = lax.dynamic_update_slice_in_dim(whole, piece, (me ^ m) * quarter, 0)
    other = swap(whole, "gx", 1)
    low = jnp.where(core == 0, whole, other)
    high = jnp.where(core == 0, other, whole)
    return jnp.concatenate([low, high], axis=0)


def halo(x, axis, dim):
    size, length = lax.axis_size(axis), x.shape[dim]
    up = [(i, i + 1) for i in range(size - 1)]
    down = [(j, i) for i, j in up]
    before = lax.ppermute(lax.slice_in_dim(x, length - 1, length, axis=dim), axis, up)
    after = lax.ppermute(lax.slice_in_dim(x, 0, 1, axis=dim), axis, down)
    return before, after


def apply_grid(v, gxe, gye, gxw, gys, center):
    above, below = halo(v, "gx", 1)
    left, right = halo(v, "gy", 2)
    east = jnp.concatenate([v[:, 1:], below], axis=1)
    west = jnp.concatenate([above, v[:, :-1]], axis=1)
    north = jnp.concatenate([v[:, :, 1:], right], axis=2)
    south = jnp.concatenate([left, v[:, :, :-1]], axis=2)
    return center * v - gxe * east - gxw * west - gye * north - gys * south


def flat(x):
    return x.reshape(x.shape[0], -1)


def products(a, b):
    return lax.dot_general(
        a, b, (((1,), (1,)), ((), ())), precision=HI, preferred_element_type=jnp.float32
    )


def mm(a, b):
    return jnp.dot(a, b, precision=HI, preferred_element_type=jnp.float32)


def clean(basis, work, gram):
    k = mm(basis.T, mm(gram, basis))
    gw = mm(gram, work)
    h = mm(basis.T, gw)
    c = 2.0 * h - mm(k, h)
    ch = mm(c.T, h)
    s = mm(work.T, gw) - ch - ch.T + mm(c.T, mm(k, c))
    lower = jnp.linalg.cholesky(0.5 * (s + s.T))
    rest = work - mm(basis, c)
    return lax.linalg.triangular_solve(lower, rest.T, left_side=True, lower=True).T


def on_device(prior, cond_x, cond_y, cap_level, decap, via, ports):
    rows_here, cols_here = prior.shape[1:]
    total_cols = cols_here * lax.axis_size("gy")
    scale = 1.0 / (rows_here * lax.axis_size("gx") * total_cols)
    gxe = 0.125 * cond_x.astype(jnp.float32)
    gye = 0.125 * cond_y.astype(jnp.float32)
    gvia = 0.5 * via.astype(jnp.float32)
    cap = 0.25 * cap_level.astype(jnp.float32) * (1.0 + 2.0 * decap.astype(jnp.float32))
    gxw = jnp.concatenate([halo(gxe, "gx", 0)[0], gxe[:-1]], axis=0)
    gys = jnp.concatenate([halo(gye, "gy", 1)[0], gye[:, :-1]], axis=1)
    center = gvia + gxe + gxw + gye + gys
    coef = (gxe, gye, gxw, gys, center)
    gp = apply_grid(prior, *coef)
    y = gp / cap
    gy_ = apply_grid(y, *coef)
    ay = gy_ / cap
    x = ay[PRIOR - B :]
    gx_ = apply_grid(x, *coef)
    ax = gx_ / cap

    p_f, y_f, x_f = flat(prior), flat(y), flat(x)
    w_f = jnp.concatenate([p_f, y_f, x_f], axis=0)
    gy_f, gx_f, gp_f = flat(gy_), flat(gx_), flat(gp)
    unit = products(w_f, w_f)
    pcp = products(p_f, flat(prior * cap))
    pgp_ygp = products(jnp.concatenate([p_f, y_f], axis=0), gp_f)
    ygy = products(y_f, gy_f)
    gx_cols = products(jnp.concatenate([y_f, x_f], axis=0), gx_f)

    port_rows = ports // total_cols - lax.axis_index("gx") * rows_here
    port_cols = ports % total_cols - lax.axis_index("gy") * cols_here
    inside = (
        (port_rows >= 0) & (port_rows < rows_here) & (port_cols >= 0) & (port_cols < cols_here)
    )
    index = jnp.clip(port_rows, 0, rows_here - 1) * cols_here + jnp.clip(
        port_cols, 0, cols_here - 1
    )
    picked = jnp.take(w_f, index, axis=1) * inside.astype(jnp.float32)[None, :]

    pack = [
        unit[:, :128],
        unit[128:, 128:256],
        jnp.pad(jnp.concatenate([unit[256:, 256:], gx_cols[128:]], axis=1), ((0, 0), (0, 64))),
        pcp,
        pgp_ygp,
        ygy,
        jnp.concatenate([gx_cols[:128], jnp.zeros((128, 96), jnp.float32)], axis=1),
        jnp.pad(picked, ((0, 0), (0, 64))),
    ]
    sizes = [part.shape[0] for part in pack]
    total = sum(sizes)
    pad = -total % 64
    stacked = jnp.concatenate(pack + [jnp.zeros((pad, 128), jnp.float32)], axis=0)
    summed = sum_over_devices(stacked)
    ends = []
    at = 0
    for size in sizes:
        ends.append(summed[at : at + size])
        at += size
    col_p, col_y, tail, pcp, pgp_ygp, ygy, gx_cols, picked = ends
    picked = picked[:, :64]
    pp, yp, xp = col_p[:128], col_p[128:256], col_p[256:]
    yy, xy = col_y[:128], col_y[128:]
    xx, xgx = tail[:, :32], tail[:, 32:64]
    pgp, ycy = pgp_ygp[:128], pgp_ygp[128:]
    ygx = gx_cols[:, :32]

    def blocks(rows):
        return jnp.concatenate([jnp.concatenate(r, axis=1) for r in rows], axis=0)

    unit = blocks([[pp, yp.T, xp.T], [yp, yy, xy.T], [xp, xy, xx]]) * scale
    pcx, ycx, xcx = ycy[:, 96:], ygy[:, 96:], ygx[96:]
    capm = blocks([[pcp, pgp, pcx], [pgp.T, ycy, ycx], [pcx.T, ycx.T, xcx]]) * scale
    gm = blocks([[pgp, ycy, ycx], [ycy, ygy, ygx], [ycx.T, ygx.T, xgx]]) * scale
    eye = jnp.eye(288, dtype=jnp.float32)
    e_p = eye[:, :128]
    t1 = clean(e_p, eye[:, 224:256], unit)
    w2 = jnp.concatenate([jnp.zeros((128, B), jnp.float32), t1[:128], t1[224:256]], axis=0)
    t2 = clean(jnp.concatenate([e_p, t1], axis=1), w2, unit)
    v = jnp.concatenate([e_p, t1, t2], axis=1)
    g_columns = mm(v.T, jnp.concatenate([mm(capm, w2), mm(gm, t2)], axis=1))
    c_reduced = mm(v.T, mm(capm, v))
    b_reduced = mm(v.T, picked)
    t12 = jnp.concatenate([t1, t2], axis=1)
    new_basis = mm(t12.T, w_f).reshape((2 * B,) + prior.shape[1:])
    aw_f = jnp.concatenate([y_f, flat(ay), flat(ax)], axis=0)
    next_image = mm(t2.T, aw_f).reshape((B,) + prior.shape[1:])
    return (new_basis, next_image, g_columns, c_reduced, b_reduced)


def solution(mesh):
    in_specs = (
        P(None, "gx", "gy"),
        P("gx", "gy"),
        P("gx", "gy"),
        P("gx", "gy"),
        P("gx", "gy"),
        P("gx", "gy"),
        P(),
    )
    out_specs = (P(None, "gx", "gy"), P(None, "gx", "gy"), P(), P(), P())
    return jax.shard_map(
        on_device, mesh=mesh, in_specs=in_specs, out_specs=out_specs, check_vma=False
    )
```

```python
import jax
import jax.numpy as jnp
from jax import lax
from jax.experimental import pallas as pl
from jax.experimental.pallas import tpu as pltpu
from jax.sharding import PartitionSpec as P

B = 32
PRIOR = 128
F32 = jnp.float32
HI = lax.Precision.HIGHEST
VMEM_LIMIT = 48 * 1024 * 1024
FIELDS = 32
DEPTH = 8


def call(kernel, out, grid, in_specs, out_specs, scratch=(), flops=0, moved=0):
    return pl.pallas_call(
        kernel,
        out_shape=out,
        grid_spec=pltpu.PrefetchScalarGridSpec(
            num_scalar_prefetch=0,
            grid=grid,
            in_specs=in_specs,
            out_specs=out_specs,
            scratch_shapes=scratch,
        ),
        compiler_params=pltpu.CompilerParams(vmem_limit_bytes=VMEM_LIMIT),
        cost_estimate=pl.CostEstimate(flops=flops, bytes_accessed=moved, transcendentals=0),
    )


def shape(*dims):
    return jax.ShapeDtypeStruct(dims, F32)


def lanes_of(dims):
    return lax.broadcasted_iota(jnp.int32, dims, len(dims) - 1)


def note_edge(edge, v, r, lane):
    return jnp.where(lane // 2 == r, pltpu.roll(v, 2 * r + 1, 1), edge)


def regroup_kernel(p_ref, out_ref, top_ref, low_ref, edge_ref):
    fields, rows, width = p_ref.shape
    flat = p_ref.reshape(fields * rows, width)
    lane = lanes_of((fields, width))

    def step(r, edge):
        v = flat[pl.ds(r, fields, stride=rows), :]
        out_ref[r] = v
        return note_edge(edge, v, r, lane)

    edge_ref[...] = lax.fori_loop(0, rows, step, jnp.zeros((fields, width), F32), unroll=8)
    top_ref[...] = out_ref[0]
    low_ref[...] = out_ref[rows - 1]


def regroup(prior):
    fields, rows, width = prior.shape
    side = pl.BlockSpec((FIELDS, width), lambda i: (i, 0))
    return call(
        regroup_kernel,
        (shape(rows, fields, width),) + (shape(fields, width),) * 3,
        (fields // FIELDS,),
        [pl.BlockSpec((FIELDS, rows, width), lambda i: (i, 0, 0))],
        (pl.BlockSpec((rows, FIELDS, width), lambda i: (0, i, 0)), side, side, side),
        flops=0,
        moved=2 * prior.size * 4,
    )(prior)


def stencil_rows(coef_ref, v_ref, above, below, from_left, from_right, put):
    rows, fields, width = v_ref.shape
    lane = lanes_of((fields, width))
    seam = jnp.where(
        lane % 2 == 1, pltpu.roll(from_left, 1, 1), pltpu.roll(from_right, width - 1, 1)
    )

    def one(r, up, v, down, edge):
        side = pltpu.roll(seam, width - 1 - 2 * r, 1)
        south = jnp.where(lane == 0, side, pltpu.roll(v, 1, 1))
        north = jnp.where(lane == width - 1, side, pltpu.roll(v, width - 1, 1))

        def row(k):
            return coef_ref[k, pl.ds(r, 1), :]

        image = row(0) * v - row(1) * down - row(2) * up - row(3) * north - row(4) * south
        y = image * row(5)
        put(r, y, image)
        return note_edge(edge, y, r, lane)

    edge = jnp.zeros((fields, width), F32)
    edge = one(0, above, v_ref[0], v_ref[1], edge)
    edge = lax.fori_loop(
        1,
        rows - 1,
        lambda r, e: one(r, v_ref[r - 1], v_ref[r], v_ref[r + 1], e),
        edge,
        unroll=2,
    )
    return one(rows - 1, v_ref[rows - 2], v_ref[rows - 1], below, edge)


def stencil_kernel(
    coef_ref, v_ref, above_ref, below_ref, fl_ref, fr_ref, y_ref, top_ref, low_ref, edge_ref
):
    def put(r, y, image):
        y_ref[r] = y

    edge_ref[...] = stencil_rows(
        coef_ref, v_ref, above_ref[...], below_ref[...], fl_ref[...], fr_ref[...], put
    )
    top_ref[...] = y_ref[0]
    low_ref[...] = y_ref[y_ref.shape[0] - 1]


def stencil(coef, v, above, below, from_left, from_right):
    rows, fields, width = v.shape
    side = pl.BlockSpec((FIELDS, width), lambda i: (i, 0))
    block = pl.BlockSpec((rows, FIELDS, width), lambda i: (0, i, 0))
    return call(
        stencil_kernel,
        (shape(rows, fields, width),) + (shape(fields, width),) * 3,
        (fields // FIELDS,),
        [pl.BlockSpec(coef.shape, lambda i: (0, 0, 0)), block, side, side, side, side],
        (block, side, side, side),
        flops=12 * v.size,
        moved=2 * v.size * 4,
    )(coef, v, above, below, from_left, from_right)


def wide(ref, start=0):
    return jnp.concatenate([ref[i, start:, :] for i in range(ref.shape[0])], axis=1)


def wide_row(ref):
    return jnp.concatenate([ref[i : i + 1, :] for i in range(ref.shape[0])], axis=1)


def halves(x):
    high = x.astype(jnp.bfloat16)
    low = (x - high.astype(F32)).astype(jnp.bfloat16)
    return jnp.concatenate([high, low], axis=0)


def nt(a, b):
    return lax.dot_general(a, b, (((1,), (1,)), ((), ())), preferred_element_type=F32)


def fold(acc, row, rows, col, cols):
    a = acc[row : row + rows, col : col + cols] + acc[row : row + rows, col + cols : col + 2 * cols]
    row += rows
    b = acc[row : row + rows, col : col + cols] + acc[row : row + rows, col + cols : col + 2 * cols]
    return a + b


def accumulate(acc_ref, term):
    @pl.when(pl.program_id(0) == 0)
    def _():
        acc_ref[...] = term

    @pl.when(pl.program_id(0) > 0)
    def _():
        acc_ref[...] += term


def at_end(fn):
    pl.when(pl.program_id(0) == pl.num_programs(0) - 1)(fn)


def gram_p_kernel(cap_ref, p_ref, pp_ref, pcp_ref, acc_ref):
    p = wide(p_ref)
    hp = halves(p)
    hc = halves(p * wide_row(cap_ref))
    accumulate(acc_ref, nt(hp, jnp.concatenate([hp, hc], axis=0)))

    @at_end
    def _():
        pp_ref[...] = fold(acc_ref, 0, 128, 0, 128)
        pcp_ref[...] = fold(acc_ref, 0, 128, 256, 128)


def gram_y_kernel(cap_ref, p_ref, y_ref, py_ref, yy_ref, pgp_ref, ygp_ref, acc_ref):
    y = wide(y_ref)
    hp = halves(wide(p_ref))
    hy = halves(y)
    hg = halves(y * wide_row(cap_ref))
    left = jnp.concatenate([hp, hy], axis=0)
    right = jnp.concatenate([hy, hg], axis=0)
    accumulate(acc_ref, nt(left, right))

    @at_end
    def _():
        py_ref[...] = fold(acc_ref, 0, 128, 0, 128)
        yy_ref[...] = fold(acc_ref, 256, 128, 0, 128)
        pgp_ref[...] = fold(acc_ref, 0, 128, 256, 128)
        ygp_ref[...] = fold(acc_ref, 256, 128, 256, 128)


def gram_x_kernel(cap_ref, p_ref, y_ref, a_ref, ygy_ref, x_ref, acc_ref, accx_ref):
    ay = wide(a_ref)
    hp = halves(wide(p_ref))
    hy = halves(wide(y_ref))
    hg = halves(ay * wide_row(cap_ref))
    hx = halves(ay[PRIOR - B :])
    accumulate(acc_ref, nt(hy, hg))
    accumulate(accx_ref, nt(jnp.concatenate([hp, hy, hg, hx], axis=0), hx))

    @at_end
    def _():
        ygy_ref[...] = fold(acc_ref, 0, 128, 0, 128)
        px = fold(accx_ref, 0, 128, 0, B)
        yx = fold(accx_ref, 256, 128, 0, B)
        gx = fold(accx_ref, 512, 128, 0, B)
        xx = fold(accx_ref, 768, B, 0, B)
        last = jnp.concatenate([xx, jnp.zeros((128 - B, B), F32)], axis=0)
        x_ref[...] = jnp.concatenate([px, yx, gx, last], axis=1)


def gram(kernel, cap, arrays, n_out, acc_shapes, flops):
    rows, fields, width = arrays[0].shape
    block = pl.BlockSpec((DEPTH, fields, width), lambda i: (i, 0, 0))
    whole = pl.BlockSpec((128, 128), lambda i: (0, 0))
    return call(
        kernel,
        (shape(128, 128),) * n_out,
        (rows // DEPTH,),
        [pl.BlockSpec((DEPTH, width), lambda i: (i, 0))] + [block] * len(arrays),
        (whole,) * n_out,
        scratch=[pltpu.VMEM(s, F32) for s in acc_shapes],
        flops=flops,
        moved=len(arrays) * arrays[0].size * 4,
    )(cap, *arrays)


def pick_kernel(where_ref, p_ref, y_ref, a_ref, py_ref, x_ref, buf_ref, sem):
    py_ref[...] = jnp.zeros_like(py_ref)
    x_ref[...] = jnp.zeros_like(x_ref)
    n = where_ref.shape[1]

    def step(k, carry):
        @pl.when(where_ref[2, k] > 0)
        def _():
            r, c = where_ref[0, k], where_ref[1, k]
            for ref, first, lanes, out_ref in (
                (p_ref, 0, 0, py_ref),
                (y_ref, 0, n, py_ref),
                (a_ref, PRIOR - B, 0, x_ref),
            ):
                copy = pltpu.make_async_copy(ref.at[r], buf_ref, sem)
                copy.start()
                copy.wait()
                v = buf_ref[first:, :]
                lane = lanes_of(v.shape)
                spot = k + lanes
                moved = pltpu.roll(v, lax.rem(spot - c + 128, 128), 1)
                out_ref[...] = jnp.where(lane == spot, moved, out_ref[...])

        return carry

    lax.fori_loop(0, n, step, 0)


def pick(where, p, y, ay):
    any_spec = pl.BlockSpec(memory_space=pl.ANY)
    return pl.pallas_call(
        pick_kernel,
        out_shape=(shape(128, 128), shape(B, 128)),
        in_specs=[pl.BlockSpec(memory_space=pltpu.SMEM), any_spec, any_spec, any_spec],
        out_specs=(pl.BlockSpec(memory_space=pltpu.VMEM),) * 2,
        scratch_shapes=[pltpu.VMEM((128, 128), F32), pltpu.SemaphoreType.DMA],
        compiler_params=pltpu.CompilerParams(vmem_limit_bytes=VMEM_LIMIT),
        cost_estimate=pl.CostEstimate(flops=0, bytes_accessed=1 << 20, transcendentals=0),
    )(where, p, y, ay)


def last_kernel(
    coef_ref, a_ref, above_ref, below_ref, fl_ref, fr_ref,
    pp_ref, pcp_ref, py_ref, yy_ref, pgp_ref, ygp_ref, ygy_ref, x_ref, kp_ref, kx_ref,
    ax_ref, pack_ref, image_ref,
):
    def put(r, y, image):
        ax_ref[r] = y
        image_ref[r] = image

    stencil_rows(coef_ref, a_ref, above_ref[...], below_ref[...], fl_ref[...], fr_ref[...], put)
    acc = jnp.zeros((2 * B, 2 * B), F32)
    for at in range(0, a_ref.shape[0], 16):
        hx = halves(jnp.concatenate([a_ref[at + i] for i in range(16)], axis=1))
        hg = halves(jnp.concatenate([image_ref[at + i] for i in range(16)], axis=1))
        acc = acc + nt(hx, hg)
    xgx = fold(acc, 0, B, 0, B)
    row = lax.broadcasted_iota(jnp.int32, (128, 128), 0)
    col = lax.broadcasted_iota(jnp.int32, (128, 128), 1)

    def diagonal(m):
        return jnp.sum(jnp.where(row == col, m, 0.0), axis=0, keepdims=True)

    pack_ref[0:128] = jnp.where(row <= col, pp_ref[...], pcp_ref[...])
    pack_ref[128:256] = jnp.where(row <= col, pgp_ref[...], ygy_ref[...])
    pack_ref[256:384] = jnp.where(row <= col, yy_ref[...], ygp_ref[...])
    pack_ref[384:512] = py_ref[...]
    pack_ref[512:640] = x_ref[...]
    pack_ref[640:768] = kp_ref[...]
    pack_ref[768:800] = kx_ref[...]
    pack_ref[800:832] = jnp.concatenate([xgx, jnp.zeros((B, 128 - B), F32)], axis=1)
    diag = [diagonal(m[...]) for m in (pcp_ref, ygy_ref, ygp_ref)]
    pack_ref[832:840] = jnp.concatenate(diag + [jnp.zeros((5, 128), F32)], axis=0)
    pack_ref[840:896] = jnp.zeros((56, 128), F32)


def last(coef, ay, sides, mats):
    rows, fields, width = ay.shape
    vm = pl.BlockSpec(memory_space=pltpu.VMEM)
    full = lambda a: pl.BlockSpec(a.shape, lambda i: (0,) * a.ndim)
    return call(
        last_kernel,
        (shape(rows, B, width), shape(896, 128)),
        (1,),
        [full(coef), pl.BlockSpec((rows, B, width), lambda i: (0, fields // B - 1, 0))]
        + [full(a) for a in sides]
        + [full(a) for a in mats],
        (
            pl.BlockSpec((rows, B, width), lambda i: (0, 0, 0)),
            pl.BlockSpec((896, 128), lambda i: (0, 0)),
        ),
        scratch=[pltpu.VMEM((rows, B, width), F32)],
        flops=1 << 27,
        moved=2 * rows * B * width * 4,
    )(coef, ay, *sides, *mats)


def combine_kernel(t_ref, p_ref, y_ref, a_ref, ax_ref, q_ref, n_ref):
    th = t_ref[...].astype(jnp.bfloat16)
    tl = (t_ref[...] - th.astype(F32)).astype(jnp.bfloat16)
    both = jnp.concatenate([th, tl], axis=0)
    two = 2 * B

    def split(x):
        high = x.astype(jnp.bfloat16)
        return high, (x - high.astype(F32)).astype(jnp.bfloat16)

    def mm(a, b):
        return jnp.dot(a, b, preferred_element_type=F32)

    def times(lhs_both, lhs_high, pair):
        rows = lhs_high.shape[0]
        big = mm(lhs_both, pair[0])
        return big[:rows] + big[rows:] + mm(lhs_high, pair[1])

    fields, width = p_ref.shape[1:]
    for j in range(0, DEPTH, 2):
        get = lambda ref: jnp.concatenate([ref[j], ref[j + 1]], axis=1)
        p, y, a, ax = (get(ref) for ref in (p_ref, y_ref, a_ref, ax_ref))
        py = split(jnp.concatenate([p, y], axis=0))
        x = split(a[PRIOR - B :])
        yr = (py[0][PRIOR:], py[1][PRIOR:])
        rest = split(jnp.concatenate([a, ax], axis=0))
        def cut(lo, hi, rows):
            high = th[rows[0] : rows[1], lo:hi]
            return jnp.concatenate([high, tl[rows[0] : rows[1], lo:hi]], axis=0), high

        q = times(*cut(0, 256, (0, two)), py) + times(*cut(256, 288, (0, two)), x)
        n = times(*cut(0, 128, (B, two)), yr) + times(*cut(128, 288, (B, two)), rest)
        for k in (0, 1):
            q_ref.reshape(two * DEPTH, width)[pl.ds(j + k, two, stride=DEPTH), :] = q[
                :, k * width : (k + 1) * width
            ]
            n_ref.reshape(B * DEPTH, width)[pl.ds(j + k, B, stride=DEPTH), :] = n[
                :, k * width : (k + 1) * width
            ]


def combine(t, p, y, ay, ax):
    rows, fields, width = p.shape
    block = pl.BlockSpec((DEPTH, fields, width), lambda i: (i, 0, 0))
    return call(
        combine_kernel,
        (shape(2 * B, rows, width), shape(B, rows, width)),
        (rows // DEPTH,),
        [
            pl.BlockSpec(t.shape, lambda i: (0, 0)),
            block,
            block,
            block,
            pl.BlockSpec((DEPTH, B, width), lambda i: (i, 0, 0)),
        ],
        (
            pl.BlockSpec((2 * B, DEPTH, width), lambda i: (0, i, 0)),
            pl.BlockSpec((B, DEPTH, width), lambda i: (0, i, 0)),
        ),
        flops=3 * 2 * 96 * 288 * rows * width,
        moved=5 * p.size * 4,
    )(t, p, y, ay, ax)


def swap(x, axis, mask):
    return lax.ppermute(x, axis, [(i, i ^ mask) for i in range(lax.axis_size(axis))])


def shift(x, axis, step):
    size = lax.axis_size(axis)
    return lax.ppermute(
        x, axis, [(i, i + step) for i in range(size) if 0 <= i + step < size]
    )


def quad_sum(parts):
    return (parts[0] + parts[1]) + (parts[2] + parts[3])


def sum_over_devices(x):
    rows = x.shape[0]
    core = lax.axis_index("gx") % 2
    half = rows // 2
    keep = lax.dynamic_slice_in_dim(x, core * half, half, 0)
    give = lax.dynamic_slice_in_dim(x, (1 - core) * half, half, 0)
    x = keep + swap(give, "gx", 1)
    me = lax.axis_index("gy")
    quarter = half // 4
    parts = [
        lax.dynamic_slice_in_dim(x, (me ^ m) * quarter, quarter, 0) for m in range(4)
    ]
    got = [parts[0]] + [swap(parts[m], "gy", m) for m in (1, 2, 3)]
    x = quad_sum(got)
    mask = 2
    while mask < lax.axis_size("gx"):
        x = x + swap(x, "gx", mask)
        mask *= 2
    whole = jnp.zeros((half, x.shape[1]), x.dtype)
    for m in range(4):
        piece = x if m == 0 else swap(x, "gy", m)
        whole = lax.dynamic_update_slice_in_dim(whole, piece, (me ^ m) * quarter, 0)
    other = swap(whole, "gx", 1)
    low = jnp.where(core == 0, whole, other)
    high = jnp.where(core == 0, other, whole)
    return jnp.concatenate([low, high], axis=0)


def exchange(top, low, edge, edge_left):
    return (
        shift(low, "gx", 1),
        shift(top, "gx", -1),
        shift(edge, "gy", 1),
        shift(edge_left, "gy", -1),
    )


def mm(a, b):
    return jnp.dot(a, b, precision=HI, preferred_element_type=F32)


def clean(basis, work, gram_matrix):
    k = mm(basis.T, mm(gram_matrix, basis))
    gw = mm(gram_matrix, work)
    h = mm(basis.T, gw)
    c = 2.0 * h - mm(k, h)
    ch = mm(c.T, h)
    s = mm(work.T, gw) - ch - ch.T + mm(c.T, mm(k, c))
    lower = jnp.linalg.cholesky(0.5 * (s + s.T))
    rest = work - mm(basis, c)
    return lax.linalg.triangular_solve(lower, rest.T, left_side=True, lower=True).T


def algebra(summed, scale):
    tri = jnp.arange(128)[:, None] - jnp.arange(128)[None, :]
    diags = summed[832:835]

    def upper(m):
        return jnp.where(tri <= 0, m, m.T)

    def below(m, d):
        return jnp.where(tri > 0, m, jnp.where(tri < 0, m.T, d[None, :]))

    m0, m1, m2 = summed[0:128], summed[128:256], summed[256:384]
    pp, pcp = upper(m0), below(m0, diags[0])
    pgp, ygy = upper(m1), below(m1, diags[1])
    yy, ycy = upper(m2), below(m2, diags[2])
    py = summed[384:512]
    xs = summed[512:640]
    px, yx, ygx, xx = xs[:, :32], xs[:, 32:64], xs[:, 64:96], xs[:B, 96:]
    xgx = summed[800:832, :B]
    kp, kx = summed[640:768], summed[768:800]
    picked = jnp.concatenate([kp[:, :64], kp[:, 64:], kx[:, :64]], axis=0)

    def blocks(rows):
        return jnp.concatenate([jnp.concatenate(r, axis=1) for r in rows], axis=0)

    unit = blocks([[pp, py, px], [py.T, yy, yx], [px.T, yx.T, xx]]) * scale
    pcx, ycx, xcx = ycy[:, 96:], ygy[:, 96:], ygx[96:]
    capm = blocks([[pcp, pgp, pcx], [pgp.T, ycy, ycx], [pcx.T, ycx.T, xcx]]) * scale
    gm = blocks([[pgp, ycy, ycx], [ycy, ygy, ygx], [ycx.T, ygx.T, xgx]]) * scale
    eye = jnp.eye(288, dtype=F32)
    e_p = eye[:, :128]
    t1 = clean(e_p, eye[:, 224:256], unit)
    w2 = jnp.concatenate([jnp.zeros((128, B), F32), t1[:128], t1[224:256]], axis=0)
    t2 = clean(jnp.concatenate([e_p, t1], axis=1), w2, unit)
    v = jnp.concatenate([e_p, t1, t2], axis=1)
    g_columns = mm(v.T, jnp.concatenate([mm(capm, w2), mm(gm, t2)], axis=1))
    c_reduced = mm(v.T, mm(capm, v))
    b_reduced = mm(v.T, picked)
    return jnp.concatenate([t1, t2], axis=1).T, g_columns, c_reduced, b_reduced


def on_device(prior, cond_x, cond_y, cap_level, decap, via, ports):
    rows_here, cols_here = prior.shape[1:]
    total_cols = cols_here * lax.axis_size("gy")
    scale = 1.0 / (rows_here * lax.axis_size("gx") * total_cols)
    gxe = 0.125 * cond_x.astype(F32)
    gye = 0.125 * cond_y.astype(F32)
    gvia = 0.5 * via.astype(F32)
    cap = 0.25 * cap_level.astype(F32) * (1.0 + 2.0 * decap.astype(F32))

    p, top, low, edge = regroup(prior)
    slot = 2 * jnp.arange(rows_here)[:, None] == jnp.arange(cols_here)[None, :]
    gye_edge = jnp.sum(jnp.where(slot, gye[:, -1:], 0.0), axis=0, keepdims=True)
    spare = jnp.zeros((7, cols_here), F32)
    low = jnp.concatenate([low, gxe[-1:], spare], axis=0)
    edge_more = jnp.concatenate([edge, gye_edge, spare], axis=0)
    above, below, fl, fr = exchange(top, low, edge_more, edge)
    gxw = jnp.concatenate([above[PRIOR : PRIOR + 1], gxe[:-1]], axis=0)
    gys_first = jnp.sum(jnp.where(slot, fl[PRIOR : PRIOR + 1], 0.0), axis=1, keepdims=True)
    gys = jnp.concatenate([gys_first, gye[:, :-1]], axis=1)
    center = gvia + gxe + gxw + gye + gys
    coef = jnp.stack([center, gxe, gxw, gye, gys, 1.0 / cap])

    unit = 2 * 128 * 128 * rows_here * cols_here
    pp, pcp = gram(gram_p_kernel, cap, [p], 2, [(256, 512)], 8 * unit)
    y, top, low, edge = stencil(coef, p, above[:PRIOR], below, fl[:PRIOR], fr)
    sides = exchange(top, low, edge, edge)
    py, yy, pgp, ygp = gram(gram_y_kernel, cap, [p, y], 4, [(512, 512)], 16 * unit)
    ay, top, low, edge = stencil(coef, y, *sides)
    top, low, edge = (a[PRIOR - B :] for a in (top, low, edge))
    sides = exchange(top, low, edge, edge)
    ygy, xs = gram(gram_x_kernel, cap, [p, y, ay], 2, [(256, 256), (832, 64)], 8 * unit)

    port_rows = ports // total_cols - lax.axis_index("gx") * rows_here
    port_cols = ports % total_cols - lax.axis_index("gy") * cols_here
    inside = (
        (port_rows >= 0) & (port_rows < rows_here) & (port_cols >= 0) & (port_cols < cols_here)
    )
    where = jnp.stack(
        [
            jnp.clip(port_rows, 0, rows_here - 1),
            jnp.clip(port_cols, 0, cols_here - 1),
            inside.astype(jnp.int32),
        ]
    )
    kp, kx = pick(where, p, y, ay)
    ax, pack = last(coef, ay, sides, [pp, pcp, py, yy, pgp, ygp, ygy, xs, kp, kx])
    t, g_columns, c_reduced, b_reduced = algebra(sum_over_devices(pack), scale)
    new_basis, next_image = combine(t, p, y, ay, ax)
    return (new_basis, next_image, g_columns, c_reduced, b_reduced)


def solution(mesh):
    in_specs = (
        P(None, "gx", "gy"),
        P("gx", "gy"),
        P("gx", "gy"),
        P("gx", "gy"),
        P("gx", "gy"),
        P("gx", "gy"),
        P(),
    )
    out_specs = (P(None, "gx", "gy"), P(None, "gx", "gy"), P(), P(), P())
    return jax.shard_map(
        on_device, mesh=mesh, in_specs=in_specs, out_specs=out_specs, check_vma=False
    )
```

```python
import functools

import jax
import jax.numpy as jnp
from jax import lax
from jax.experimental import pallas as pl
from jax.experimental.pallas import tpu as pltpu
from jax.sharding import PartitionSpec as P

B = 32
PRIOR = 128
F32 = jnp.float32
HI = lax.Precision.HIGHEST
VMEM_LIMIT = 60 * 1024 * 1024
FIELDS = 32
DEPTH = 8
PACK = 832


def call(kernel, out, grid, in_specs, out_specs, scratch=(), flops=0, moved=0):
    return pl.pallas_call(
        kernel,
        out_shape=out,
        grid_spec=pltpu.PrefetchScalarGridSpec(
            num_scalar_prefetch=0,
            grid=grid,
            in_specs=in_specs,
            out_specs=out_specs,
            scratch_shapes=scratch,
        ),
        compiler_params=pltpu.CompilerParams(vmem_limit_bytes=VMEM_LIMIT),
        cost_estimate=pl.CostEstimate(flops=flops, bytes_accessed=moved, transcendentals=0),
    )


def shape(*dims):
    return jax.ShapeDtypeStruct(dims, F32)


def lanes_of(dims):
    return lax.broadcasted_iota(jnp.int32, dims, len(dims) - 1)


def note_edge(edge, v, r, lane):
    return jnp.where(lane // 2 == r, pltpu.roll(v, 2 * r + 1, 1), edge)


def regroup_kernel(p_ref, out_ref, top_ref, low_ref, edge_ref):
    fields, rows, width = p_ref.shape
    flat = p_ref.reshape(fields * rows, width)
    lane = lanes_of((fields, width))

    edge = jnp.zeros((fields, width), F32)
    for r in range(rows):
        v = flat[pl.ds(r, fields, stride=rows), :]
        out_ref[r] = v
        edge = note_edge(edge, v, r, lane)
    edge_ref[...] = edge
    top_ref[...] = out_ref[0]
    low_ref[...] = out_ref[rows - 1]


def regroup(prior):
    fields, rows, width = prior.shape
    side = pl.BlockSpec((FIELDS, width), lambda i: (i, 0))
    return call(
        regroup_kernel,
        (shape(rows, fields, width),) + (shape(fields, width),) * 3,
        (fields // FIELDS,),
        [pl.BlockSpec((FIELDS, rows, width), lambda i: (i, 0, 0))],
        (pl.BlockSpec((rows, FIELDS, width), lambda i: (0, i, 0)), side, side, side),
        flops=0,
        moved=2 * prior.size * 4,
    )(prior)


def stencil_rows(coef_ref, v_ref, above, below, from_left, from_right, put):
    rows, fields, width = v_ref.shape
    lane = lanes_of((fields, width))
    seam = jnp.where(
        lane % 2 == 1, pltpu.roll(from_left, 1, 1), pltpu.roll(from_right, width - 1, 1)
    )

    def one(r, up, v, down, edge):
        side = pltpu.roll(seam, width - 1 - 2 * r, 1)
        south = jnp.where(lane == 0, side, pltpu.roll(v, 1, 1))
        north = jnp.where(lane == width - 1, side, pltpu.roll(v, width - 1, 1))

        def row(k):
            return coef_ref[k, r : r + 1, :]

        image = row(0) * v - row(1) * down - row(2) * up - row(3) * north - row(4) * south
        y = image * row(5)
        put(r, y, image)
        return note_edge(edge, y, r, lane)

    edge = jnp.zeros((fields, width), F32)
    up, v = above, v_ref[0]
    for r in range(rows):
        down = v_ref[r + 1] if r + 1 < rows else below
        edge = one(r, up, v, down, edge)
        up, v = v, down
    return edge


def stencil_kernel(
    coef_ref, v_ref, above_ref, below_ref, fl_ref, fr_ref, y_ref, top_ref, low_ref, edge_ref
):
    def put(r, y, image):
        y_ref[r] = y

    edge_ref[...] = stencil_rows(
        coef_ref, v_ref, above_ref[...], below_ref[...], fl_ref[...], fr_ref[...], put
    )
    top_ref[...] = y_ref[0]
    low_ref[...] = y_ref[y_ref.shape[0] - 1]


def stencil(coef, v, above, below, from_left, from_right):
    rows, fields, width = v.shape
    side = pl.BlockSpec((FIELDS, width), lambda i: (i, 0))
    block = pl.BlockSpec((rows, FIELDS, width), lambda i: (0, i, 0))
    return call(
        stencil_kernel,
        (shape(rows, fields, width),) + (shape(fields, width),) * 3,
        (fields // FIELDS,),
        [pl.BlockSpec(coef.shape, lambda i: (0, 0, 0)), block, side, side, side, side],
        (block, side, side, side),
        flops=12 * v.size,
        moved=2 * v.size * 4,
    )(coef, v, above, below, from_left, from_right)


def wide(ref, start=0):
    return jnp.concatenate([ref[i, start:, :] for i in range(ref.shape[0])], axis=1)


def wide_row(ref):
    return jnp.concatenate([ref[i : i + 1, :] for i in range(ref.shape[0])], axis=1)


def halves(x):
    high = x.astype(jnp.bfloat16)
    low = (x - high.astype(F32)).astype(jnp.bfloat16)
    return jnp.concatenate([high, low], axis=0)


def nt(a, b):
    return lax.dot_general(a, b, (((1,), (1,)), ((), ())), preferred_element_type=F32)


def fold(acc, row, rows, col, cols):
    a = acc[row : row + rows, col : col + cols] + acc[row : row + rows, col + cols : col + 2 * cols]
    row += rows
    b = acc[row : row + rows, col : col + cols] + acc[row : row + rows, col + cols : col + 2 * cols]
    return a + b


def accumulate(acc_ref, term):
    @pl.when(pl.program_id(0) == 0)
    def _():
        acc_ref[...] = term

    @pl.when(pl.program_id(0) > 0)
    def _():
        acc_ref[...] += term


def at_end(fn):
    pl.when(pl.program_id(0) == pl.num_programs(0) - 1)(fn)


def gram_p_kernel(cap_ref, p_ref, pp_ref, pcp_ref, acc_ref):
    p = wide(p_ref)
    hp = halves(p)
    hc = halves(p * wide_row(cap_ref))
    accumulate(acc_ref, nt(hp, jnp.concatenate([hp, hc], axis=0)))

    @at_end
    def _():
        pp_ref[...] = fold(acc_ref, 0, 128, 0, 128)
        pcp_ref[...] = fold(acc_ref, 0, 128, 256, 128)


def gram_y_kernel(cap_ref, p_ref, y_ref, py_ref, yy_ref, pgp_ref, ygp_ref, acc_ref):
    y = wide(y_ref)
    hp = halves(wide(p_ref))
    hy = halves(y)
    hg = halves(y * wide_row(cap_ref))
    left = jnp.concatenate([hp, hy], axis=0)
    right = jnp.concatenate([hy, hg], axis=0)
    accumulate(acc_ref, nt(left, right))

    @at_end
    def _():
        py_ref[...] = fold(acc_ref, 0, 128, 0, 128)
        yy_ref[...] = fold(acc_ref, 256, 128, 0, 128)
        pgp_ref[...] = fold(acc_ref, 0, 128, 256, 128)
        ygp_ref[...] = fold(acc_ref, 256, 128, 256, 128)


def gram_x_kernel(cap_ref, p_ref, y_ref, a_ref, ygy_ref, x_ref, acc_ref, accx_ref):
    ay = wide(a_ref)
    hp = halves(wide(p_ref))
    hy = halves(wide(y_ref))
    hg = halves(ay * wide_row(cap_ref))
    hx = halves(ay[PRIOR - B :])
    accumulate(acc_ref, nt(hy, hg))
    accumulate(accx_ref, nt(jnp.concatenate([hp, hy, hg, hx], axis=0), hx))

    @at_end
    def _():
        ygy_ref[...] = fold(acc_ref, 0, 128, 0, 128)
        px = fold(accx_ref, 0, 128, 0, B)
        yx = fold(accx_ref, 256, 128, 0, B)
        gx = fold(accx_ref, 512, 128, 0, B)
        xx = fold(accx_ref, 768, B, 0, B)
        last = jnp.concatenate([xx, jnp.zeros((128 - B, B), F32)], axis=0)
        x_ref[...] = jnp.concatenate([px, yx, gx, last], axis=1)


def gram(kernel, cap, arrays, n_out, acc_shapes, flops):
    rows, fields, width = arrays[0].shape
    block = pl.BlockSpec((DEPTH, fields, width), lambda i: (i, 0, 0))
    whole = pl.BlockSpec((128, 128), lambda i: (0, 0))
    return call(
        kernel,
        (shape(128, 128),) * n_out,
        (rows // DEPTH,),
        [pl.BlockSpec((DEPTH, width), lambda i: (i, 0))] + [block] * len(arrays),
        (whole,) * n_out,
        scratch=[pltpu.VMEM(s, F32) for s in acc_shapes],
        flops=flops,
        moved=len(arrays) * arrays[0].size * 4,
    )(cap, *arrays)


def pick_kernel(where_ref, p_ref, y_ref, a_ref, py_ref, x_ref, buf_ref, sem):
    py_ref[...] = jnp.zeros_like(py_ref)
    x_ref[...] = jnp.zeros_like(x_ref)
    n = where_ref.shape[1]

    def step(k, carry):
        @pl.when(where_ref[2, k] > 0)
        def _():
            r, c = where_ref[0, k], where_ref[1, k]
            for ref, first, lanes, out_ref in (
                (p_ref, 0, 0, py_ref),
                (y_ref, 0, n, py_ref),
                (a_ref, PRIOR - B, 0, x_ref),
            ):
                copy = pltpu.make_async_copy(ref.at[r], buf_ref, sem)
                copy.start()
                copy.wait()
                v = buf_ref[first:, :]
                lane = lanes_of(v.shape)
                spot = k + lanes
                moved = pltpu.roll(v, lax.rem(spot - c + 128, 128), 1)
                out_ref[...] = jnp.where(lane == spot, moved, out_ref[...])

        return carry

    lax.fori_loop(0, n, step, 0)


def pick(where, p, y, ay):
    any_spec = pl.BlockSpec(memory_space=pl.ANY)
    return pl.pallas_call(
        pick_kernel,
        out_shape=(shape(128, 128), shape(B, 128)),
        in_specs=[pl.BlockSpec(memory_space=pltpu.SMEM), any_spec, any_spec, any_spec],
        out_specs=(pl.BlockSpec(memory_space=pltpu.VMEM),) * 2,
        scratch_shapes=[pltpu.VMEM((128, 128), F32), pltpu.SemaphoreType.DMA],
        compiler_params=pltpu.CompilerParams(vmem_limit_bytes=VMEM_LIMIT),
        cost_estimate=pl.CostEstimate(flops=0, bytes_accessed=1 << 20, transcendentals=0),
    )(where, p, y, ay)


def last_kernel(
    core_ref, coef_ref, a_ref, above_ref, below_ref, fl_ref, fr_ref,
    pp_ref, pcp_ref, py_ref, yy_ref, pgp_ref, ygp_ref, ygy_ref, x_ref, kp_ref, kx_ref,
    ax_ref, keep_ref, give_ref, image_ref, pack_ref,
):
    def put(r, y, image):
        ax_ref[r] = y
        image_ref[r] = image

    stencil_rows(coef_ref, a_ref, above_ref[...], below_ref[...], fl_ref[...], fr_ref[...], put)
    acc = jnp.zeros((2 * B, 2 * B), F32)
    for at in range(0, a_ref.shape[0], 16):
        hx = halves(jnp.concatenate([a_ref[at + i] for i in range(16)], axis=1))
        hg = halves(jnp.concatenate([image_ref[at + i] for i in range(16)], axis=1))
        acc = acc + nt(hx, hg)
    xgx = fold(acc, 0, B, 0, B)
    row = lax.broadcasted_iota(jnp.int32, (128, 128), 0)
    col = lax.broadcasted_iota(jnp.int32, (128, 128), 1)

    def diagonal(m):
        return jnp.sum(jnp.where(row == col, m, 0.0), axis=0, keepdims=True)

    pack_ref[0:128] = jnp.where(row <= col, pp_ref[...], pcp_ref[...])
    pack_ref[128:256] = jnp.where(row <= col, pgp_ref[...], ygy_ref[...])
    pack_ref[256:384] = jnp.where(row <= col, yy_ref[...], ygp_ref[...])
    pack_ref[384:512] = py_ref[...]
    kx = kx_ref[...]
    extra = jnp.concatenate([jnp.zeros((B, B), F32), kx[:, :B], kx[:, B : 2 * B], xgx], axis=0)
    pack_ref[512:640] = x_ref[...] + jnp.concatenate([jnp.zeros((128, 96), F32), extra], axis=1)
    pack_ref[640:768] = kp_ref[...]
    diag = [diagonal(m[...]) for m in (pcp_ref, ygy_ref, ygp_ref)]
    pack_ref[768:776] = jnp.concatenate(diag + [jnp.zeros((5, 128), F32)], axis=0)
    pack_ref[776:832] = jnp.zeros((56, 128), F32)
    half = PACK // 2
    core = core_ref[0]
    keep_ref[...] = pack_ref[pl.ds(pl.multiple_of(core * half, 8), half), :]
    give_ref[...] = pack_ref[pl.ds(pl.multiple_of((1 - core) * half, 8), half), :]


def last(core, coef, ay, sides, mats):
    rows, fields, width = ay.shape
    vm = pl.BlockSpec(memory_space=pltpu.VMEM)
    full = lambda a: pl.BlockSpec(a.shape, lambda i: (0,) * a.ndim)
    return call(
        last_kernel,
        (shape(rows, B, width), shape(PACK // 2, 128), shape(PACK // 2, 128)),
        (1,),
        [pl.BlockSpec(memory_space=pltpu.SMEM), full(coef), pl.BlockSpec((rows, B, width), lambda i: (0, fields // B - 1, 0))]
        + [full(a) for a in sides]
        + [full(a) for a in mats],
        (
            pl.BlockSpec((rows, B, width), lambda i: (0, 0, 0)),
            pl.BlockSpec((PACK // 2, 128), lambda i: (0, 0)),
            pl.BlockSpec((PACK // 2, 128), lambda i: (0, 0)),
        ),
        scratch=[pltpu.VMEM((rows, B, width), F32), pltpu.VMEM((PACK, 128), F32)],
        flops=1 << 27,
        moved=2 * rows * B * width * 4,
    )(core, coef, ay, *sides, *mats)


def combine_kernel(t_ref, p_ref, y_ref, a_ref, ax_ref, q_ref, n_ref):
    th = t_ref[...].astype(jnp.bfloat16)
    tl = (t_ref[...] - th.astype(F32)).astype(jnp.bfloat16)
    both = jnp.concatenate([th, tl], axis=0)
    two = 2 * B

    def split(x):
        high = x.astype(jnp.bfloat16)
        return high, (x - high.astype(F32)).astype(jnp.bfloat16)

    def mm(a, b):
        return jnp.dot(a, b, preferred_element_type=F32)

    def times(lhs_both, lhs_high, pair):
        rows = lhs_high.shape[0]
        big = mm(lhs_both, pair[0])
        return big[:rows] + big[rows:] + mm(lhs_high, pair[1])

    fields, width = p_ref.shape[1:]
    for j in range(0, DEPTH, 2):
        get = lambda ref: jnp.concatenate([ref[j], ref[j + 1]], axis=1)
        p, y, a, ax = (get(ref) for ref in (p_ref, y_ref, a_ref, ax_ref))
        py = split(jnp.concatenate([p, y], axis=0))
        x = split(a[PRIOR - B :])
        yr = (py[0][PRIOR:], py[1][PRIOR:])
        rest = split(jnp.concatenate([a, ax], axis=0))
        def cut(lo, hi, rows):
            high = th[rows[0] : rows[1], lo:hi]
            return jnp.concatenate([high, tl[rows[0] : rows[1], lo:hi]], axis=0), high

        q = times(*cut(0, 256, (0, two)), py) + times(*cut(256, 288, (0, two)), x)
        n = times(*cut(0, 128, (B, two)), yr) + times(*cut(128, 288, (B, two)), rest)
        for k in (0, 1):
            q_ref.reshape(two * DEPTH, width)[pl.ds(j + k, two, stride=DEPTH), :] = q[
                :, k * width : (k + 1) * width
            ]
            n_ref.reshape(B * DEPTH, width)[pl.ds(j + k, B, stride=DEPTH), :] = n[
                :, k * width : (k + 1) * width
            ]


def combine(t, p, y, ay, ax):
    rows, fields, width = p.shape
    block = pl.BlockSpec((DEPTH, fields, width), lambda i: (i, 0, 0))
    return call(
        combine_kernel,
        (shape(2 * B, rows, width), shape(B, rows, width)),
        (rows // DEPTH,),
        [
            pl.BlockSpec(t.shape, lambda i: (0, 0)),
            block,
            block,
            block,
            pl.BlockSpec((DEPTH, B, width), lambda i: (i, 0, 0)),
        ],
        (
            pl.BlockSpec((2 * B, DEPTH, width), lambda i: (0, i, 0)),
            pl.BlockSpec((B, DEPTH, width), lambda i: (0, i, 0)),
        ),
        flops=3 * 2 * 96 * 288 * rows * width,
        moved=5 * p.size * 4,
    )(t, p, y, ay, ax)


def swap(x, axis, mask):
    return lax.ppermute(x, axis, [(i, i ^ mask) for i in range(lax.axis_size(axis))])


def shift(x, axis, step):
    size = lax.axis_size(axis)
    return lax.ppermute(
        x, axis, [(i, i + step) for i in range(size) if 0 <= i + step < size]
    )


def quad_sum(parts):
    return (parts[0] + parts[1]) + (parts[2] + parts[3])


def sum_over_devices(keep, give):
    x = keep + swap(give, "gx", 1)
    me = lax.axis_index("gy")
    quarter = x.shape[0] // 4
    parts = [
        lax.dynamic_slice_in_dim(x, (me ^ m) * quarter, quarter, 0) for m in range(4)
    ]
    x = quad_sum([parts[0]] + [swap(parts[m], "gy", m) for m in (1, 2, 3)])
    mask = 2
    while mask < lax.axis_size("gx"):
        x = x + swap(x, "gx", mask)
        mask *= 2
    x = jnp.concatenate([x, swap(x, "gx", 1)], axis=0)
    return [x] + [swap(x, "gy", m) for m in (1, 2, 3)]


def exchange(top, low, edge, edge_left):
    return (
        shift(low, "gx", 1),
        shift(top, "gx", -1),
        shift(edge, "gy", 1),
        shift(edge_left, "gy", -1),
    )


def dot(a, b):
    return jnp.dot(a, b, precision=HI, preferred_element_type=F32)


def tdot(a, b):
    return lax.dot_general(
        a, b, (((0,), (0,)), ((), ())), precision=HI, preferred_element_type=F32
    )


def inverse_factor(s):
    n = s.shape[0]
    s = 0.5 * (s + s.T)
    row = lax.broadcasted_iota(jnp.int32, (n, 128), 0)
    lane = lax.broadcasted_iota(jnp.int32, (n, 128), 1)
    eye = jnp.where(row + n == lane, 1.0, 0.0)
    a = jnp.concatenate([s, jnp.zeros((n, 128 - n), F32)], axis=1) + eye
    for j in range(n):
        pivot = a[j : j + 1, :]
        inv = 1.0 / jnp.sqrt(pivot[:, j : j + 1])
        pivot = pivot * inv
        factor = a[:, j : j + 1] * inv
        a = jnp.where(row > j, a - factor * pivot, jnp.where(row == j, pivot, a))
    return a[:, n : 2 * n]


def algebra_kernel(
    scale, place_ref, b0_ref, b1_ref, b2_ref, b3_ref, t_ref, g_ref, c_ref, b_ref, all_ref
):
    me, core = place_ref[0], place_ref[1]
    quarter = PACK // 8
    for m, ref in enumerate((b0_ref, b1_ref, b2_ref, b3_ref)):
        for h in (0, 1):
            at = (core ^ h) * 4 + (me ^ m)
            all_ref[pl.ds(pl.multiple_of(at * quarter, 8), quarter), :] = ref[
                h * quarter : (h + 1) * quarter
            ]
    row = lax.broadcasted_iota(jnp.int32, (128, 128), 0)
    col = lax.broadcasted_iota(jnp.int32, (128, 128), 1)

    def pair(at, d):
        m = all_ref[at : at + 128] * scale
        t = m.T
        diag = all_ref[768 + d : 769 + d] * scale
        return (
            jnp.where(row <= col, m, t),
            jnp.where(row > col, m, jnp.where(row < col, t, diag)),
        )

    pp, pcp = pair(0, 0)
    pgp, ygy = pair(128, 1)
    yy, ycy = pair(256, 2)
    py = all_ref[384:512] * scale
    xs = all_ref[512:640] * scale
    px, yx, ygx = xs[:, :32], xs[:, 32:64], xs[:, 64:96]
    xx, xgx = xs[:32, 96:], xs[96:, 96:]
    z = PRIOR - B

    h = py[:, z:]
    c = 2.0 * h - dot(pp, h)
    s = yy[z:, z:] + tdot(c, dot(pp, c) - 2.0 * h)
    inv_t = inverse_factor(s).T
    a, b = -dot(c, inv_t), inv_t

    hp = dot(py, a) + dot(px, b)
    wy = dot(yy, a) + dot(yx, b)
    wx = tdot(yx, a) + dot(xx, b)
    hq = tdot(a, hp) + tdot(b, wy[z:])
    kq = dot(pp, a) + dot(h, b)
    kqq = tdot(a, kq) + tdot(b, tdot(h, a) + dot(yy[z:, z:], b))
    cp = 2.0 * hp - dot(pp, hp) - dot(kq, hq)
    cq = 2.0 * hq - tdot(kq, hp) - dot(kqq, hq)
    s = (
        tdot(a, wy)
        + tdot(b, wx)
        + tdot(cp, dot(pp, cp) + dot(kq, cq) - 2.0 * hp)
        + tdot(cq, tdot(kq, cp) + dot(kqq, cq) - 2.0 * hq)
    )
    inv_t = inverse_factor(s).T
    zero_z = jnp.zeros((z, B), F32)
    u = -dot(cp + dot(a, cq), inv_t)
    v = dot(a - jnp.concatenate([zero_z, dot(b, cq)], axis=0), inv_t)
    x = dot(b, inv_t)

    zero = jnp.zeros((B, B), F32)
    tp = jnp.concatenate([a, u, jnp.zeros((128, B), F32)], axis=1)
    ty = jnp.concatenate([jnp.concatenate([zero_z, b], axis=0), v, a], axis=1)
    tx = jnp.concatenate([zero, x, b], axis=1)
    t_ref[...] = jnp.concatenate([tp[:, :64], ty[:, :64], tx[:, :64]], axis=0)

    pcx, ycx, xcx = ycy[:, z:], ygy[:, z:], ygx[z:]
    cpt = dot(pcp, tp) + dot(pgp, ty) + dot(pcx, tx)
    cyt = dot(pgp, tp) + dot(ycy, ty) + dot(ycx, tx)
    cxt = tdot(pcx, tp) + tdot(ycx, ty) + dot(xcx, tx)
    qp, qy, qx = tp[:, :64], ty[:, :64], tx[:, :64]
    r = tdot(qp, cpt) + tdot(qy, cyt) + tdot(qx, cxt)
    side = cpt[:, :64]
    c_ref[0:128, 0:128] = pcp
    c_ref[0:128, 128:192] = side
    c_ref[128:192, 0:128] = side.T
    c_ref[128:192, 128:192] = r[:, :64]
    gpt = cyt[:, 32:64]
    gyt = dot(ycy, u) + dot(ygy, v) + dot(ygx, x)
    gxt = tdot(ycx, u) + tdot(ygx, v) + dot(xgx, x)
    g_ref[0:128] = jnp.concatenate([cpt[:, 64:96], gpt], axis=1)
    g2 = tdot(qp, gpt) + tdot(qy, gyt) + tdot(qx, gxt)
    g_ref[128:192] = jnp.concatenate([r[:, 64:96], g2], axis=1)
    kp = all_ref[640:768]
    extra = all_ref[512:640][:, 96:]
    kx = jnp.concatenate([extra[32:64], extra[64:96]], axis=1)
    b_ref[0:128] = kp[:, :64]
    b_ref[128:192] = tdot(qp, kp[:, :64]) + tdot(qy, kp[:, 64:]) + tdot(qx, kx)


def algebra(place, pieces, scale):
    vm = pl.BlockSpec(memory_space=pltpu.VMEM)
    return pl.pallas_call(
        functools.partial(algebra_kernel, scale),
        out_shape=(shape(288, 64), shape(192, 64), shape(192, 192), shape(192, 64)),
        in_specs=[pl.BlockSpec(memory_space=pltpu.SMEM)] + [vm] * 4,
        out_specs=(vm,) * 4,
        scratch_shapes=[pltpu.VMEM((PACK, 128), F32)],
        compiler_params=pltpu.CompilerParams(vmem_limit_bytes=VMEM_LIMIT),
        cost_estimate=pl.CostEstimate(flops=1 << 28, bytes_accessed=1 << 20, transcendentals=0),
    )(place, *pieces)


def on_device(prior, cond_x, cond_y, cap_level, decap, via, ports):
    rows_here, cols_here = prior.shape[1:]
    total_cols = cols_here * lax.axis_size("gy")
    scale = 1.0 / (rows_here * lax.axis_size("gx") * total_cols)
    gxe = 0.125 * cond_x.astype(F32)
    gye = 0.125 * cond_y.astype(F32)
    gvia = 0.5 * via.astype(F32)
    cap = 0.25 * cap_level.astype(F32) * (1.0 + 2.0 * decap.astype(F32))

    p, top, low, edge = regroup(prior)
    slot = 2 * jnp.arange(rows_here)[:, None] == jnp.arange(cols_here)[None, :]
    gye_edge = jnp.sum(jnp.where(slot, gye[:, -1:], 0.0), axis=0, keepdims=True)
    spare = jnp.zeros((7, cols_here), F32)
    low = jnp.concatenate([low, gxe[-1:], spare], axis=0)
    edge_more = jnp.concatenate([edge, gye_edge, spare], axis=0)
    above, below, fl, fr = exchange(top, low, edge_more, edge)
    gxw = jnp.concatenate([above[PRIOR : PRIOR + 1], gxe[:-1]], axis=0)
    gys_first = jnp.sum(jnp.where(slot, fl[PRIOR : PRIOR + 1], 0.0), axis=1, keepdims=True)
    gys = jnp.concatenate([gys_first, gye[:, :-1]], axis=1)
    center = gvia + gxe + gxw + gye + gys
    coef = jnp.stack([center, gxe, gxw, gye, gys, 1.0 / cap])

    unit = 2 * 128 * 128 * rows_here * cols_here
    pp, pcp = gram(gram_p_kernel, cap, [p], 2, [(256, 512)], 8 * unit)
    y, top, low, edge = stencil(coef, p, above[:PRIOR], below, fl[:PRIOR], fr)
    sides = exchange(top, low, edge, edge)
    py, yy, pgp, ygp = gram(gram_y_kernel, cap, [p, y], 4, [(512, 512)], 16 * unit)
    ay, top, low, edge = stencil(coef, y, *sides)
    top, low, edge = (a[PRIOR - B :] for a in (top, low, edge))
    sides = exchange(top, low, edge, edge)
    ygy, xs = gram(gram_x_kernel, cap, [p, y, ay], 2, [(256, 256), (832, 64)], 8 * unit)

    port_rows = ports // total_cols - lax.axis_index("gx") * rows_here
    port_cols = ports % total_cols - lax.axis_index("gy") * cols_here
    inside = (
        (port_rows >= 0) & (port_rows < rows_here) & (port_cols >= 0) & (port_cols < cols_here)
    )
    where = jnp.stack(
        [
            jnp.clip(port_rows, 0, rows_here - 1),
            jnp.clip(port_cols, 0, cols_here - 1),
            inside.astype(jnp.int32),
        ]
    )
    kp, kx = pick(where, p, y, ay)
    core = lax.axis_index("gx") % 2
    ax, keep, give = last(
        core[None], coef, ay, sides, [pp, pcp, py, yy, pgp, ygp, ygy, xs, kp, kx]
    )
    place = jnp.stack([lax.axis_index("gy"), core])
    pieces = sum_over_devices(keep, give)
    t, g_columns, c_reduced, b_reduced = algebra(place, pieces, scale)
    t = t.T
    new_basis, next_image = combine(t, p, y, ay, ax)
    return (new_basis, next_image, g_columns, c_reduced, b_reduced)


def solution(mesh):
    in_specs = (
        P(None, "gx", "gy"),
        P("gx", "gy"),
        P("gx", "gy"),
        P("gx", "gy"),
        P("gx", "gy"),
        P("gx", "gy"),
        P(),
    )
    out_specs = (P(None, "gx", "gy"), P(None, "gx", "gy"), P(), P(), P())
    return jax.shard_map(
        on_device, mesh=mesh, in_specs=in_specs, out_specs=out_specs, check_vma=False
    )
```

```python
import functools

import jax
import jax.numpy as jnp
from jax import lax
from jax.experimental import pallas as pl
from jax.experimental.pallas import tpu as pltpu
from jax.sharding import PartitionSpec as P

B = 32
PRIOR = 128
F32 = jnp.float32
HI = lax.Precision.HIGHEST
VMEM_LIMIT = 24 * 1024 * 1024
TILE = 32
CHUNK = 16
DEPTH = 8
PACK = 832
VM = pl.BlockSpec(memory_space=pltpu.VMEM)
SM = pl.BlockSpec(memory_space=pltpu.SMEM)
HBM = pl.BlockSpec(memory_space=pltpu.HBM)


def call(kernel, out, in_specs, out_specs, scratch=(), flops=0, moved=0):
    return pl.pallas_call(
        kernel,
        out_shape=out,
        in_specs=in_specs,
        out_specs=out_specs,
        scratch_shapes=scratch,
        compiler_params=pltpu.CompilerParams(vmem_limit_bytes=VMEM_LIMIT),
        cost_estimate=pl.CostEstimate(flops=flops, bytes_accessed=moved, transcendentals=0),
    )


def shape(*dims):
    return jax.ShapeDtypeStruct(dims, F32)


def held(*dims):
    return pltpu.VMEM(dims, F32)


def lanes_of(dims):
    return lax.broadcasted_iota(jnp.int32, dims, len(dims) - 1)


def pack_edges(v_ref, edge_ref):
    rows, fields, width = v_ref.shape
    slot = lanes_of((TILE, width)) >> 1
    for at in range(0, fields, TILE):
        edge = jnp.zeros((TILE, width), F32)
        for r in range(rows):
            edge = jnp.where(
                slot == r, pltpu.roll(v_ref[r, at : at + TILE, :], 2 * r + 1, 1), edge
            )
        edge_ref[at : at + TILE] = edge


def ends(v_ref, top_ref, low_ref):
    top_ref[...] = v_ref[0]
    low_ref[...] = v_ref[v_ref.shape[0] - 1]


def regroup_kernel(p_ref, out_ref, top_ref, low_ref, edge_ref, buf_ref, sems):
    parts, fields, rows, width = buf_ref.shape
    copies = [
        pltpu.make_async_copy(p_ref.at[pl.ds(i * fields, fields)], buf_ref.at[i], sems.at[i])
        for i in range(parts)
    ]
    for copy in copies:
        copy.start()
    for i in range(parts):
        copies[i].wait()
        for at in range(0, rows, DEPTH):
            flat = buf_ref.at[i].reshape(fields * rows, width)
            got = [flat[pl.ds(at + k, fields, stride=rows), :] for k in range(DEPTH)]
            for k in range(DEPTH):
                out_ref[at + k, i * fields : (i + 1) * fields, :] = got[k]
    pack_edges(out_ref, edge_ref)
    ends(out_ref, top_ref, low_ref)


def regroup(prior):
    fields, rows, width = prior.shape
    parts = fields // CHUNK
    return call(
        regroup_kernel,
        (held(rows, fields, width),) + (shape(fields, width),) * 3,
        [HBM],
        (VM,) * 4,
        scratch=[
            pltpu.VMEM((parts, CHUNK, rows, width), F32),
            pltpu.SemaphoreType.DMA((parts,)),
        ],
        moved=prior.size * 4,
    )(prior)


def stencil_rows(coef_ref, v_ref, first, above_ref, below_ref, fl_ref, fr_ref, seam_ref, put):
    rows, width = v_ref.shape[0], v_ref.shape[2]
    fields = above_ref.shape[0]
    tile = 8
    lane = lanes_of((tile, width))
    odd, start, stop = (lane & 1) == 1, lane == 0, lane == width - 1
    for at in range(0, fields, tile):
        cut = slice(at, at + tile)
        seam_ref[cut] = jnp.where(
            odd, pltpu.roll(fl_ref[cut], 1, 1), pltpu.roll(fr_ref[cut], width - 1, 1)
        )
    for r in range(rows):
        c = [jnp.broadcast_to(coef_ref[k, r : r + 1, :], (tile, width)) for k in range(6)]
        for at in range(0, fields, tile):
            cut = slice(at, at + tile)
            src = slice(first + at, first + at + tile)
            v = v_ref[r, src, :]
            up = above_ref[cut] if r == 0 else v_ref[r - 1, src, :]
            down = below_ref[cut] if r == rows - 1 else v_ref[r + 1, src, :]
            side = pltpu.roll(seam_ref[cut], width - 1 - 2 * r, 1)
            south = jnp.where(start, side, pltpu.roll(v, 1, 1))
            north = jnp.where(stop, side, pltpu.roll(v, width - 1, 1))
            put(r, cut, c[0] * v - c[1] * down - c[2] * up - c[3] * north - c[4] * south, c[5])


def stencil_kernel(
    coef_ref, v_ref, above_ref, below_ref, fl_ref, fr_ref, y_ref, top_ref, low_ref, edge_ref,
    seam_ref,
):
    def put(r, cut, image, inv_cap):
        y_ref[r, cut, :] = image * inv_cap

    stencil_rows(coef_ref, v_ref, 0, above_ref, below_ref, fl_ref, fr_ref, seam_ref, put)
    pack_edges(y_ref, edge_ref)
    ends(y_ref, top_ref, low_ref)


def stencil(coef, v, above, below, from_left, from_right):
    rows, fields, width = v.shape
    return call(
        stencil_kernel,
        (held(rows, fields, width),) + (shape(fields, width),) * 3,
        [VM] * 6,
        (VM,) * 4,
        scratch=[pltpu.VMEM((fields, width), F32)],
        flops=12 * v.size,
        moved=2 * v.size * 4,
    )(coef, v, above, below, from_left, from_right)


def wide(ref, at):
    return jnp.concatenate([ref[at + i] for i in range(CHUNK)], axis=1)


def wide_row(ref, at):
    return jnp.concatenate([ref[pl.ds(at + i, 1), :] for i in range(CHUNK)], axis=1)


def halves(x):
    high = x.astype(jnp.bfloat16)
    low = (x - high.astype(F32)).astype(jnp.bfloat16)
    return jnp.concatenate([high, low], axis=0)


def nt(a, b):
    return lax.dot_general(a, b, (((1,), (1,)), ((), ())), preferred_element_type=F32)


def fold(acc, row, rows, col, cols):
    a = acc[row : row + rows, col : col + cols] + acc[row : row + rows, col + cols : col + 2 * cols]
    row += rows
    b = acc[row : row + rows, col : col + cols] + acc[row : row + rows, col + cols : col + 2 * cols]
    return a + b


def over_chunks(rows, accs, terms):
    def add(i, carry):
        for acc, term in zip(accs, terms(i * CHUNK)):
            acc[...] += term
        return carry

    for acc in accs:
        acc[...] = jnp.zeros_like(acc)
    lax.fori_loop(0, rows // CHUNK, add, 0)


def gram_y_kernel(
    cap_ref, p_ref, y_ref, pp_ref, pcp_ref, py_ref, yy_ref, pgp_ref, ygp_ref, accp_ref, accy_ref
):
    def terms(at):
        p, y, cap = wide(p_ref, at), wide(y_ref, at), wide_row(cap_ref, at)
        hp, hy, hg = halves(p), halves(y), halves(y * cap)
        right = jnp.concatenate([hy, hg], axis=0)
        yield nt(hp, jnp.concatenate([right, hp, halves(p * cap)], axis=0))
        yield nt(hy, right)

    over_chunks(p_ref.shape[0], (accp_ref, accy_ref), terms)
    py_ref[...] = fold(accp_ref, 0, 128, 0, 128)
    pgp_ref[...] = fold(accp_ref, 0, 128, 256, 128)
    pp_ref[...] = fold(accp_ref, 0, 128, 512, 128)
    pcp_ref[...] = fold(accp_ref, 0, 128, 768, 128)
    yy_ref[...] = fold(accy_ref, 0, 128, 0, 128)
    ygp_ref[...] = fold(accy_ref, 0, 128, 256, 128)


def gram_x_kernel(
    where_ref, cap_ref, p_ref, y_ref, a_ref, ygy_ref, x_ref, kp_ref, kx_ref, acc_ref, accx_ref
):
    def terms(at):
        ay = wide(a_ref, at)
        hp, hy = halves(wide(p_ref, at)), halves(wide(y_ref, at))
        hg = halves(ay * wide_row(cap_ref, at))
        hx = halves(ay[PRIOR - B :])
        yield nt(hy, hg)
        yield nt(jnp.concatenate([hp, hy, hg, hx], axis=0), hx)

    over_chunks(p_ref.shape[0], (acc_ref, accx_ref), terms)
    ygy_ref[...] = fold(acc_ref, 0, 128, 0, 128)
    px = fold(accx_ref, 0, 128, 0, B)
    yx = fold(accx_ref, 256, 128, 0, B)
    gx = fold(accx_ref, 512, 128, 0, B)
    xx = fold(accx_ref, 768, B, 0, B)
    rest = jnp.concatenate([xx, jnp.zeros((128 - B, B), F32)], axis=0)
    x_ref[...] = jnp.concatenate([px, yx, gx, rest], axis=1)

    kp_ref[...] = jnp.zeros_like(kp_ref)
    kx_ref[...] = jnp.zeros_like(kx_ref)
    n = where_ref.shape[1]

    def step(k, carry):
        @pl.when(where_ref[2, k] > 0)
        def _():
            r, c = where_ref[0, k], where_ref[1, k]
            for v, spot, out_ref in (
                (p_ref[r], k, kp_ref),
                (y_ref[r], k + n, kp_ref),
                (a_ref[r][PRIOR - B :], k, kx_ref),
            ):
                moved = pltpu.roll(v, lax.rem(spot - c + 128, 128), 1)
                out_ref[...] = jnp.where(lanes_of(v.shape) == spot, moved, out_ref[...])

        return carry

    lax.fori_loop(0, n, step, 0)


def gram_y(cap, p, y):
    return call(
        gram_y_kernel,
        (shape(128, 128),) * 6,
        [VM] * 3,
        (VM,) * 6,
        scratch=[pltpu.VMEM((256, 1024), F32), pltpu.VMEM((256, 512), F32)],
        flops=6 * 2 * 256 * 256 * p.shape[0] * 128,
        moved=2 * p.size * 4,
    )(cap, p, y)


def gram_x(where, cap, p, y, ay):
    return call(
        gram_x_kernel,
        (shape(128, 128),) * 3 + (shape(B, 128),),
        [SM] + [VM] * 4,
        (VM,) * 4,
        scratch=[pltpu.VMEM((256, 256), F32), pltpu.VMEM((832, 64), F32)],
        flops=4 * 2 * 256 * 256 * p.shape[0] * 128,
        moved=3 * p.size * 4,
    )(where, cap, p, y, ay)


def last_kernel(
    core_ref, coef_ref, a_ref, above_ref, below_ref, fl_ref, fr_ref,
    pp_ref, pcp_ref, py_ref, yy_ref, pgp_ref, ygp_ref, ygy_ref, x_ref, kp_ref, kx_ref,
    ax_ref, keep_ref, give_ref, image_ref, pack_ref, seam_ref,
):
    def put(r, cut, image, inv_cap):
        ax_ref[r, cut, :] = image * inv_cap
        image_ref[r, cut, :] = image

    stencil_rows(
        coef_ref, a_ref, PRIOR - B, above_ref, below_ref, fl_ref, fr_ref, seam_ref, put
    )
    acc = jnp.zeros((2 * B, 2 * B), F32)
    for at in range(0, a_ref.shape[0], CHUNK):
        hx = halves(wide(a_ref, at)[PRIOR - B :])
        acc = acc + nt(hx, halves(wide(image_ref, at)))
    xgx = fold(acc, 0, B, 0, B)
    row = lax.broadcasted_iota(jnp.int32, (128, 128), 0)
    col = lax.broadcasted_iota(jnp.int32, (128, 128), 1)

    def diagonal(m):
        return jnp.sum(jnp.where(row == col, m, 0.0), axis=0, keepdims=True)

    pack_ref[0:128] = jnp.where(row <= col, pp_ref[...], pcp_ref[...])
    pack_ref[128:256] = jnp.where(row <= col, pgp_ref[...], ygy_ref[...])
    pack_ref[256:384] = jnp.where(row <= col, yy_ref[...], ygp_ref[...])
    pack_ref[384:512] = py_ref[...]
    kx = kx_ref[...]
    extra = jnp.concatenate([jnp.zeros((B, B), F32), kx[:, :B], kx[:, B : 2 * B], xgx], axis=0)
    pack_ref[512:640] = x_ref[...] + jnp.concatenate([jnp.zeros((128, 96), F32), extra], axis=1)
    pack_ref[640:768] = kp_ref[...]
    diag = [diagonal(m[...]) for m in (pcp_ref, ygy_ref, ygp_ref)]
    pack_ref[768:776] = jnp.concatenate(diag + [jnp.zeros((5, 128), F32)], axis=0)
    pack_ref[776:832] = jnp.zeros((56, 128), F32)
    half = PACK // 2
    core = core_ref[0]
    keep_ref[...] = pack_ref[pl.ds(pl.multiple_of(core * half, 8), half), :]
    give_ref[...] = pack_ref[pl.ds(pl.multiple_of((1 - core) * half, 8), half), :]


def last(core, coef, ay, sides, mats):
    rows, fields, width = ay.shape
    return call(
        last_kernel,
        (held(rows, B, width), shape(PACK // 2, 128), shape(PACK // 2, 128)),
        [SM] + [VM] * (2 + len(sides) + len(mats)),
        (VM,) * 3,
        scratch=[
            pltpu.VMEM((rows, B, width), F32),
            pltpu.VMEM((PACK, 128), F32),
            pltpu.VMEM((B, width), F32),
        ],
        flops=1 << 27,
        moved=2 * rows * B * width * 4,
    )(core, coef, ay, *sides, *mats)


def split(x):
    high = x.astype(jnp.bfloat16)
    return high, (x - high.astype(F32)).astype(jnp.bfloat16)


def times(t, pair):
    rows = t.shape[0] // 2
    big = jnp.dot(t, pair[0], preferred_element_type=F32)
    return big[:rows] + big[rows:] + jnp.dot(t[:rows], pair[1], preferred_element_type=F32)


def combine(t, p_ref, y_ref, a_ref, ax_ref, q_ref, n_ref, qbuf_ref, nbuf_ref, sems):
    two = 2 * B
    high, low = split(t)

    def cut(lo, hi, first):
        return jnp.concatenate([high[first:, lo:hi], low[first:, lo:hi]], axis=0)

    t_py, t_x, t_y, t_rest = cut(0, 256, 0), cut(256, 288, 0), cut(0, 128, B), cut(128, 288, B)
    rows, fields, width = p_ref.shape
    copies = []
    for at in range(0, rows, DEPTH):

        def row_block(ref):
            return jnp.concatenate([ref[at + i] for i in range(DEPTH)], axis=1)

        p, y = split(row_block(p_ref)), split(row_block(y_ref))
        a, ax = split(row_block(a_ref)), split(row_block(ax_ref))
        py = tuple(jnp.concatenate(pair, axis=0) for pair in zip(p, y))
        rest = tuple(jnp.concatenate(pair, axis=0) for pair in zip(a, ax))
        x = tuple(part[PRIOR - B :] for part in a)
        q = times(t_py, py) + times(t_x, x)
        n = times(t_y, y) + times(t_rest, rest)
        step = at // DEPTH
        for k in range(DEPTH):
            lanes = slice(k * width, (k + 1) * width)
            qbuf_ref.at[step].reshape(two * DEPTH, width)[pl.ds(k, two, stride=DEPTH), :] = q[
                :, lanes
            ]
            nbuf_ref.at[step].reshape(B * DEPTH, width)[pl.ds(k, B, stride=DEPTH), :] = n[
                :, lanes
            ]
        for j, (src, dst) in enumerate(((qbuf_ref, q_ref), (nbuf_ref, n_ref))):
            copy = pltpu.make_async_copy(
                src.at[step], dst.at[:, pl.ds(at, DEPTH), :], sems.at[j, step]
            )
            copy.start()
            copies.append(copy)
    return copies


def swap(x, axis, mask):
    return lax.ppermute(x, axis, [(i, i ^ mask) for i in range(lax.axis_size(axis))])


def shift(x, axis, step):
    size = lax.axis_size(axis)
    return lax.ppermute(
        x, axis, [(i, i + step) for i in range(size) if 0 <= i + step < size]
    )


def quad_sum(parts):
    return (parts[0] + parts[1]) + (parts[2] + parts[3])


def sum_over_devices(keep, give):
    x = keep + swap(give, "gx", 1)
    me = lax.axis_index("gy")
    quarter = x.shape[0] // 4
    parts = [
        lax.dynamic_slice_in_dim(x, (me ^ m) * quarter, quarter, 0) for m in range(4)
    ]
    x = quad_sum([parts[0]] + [swap(parts[m], "gy", m) for m in (1, 2, 3)])
    mask = 2
    while mask < lax.axis_size("gx"):
        x = x + swap(x, "gx", mask)
        mask *= 2
    x = jnp.concatenate([x, swap(x, "gx", 1)], axis=0)
    return [x] + [swap(x, "gy", m) for m in (1, 2, 3)]


def exchange(top, low, edge, edge_left):
    return (
        shift(low, "gx", 1),
        shift(top, "gx", -1),
        shift(edge, "gy", 1),
        shift(edge_left, "gy", -1),
    )


def dot(a, b):
    return jnp.dot(a, b, precision=HI, preferred_element_type=F32)


def tdot(a, b):
    return lax.dot_general(
        a, b, (((0,), (0,)), ((), ())), precision=HI, preferred_element_type=F32
    )


def inverse_factor(s):
    n = s.shape[0]
    s = 0.5 * (s + s.T)
    row = lax.broadcasted_iota(jnp.int32, (n, 128), 0)
    lane = lax.broadcasted_iota(jnp.int32, (n, 128), 1)
    eye = jnp.where(row + n == lane, 1.0, 0.0)
    a = jnp.concatenate([s, jnp.zeros((n, 128 - n), F32)], axis=1) + eye
    for j in range(n):
        pivot = a[j : j + 1, :]
        inv = 1.0 / jnp.sqrt(pivot[:, j : j + 1])
        pivot = pivot * inv
        factor = a[:, j : j + 1] * inv
        a = jnp.where(row > j, a - factor * pivot, jnp.where(row == j, pivot, a))
    return a[:, n : 2 * n]


def final_kernel(
    scale, place_ref, b0_ref, b1_ref, b2_ref, b3_ref, p_ref, y_ref, a_ref, ax_ref,
    q_ref, n_ref, g_out, c_out, b_out, all_ref, qbuf_ref, nbuf_ref, g_ref, c_ref, b_ref,
    sems, small_sems,
):
    me, core = place_ref[0], place_ref[1]
    quarter = PACK // 8
    for m, ref in enumerate((b0_ref, b1_ref, b2_ref, b3_ref)):
        for h in (0, 1):
            at = (core ^ h) * 4 + (me ^ m)
            all_ref[pl.ds(pl.multiple_of(at * quarter, 8), quarter), :] = ref[
                h * quarter : (h + 1) * quarter
            ]
    row = lax.broadcasted_iota(jnp.int32, (128, 128), 0)
    col = lax.broadcasted_iota(jnp.int32, (128, 128), 1)

    def pair(at, d):
        m = all_ref[at : at + 128] * scale
        t = m.T
        diag = all_ref[768 + d : 769 + d] * scale
        return (
            jnp.where(row <= col, m, t),
            jnp.where(row > col, m, jnp.where(row < col, t, diag)),
        )

    pp, pcp = pair(0, 0)
    pgp, ygy = pair(128, 1)
    yy, ycy = pair(256, 2)
    py = all_ref[384:512] * scale
    xs = all_ref[512:640] * scale
    px, yx, ygx = xs[:, :32], xs[:, 32:64], xs[:, 64:96]
    xx, xgx = xs[:32, 96:], xs[96:, 96:]
    z = PRIOR - B

    h = py[:, z:]
    c = 2.0 * h - dot(pp, h)
    s = yy[z:, z:] + tdot(c, dot(pp, c) - 2.0 * h)
    inv_t = inverse_factor(s).T
    a, b = -dot(c, inv_t), inv_t

    hp = dot(py, a) + dot(px, b)
    wy = dot(yy, a) + dot(yx, b)
    wx = tdot(yx, a) + dot(xx, b)
    hq = tdot(a, hp) + tdot(b, wy[z:])
    kq = dot(pp, a) + dot(h, b)
    kqq = tdot(a, kq) + tdot(b, tdot(h, a) + dot(yy[z:, z:], b))
    cp = 2.0 * hp - dot(pp, hp) - dot(kq, hq)
    cq = 2.0 * hq - tdot(kq, hp) - dot(kqq, hq)
    s = (
        tdot(a, wy)
        + tdot(b, wx)
        + tdot(cp, dot(pp, cp) + dot(kq, cq) - 2.0 * hp)
        + tdot(cq, tdot(kq, cp) + dot(kqq, cq) - 2.0 * hq)
    )
    inv_t = inverse_factor(s).T
    zero_z = jnp.zeros((z, B), F32)
    u = -dot(cp + dot(a, cq), inv_t)
    v = dot(a - jnp.concatenate([zero_z, dot(b, cq)], axis=0), inv_t)
    x = dot(b, inv_t)

    zero = jnp.zeros((B, B), F32)
    tp = jnp.concatenate([a, u, jnp.zeros((128, B), F32)], axis=1)
    ty = jnp.concatenate([jnp.concatenate([zero_z, b], axis=0), v, a], axis=1)
    tx = jnp.concatenate([zero, x, b], axis=1)
    t = jnp.concatenate([m[:, :64].T for m in (tp, ty, tx)], axis=1)
    copies = combine(t, p_ref, y_ref, a_ref, ax_ref, q_ref, n_ref, qbuf_ref, nbuf_ref, sems)

    pcx, ycx, xcx = ycy[:, z:], ygy[:, z:], ygx[z:]
    cpt = dot(pcp, tp) + dot(pgp, ty) + dot(pcx, tx)
    cyt = dot(pgp, tp) + dot(ycy, ty) + dot(ycx, tx)
    cxt = tdot(pcx, tp) + tdot(ycx, ty) + dot(xcx, tx)
    qp, qy, qx = tp[:, :64], ty[:, :64], tx[:, :64]
    r = tdot(qp, cpt) + tdot(qy, cyt) + tdot(qx, cxt)
    side = cpt[:, :64]
    c_ref[0:128, 0:128] = pcp
    c_ref[0:128, 128:192] = side
    c_ref[128:192, 0:128] = side.T
    c_ref[128:192, 128:192] = r[:, :64]
    gpt = cyt[:, 32:64]
    gyt = dot(ycy, u) + dot(ygy, v) + dot(ygx, x)
    gxt = tdot(ycx, u) + tdot(ygx, v) + dot(xgx, x)
    g_ref[0:128] = jnp.concatenate([cpt[:, 64:96], gpt], axis=1)
    g2 = tdot(qp, gpt) + tdot(qy, gyt) + tdot(qx, gxt)
    g_ref[128:192] = jnp.concatenate([r[:, 64:96], g2], axis=1)
    kp = all_ref[640:768]
    extra = all_ref[512:640][:, 96:]
    kx = jnp.concatenate([extra[32:64], extra[64:96]], axis=1)
    b_ref[0:128] = kp[:, :64]
    b_ref[128:192] = tdot(qp, kp[:, :64]) + tdot(qy, kp[:, 64:]) + tdot(qx, kx)


    for j, (src, dst) in enumerate(((g_ref, g_out), (c_ref, c_out), (b_ref, b_out))):
        copy = pltpu.make_async_copy(src, dst, small_sems.at[j])
        copy.start()
        copies.append(copy)
    for copy in copies:
        copy.wait()


def final(place, pieces, p, y, ay, ax, scale):
    rows, fields, width = p.shape
    steps = rows // DEPTH
    small = ((192, 64), (192, 192), (192, 64))
    return call(
        functools.partial(final_kernel, scale),
        (shape(2 * B, rows, width), shape(B, rows, width)) + tuple(shape(*d) for d in small),
        [SM] + [VM] * 8,
        (HBM,) * 5,
        scratch=[
            pltpu.VMEM((PACK, 128), F32),
            pltpu.VMEM((steps, 2 * B, DEPTH, width), F32),
            pltpu.VMEM((steps, B, DEPTH, width), F32),
        ]
        + [pltpu.VMEM(d, F32) for d in small]
        + [pltpu.SemaphoreType.DMA((2, steps)), pltpu.SemaphoreType.DMA((3,))],
        flops=1 << 30,
        moved=5 * p.size * 4,
    )(place, *pieces, p, y, ay, ax)


def on_device(prior, cond_x, cond_y, cap_level, decap, via, ports):
    rows_here, cols_here = prior.shape[1:]
    total_cols = cols_here * lax.axis_size("gy")
    scale = 1.0 / (rows_here * lax.axis_size("gx") * total_cols)
    gxe = 0.125 * cond_x.astype(F32)
    gye = 0.125 * cond_y.astype(F32)
    gvia = 0.5 * via.astype(F32)
    cap = 0.25 * cap_level.astype(F32) * (1.0 + 2.0 * decap.astype(F32))

    p, top, low, edge = regroup(prior)
    slot = 2 * jnp.arange(rows_here)[:, None] == jnp.arange(cols_here)[None, :]
    gye_edge = jnp.sum(jnp.where(slot, gye[:, -1:], 0.0), axis=0, keepdims=True)
    spare = jnp.zeros((7, cols_here), F32)
    low = jnp.concatenate([low, gxe[-1:], spare], axis=0)
    edge_more = jnp.concatenate([edge, gye_edge, spare], axis=0)
    above, below, fl, fr = exchange(top, low, edge_more, edge)
    gxw = jnp.concatenate([above[PRIOR : PRIOR + 1], gxe[:-1]], axis=0)
    gys_first = jnp.sum(jnp.where(slot, fl[PRIOR : PRIOR + 1], 0.0), axis=1, keepdims=True)
    gys = jnp.concatenate([gys_first, gye[:, :-1]], axis=1)
    center = gvia + gxe + gxw + gye + gys
    coef = jnp.stack([center, gxe, gxw, gye, gys, 1.0 / cap])

    y, top, low, edge = stencil(coef, p, above[:PRIOR], below, fl[:PRIOR], fr)
    sides = exchange(top, low, edge, edge)
    pp, pcp, py, yy, pgp, ygp = gram_y(cap, p, y)
    ay, top, low, edge = stencil(coef, y, *sides)
    top, low, edge = (a[PRIOR - B :] for a in (top, low, edge))
    sides = exchange(top, low, edge, edge)

    port_rows = ports // total_cols - lax.axis_index("gx") * rows_here
    port_cols = ports % total_cols - lax.axis_index("gy") * cols_here
    inside = (
        (port_rows >= 0) & (port_rows < rows_here) & (port_cols >= 0) & (port_cols < cols_here)
    )
    where = jnp.stack(
        [
            jnp.clip(port_rows, 0, rows_here - 1),
            jnp.clip(port_cols, 0, cols_here - 1),
            inside.astype(jnp.int32),
        ]
    )
    ygy, xs, kp, kx = gram_x(where, cap, p, y, ay)
    core = lax.axis_index("gx") % 2
    ax, keep, give = last(
        core[None], coef, ay, sides, [pp, pcp, py, yy, pgp, ygp, ygy, xs, kp, kx]
    )
    place = jnp.stack([lax.axis_index("gy"), core])
    pieces = sum_over_devices(keep, give)
    return tuple(final(place, pieces, p, y, ay, ax, scale))


def solution(mesh):
    in_specs = (
        P(None, "gx", "gy"),
        P("gx", "gy"),
        P("gx", "gy"),
        P("gx", "gy"),
        P("gx", "gy"),
        P("gx", "gy"),
        P(),
    )
    out_specs = (P(None, "gx", "gy"), P(None, "gx", "gy"), P(), P(), P())
    return jax.shard_map(
        on_device, mesh=mesh, in_specs=in_specs, out_specs=out_specs, check_vma=False
    )
```

```python
import functools

import jax
import jax.numpy as jnp
from jax import lax
from jax.experimental import pallas as pl
from jax.experimental.pallas import tpu as pltpu
from jax.sharding import PartitionSpec as P

B = 32
PRIOR = 128
F32 = jnp.float32
HI = lax.Precision.HIGHEST
MIB = 1024 * 1024
TILE = 32
CHUNK = 16
DEPTH = 8
PACK = 832
VM = pl.BlockSpec(memory_space=pltpu.VMEM)
SM = pl.BlockSpec(memory_space=pltpu.SMEM)
HBM = pl.BlockSpec(memory_space=pltpu.HBM)
ANY = pl.BlockSpec(memory_space=pl.ANY)


def call(kernel, out, in_specs, out_specs, scratch=(), flops=0, moved=0, limit=24, aliases={}):
    return pl.pallas_call(
        kernel,
        out_shape=out,
        in_specs=in_specs,
        out_specs=out_specs,
        scratch_shapes=scratch,
        input_output_aliases=aliases,
        compiler_params=pltpu.CompilerParams(vmem_limit_bytes=limit * MIB),
        cost_estimate=pl.CostEstimate(flops=flops, bytes_accessed=moved, transcendentals=0),
    )


def shape(*dims):
    return jax.ShapeDtypeStruct(dims, F32)


def held(*dims):
    return pltpu.VMEM(dims, F32)


def in_hbm(x):
    return pltpu.with_memory_space_constraint(x, pltpu.HBM)


def lanes_of(dims):
    return lax.broadcasted_iota(jnp.int32, dims, len(dims) - 1)


def pack_edges(v_ref, edge_ref):
    rows, fields, width = v_ref.shape
    slot = lanes_of((TILE, width)) >> 1
    for at in range(0, fields, TILE):
        edge = jnp.zeros((TILE, width), F32)
        for r in range(rows):
            edge = jnp.where(
                slot == r, pltpu.roll(v_ref[r, at : at + TILE, :], 2 * r + 1, 1), edge
            )
        edge_ref[at : at + TILE] = edge


def ends(v_ref, top_ref, low_ref):
    top_ref[...] = v_ref[0]
    low_ref[...] = v_ref[v_ref.shape[0] - 1]


def regroup_kernel(p_ref, out_hbm, top_ref, low_ref, edge_ref, buf_ref, out_ref, sems):
    parts, fields, rows, width = buf_ref.shape
    copies = [
        pltpu.make_async_copy(p_ref.at[pl.ds(i * fields, fields)], buf_ref.at[i], sems.at[0, i])
        for i in range(parts)
    ]
    back = []
    for copy in copies:
        copy.start()
    for i in range(parts):
        copies[i].wait()
        cut = slice(i * fields, (i + 1) * fields)
        for at in range(0, rows, DEPTH):
            flat = buf_ref.at[i].reshape(fields * rows, width)
            got = [flat[pl.ds(at + k, fields, stride=rows), :] for k in range(DEPTH)]
            for k in range(DEPTH):
                out_ref[at + k, cut, :] = got[k]
        held_part = (slice(None), pl.ds(i * fields, fields), slice(None))
        back.append(
            pltpu.make_async_copy(out_ref.at[held_part], out_hbm.at[held_part], sems.at[1, i])
        )
        back[-1].start()
    pack_edges(out_ref, edge_ref)
    ends(out_ref, top_ref, low_ref)
    for copy in back:
        copy.wait()


def regroup(prior):
    fields, rows, width = prior.shape
    parts = fields // CHUNK
    return call(
        regroup_kernel,
        (pltpu.HBM((rows, fields, width), F32),) + (shape(fields, width),) * 3,
        [HBM],
        (HBM,) + (VM,) * 3,
        scratch=[
            pltpu.VMEM((parts, CHUNK, rows, width), F32),
            pltpu.VMEM((rows, fields, width), F32),
            pltpu.SemaphoreType.DMA((2, parts)),
        ],
        moved=2 * prior.size * 4,
        limit=40,
    )(in_hbm(prior))


def stencil_rows(
    coef_ref, v_ref, first, above_ref, below_ref, fl_ref, fr_ref, seam_ref, put, ready=None
):
    rows, width = v_ref.shape[0], v_ref.shape[2]
    fields = above_ref.shape[0]
    tile = 8
    lane = lanes_of((tile, width))
    odd, start, stop = (lane & 1) == 1, lane == 0, lane == width - 1
    for at in range(0, fields, tile):
        cut = slice(at, at + tile)
        seam_ref[cut] = jnp.where(
            odd, pltpu.roll(fl_ref[cut], 1, 1), pltpu.roll(fr_ref[cut], width - 1, 1)
        )
    for r in range(rows):
        if ready is not None:
            ready(r)
        c = [jnp.broadcast_to(coef_ref[k, r : r + 1, :], (tile, width)) for k in range(6)]
        for at in range(0, fields, tile):
            cut = slice(at, at + tile)
            src = slice(first + at, first + at + tile)
            v = v_ref[r, src, :]
            up = above_ref[cut] if r == 0 else v_ref[r - 1, src, :]
            down = below_ref[cut] if r == rows - 1 else v_ref[r + 1, src, :]
            side = pltpu.roll(seam_ref[cut], width - 1 - 2 * r, 1)
            south = jnp.where(start, side, pltpu.roll(v, 1, 1))
            north = jnp.where(stop, side, pltpu.roll(v, width - 1, 1))
            put(r, cut, c[0] * v - c[1] * down - c[2] * up - c[3] * north - c[4] * south, c[5])


def stencil_kernel(
    coef_ref, v_ref, above_ref, below_ref, fl_ref, fr_ref, y_ref, top_ref, low_ref, edge_ref,
    seam_ref,
):
    def put(r, cut, image, inv_cap):
        y_ref[r, cut, :] = image * inv_cap

    stencil_rows(coef_ref, v_ref, 0, above_ref, below_ref, fl_ref, fr_ref, seam_ref, put)
    pack_edges(y_ref, edge_ref)
    ends(y_ref, top_ref, low_ref)


def first_stencil_kernel(
    coef_ref, p_hbm, above_ref, below_ref, fl_ref, fr_ref, y_ref, p_ref, top_ref, low_ref,
    edge_ref, seam_ref, sems,
):
    rows = p_ref.shape[0]
    copies = []
    for i in range(rows // CHUNK):
        part = pl.ds(i * CHUNK, CHUNK)
        copies.append(pltpu.make_async_copy(p_hbm.at[part], p_ref.at[part], sems.at[i]))
        copies[-1].start()

    def ready(r):
        if r == 0:
            copies[0].wait()
        if r % CHUNK == CHUNK - 1 and r + 1 < rows:
            copies[r // CHUNK + 1].wait()

    def put(r, cut, image, inv_cap):
        y_ref[r, cut, :] = image * inv_cap

    stencil_rows(
        coef_ref, p_ref, 0, above_ref, below_ref, fl_ref, fr_ref, seam_ref, put, ready
    )
    pack_edges(y_ref, edge_ref)
    ends(y_ref, top_ref, low_ref)


def first_stencil(coef, p, above, below, from_left, from_right):
    rows, fields, width = p.shape
    return call(
        first_stencil_kernel,
        (held(rows, fields, width),) * 2 + (shape(fields, width),) * 3,
        [VM, HBM] + [VM] * 4,
        (VM,) * 5,
        scratch=[pltpu.VMEM((fields, width), F32), pltpu.SemaphoreType.DMA((rows // CHUNK,))],
        flops=12 * p.size,
        moved=2 * p.size * 4,
        limit=32,
    )(coef, in_hbm(p), above, below, from_left, from_right)


def stencil(coef, v, above, below, from_left, from_right):
    rows, fields, width = v.shape
    return call(
        stencil_kernel,
        (held(rows, fields, width),) + (shape(fields, width),) * 3,
        [VM] * 6,
        (VM,) * 4,
        scratch=[pltpu.VMEM((fields, width), F32)],
        flops=12 * v.size,
        moved=2 * v.size * 4,
    )(coef, v, above, below, from_left, from_right)


def wide(ref, at):
    return jnp.concatenate([ref[at + i] for i in range(CHUNK)], axis=1)


def wide_row(ref, at):
    return jnp.concatenate([ref[pl.ds(at + i, 1), :] for i in range(CHUNK)], axis=1)


def halves(x):
    high = x.astype(jnp.bfloat16)
    low = (x - high.astype(F32)).astype(jnp.bfloat16)
    return jnp.concatenate([high, low], axis=0)


def nt(a, b):
    return lax.dot_general(a, b, (((1,), (1,)), ((), ())), preferred_element_type=F32)


def fold(acc, row, rows, col, cols):
    a = acc[row : row + rows, col : col + cols] + acc[row : row + rows, col + cols : col + 2 * cols]
    row += rows
    b = acc[row : row + rows, col : col + cols] + acc[row : row + rows, col + cols : col + 2 * cols]
    return a + b


def over_chunks(rows, accs, terms):
    def add(i, carry):
        for acc, term in zip(accs, terms(i * CHUNK)):
            acc[...] += term
        return carry

    for acc in accs:
        acc[...] = jnp.zeros_like(acc)
    lax.fori_loop(0, rows // CHUNK, add, 0)


def gram_p_kernel(cap_ref, p_ref, pp_ref, pcp_ref, acc_ref):
    def terms(at):
        p = wide(p_ref, at)
        hp = halves(p)
        yield nt(hp, jnp.concatenate([hp, halves(p * wide_row(cap_ref, at))], axis=0))

    over_chunks(p_ref.shape[0], (acc_ref,), terms)
    pp_ref[...] = fold(acc_ref, 0, 128, 0, 128)
    pcp_ref[...] = fold(acc_ref, 0, 128, 256, 128)


def gram_y_kernel(cap_ref, p_ref, y_ref, py_ref, pgp_ref, acc_ref):
    def terms(at):
        y = wide(y_ref, at)
        right = jnp.concatenate([halves(y), halves(y * wide_row(cap_ref, at))], axis=0)
        yield nt(halves(wide(p_ref, at)), right)

    over_chunks(p_ref.shape[0], (acc_ref,), terms)
    py_ref[...] = fold(acc_ref, 0, 128, 0, 128)
    pgp_ref[...] = fold(acc_ref, 0, 128, 256, 128)


def gram_a_kernel(cap_ref, y_ref, a_ref, ygy_ref, acc_ref):
    def terms(at):
        yield nt(halves(wide(y_ref, at)), halves(wide(a_ref, at) * wide_row(cap_ref, at)))

    over_chunks(y_ref.shape[0], (acc_ref,), terms)
    ygy_ref[...] = fold(acc_ref, 0, 128, 0, 128)


def gram_x_kernel(cap_ref, p_ref, y_ref, a_ref, x_ref, acc_ref):
    def terms(at):
        ay = wide(a_ref, at)
        hx = halves(ay[PRIOR - B :])
        left = [halves(wide(p_ref, at)), halves(wide(y_ref, at))]
        yield nt(jnp.concatenate(left + [halves(ay * wide_row(cap_ref, at)), hx], axis=0), hx)

    over_chunks(p_ref.shape[0], (acc_ref,), terms)
    px = fold(acc_ref, 0, 128, 0, B)
    yx = fold(acc_ref, 256, 128, 0, B)
    gx = fold(acc_ref, 512, 128, 0, B)
    xx = fold(acc_ref, 768, B, 0, B)
    rest = jnp.concatenate([xx, jnp.zeros((128 - B, B), F32)], axis=0)
    x_ref[...] = jnp.concatenate([px, yx, gx, rest], axis=1)


def pick_kernel(where_ref, p_ref, y_ref, a_ref, kp_ref, kx_ref):
    kp_ref[...] = jnp.zeros_like(kp_ref)
    kx_ref[...] = jnp.zeros_like(kx_ref)
    n = where_ref.shape[1]

    def step(k, carry):
        @pl.when(where_ref[2, k] > 0)
        def _():
            r, c = where_ref[0, k], where_ref[1, k]
            for v, spot, out_ref in (
                (p_ref[r], k, kp_ref),
                (y_ref[r], k + n, kp_ref),
                (a_ref[r][PRIOR - B :], k, kx_ref),
            ):
                moved = pltpu.roll(v, lax.rem(spot - c + 128, 128), 1)
                out_ref[...] = jnp.where(lanes_of(v.shape) == spot, moved, out_ref[...])

        return carry

    lax.fori_loop(0, n, step, 0)


def gram(kernel, cap, arrays, n_out, acc, thread):
    def body(*refs):
        inputs = 1 + len(arrays)
        kernel(*refs[:inputs], *refs[inputs + 1 : inputs + 1 + n_out], refs[-1])

    return call(
        body,
        (shape(128, 128),) * n_out + (shape(*thread.shape),),
        [VM] * (1 + len(arrays)) + [ANY],
        (VM,) * n_out + (ANY,),
        scratch=[pltpu.VMEM(acc, F32)],
        flops=2 * acc[0] * acc[1] * arrays[0].shape[0] * 128,
        moved=len(arrays) * arrays[0].size * 4,
        aliases={1 + len(arrays): n_out},
    )(cap, *arrays, thread)


def pick(where, p, y, ay, thread):
    def body(where_ref, p_ref, y_ref, a_ref, t_ref, kp_ref, kx_ref, t_out):
        pick_kernel(where_ref, p_ref, y_ref, a_ref, kp_ref, kx_ref)

    return call(
        body,
        (shape(128, 128), shape(B, 128), shape(*thread.shape)),
        [SM] + [VM] * 3 + [ANY],
        (VM,) * 2 + (ANY,),
        moved=1 << 18,
        aliases={4: 2},
    )(where, p, y, ay, thread)


def last_kernel(
    core_ref, coef_ref, a_ref, above_ref, below_ref, fl_ref, fr_ref,
    pp_ref, pcp_ref, py_ref, yy_ref, pgp_ref, ygp_ref, ygy_ref, x_ref, kp_ref, kx_ref,
    ax_hbm, keep_ref, give_ref, ax_ref, image_ref, pack_ref, seam_ref, sem,
):
    def put(r, cut, image, inv_cap):
        ax_ref[r, cut, :] = image * inv_cap
        image_ref[r, cut, :] = image

    stencil_rows(
        coef_ref, a_ref, PRIOR - B, above_ref, below_ref, fl_ref, fr_ref, seam_ref, put
    )
    copy = pltpu.make_async_copy(ax_ref, ax_hbm, sem)
    copy.start()
    acc = jnp.zeros((2 * B, 2 * B), F32)
    for at in range(0, a_ref.shape[0], CHUNK):
        hx = halves(wide(a_ref, at)[PRIOR - B :])
        acc = acc + nt(hx, halves(wide(image_ref, at)))
    xgx = fold(acc, 0, B, 0, B)
    row = lax.broadcasted_iota(jnp.int32, (128, 128), 0)
    col = lax.broadcasted_iota(jnp.int32, (128, 128), 1)

    def diagonal(m):
        return jnp.sum(jnp.where(row == col, m, 0.0), axis=0, keepdims=True)

    pack_ref[0:128] = jnp.where(row <= col, pp_ref[...], pcp_ref[...])
    pack_ref[128:256] = jnp.where(row <= col, pgp_ref[...], ygy_ref[...])
    pack_ref[256:384] = jnp.where(row <= col, yy_ref[...], ygp_ref[...])
    pack_ref[384:512] = py_ref[...]
    kx = kx_ref[...]
    extra = jnp.concatenate([jnp.zeros((B, B), F32), kx[:, :B], kx[:, B : 2 * B], xgx], axis=0)
    pack_ref[512:640] = x_ref[...] + jnp.concatenate([jnp.zeros((128, 96), F32), extra], axis=1)
    pack_ref[640:768] = kp_ref[...]
    diag = [diagonal(m[...]) for m in (pcp_ref, ygy_ref, ygp_ref)]
    pack_ref[768:776] = jnp.concatenate(diag + [jnp.zeros((5, 128), F32)], axis=0)
    pack_ref[776:832] = jnp.zeros((56, 128), F32)
    half = PACK // 2
    core = core_ref[0]
    keep_ref[...] = pack_ref[pl.ds(pl.multiple_of(core * half, 8), half), :]
    give_ref[...] = pack_ref[pl.ds(pl.multiple_of((1 - core) * half, 8), half), :]
    copy.wait()


def last(core, coef, ay, sides, mats):
    rows, fields, width = ay.shape
    return call(
        last_kernel,
        (pltpu.HBM((rows, B, width), F32), shape(PACK // 2, 128), shape(PACK // 2, 128)),
        [SM] + [VM] * (2 + len(sides) + len(mats)),
        (HBM, VM, VM),
        scratch=[
            pltpu.VMEM((rows, B, width), F32),
            pltpu.VMEM((rows, B, width), F32),
            pltpu.VMEM((PACK, 128), F32),
            pltpu.VMEM((B, width), F32),
            pltpu.SemaphoreType.DMA,
        ],
        flops=1 << 27,
        moved=2 * rows * B * width * 4,
    )(core, coef, ay, *sides, *mats)


def split(x):
    high = x.astype(jnp.bfloat16)
    return high, (x - high.astype(F32)).astype(jnp.bfloat16)


def times(t, pair):
    rows = t.shape[0] // 2
    big = jnp.dot(t, pair[0], preferred_element_type=F32)
    return big[:rows] + big[rows:] + jnp.dot(t[:rows], pair[1], preferred_element_type=F32)


def combine(t, p_ref, y_ref, a_ref, ax_ref, q_ref, n_ref, qbuf_ref, nbuf_ref, sems):
    two = 2 * B
    high, low = split(t)

    def cut(lo, hi, first):
        return jnp.concatenate([high[first:, lo:hi], low[first:, lo:hi]], axis=0)

    t_py, t_x, t_y, t_rest = cut(0, 256, 0), cut(256, 288, 0), cut(0, 128, B), cut(128, 288, B)
    rows, fields, width = p_ref.shape
    copies = []
    for at in range(0, rows, DEPTH):

        def row_block(ref):
            return jnp.concatenate([ref[at + i] for i in range(DEPTH)], axis=1)

        p, y = split(row_block(p_ref)), split(row_block(y_ref))
        a, ax = split(row_block(a_ref)), split(row_block(ax_ref))
        py = tuple(jnp.concatenate(pair, axis=0) for pair in zip(p, y))
        rest = tuple(jnp.concatenate(pair, axis=0) for pair in zip(a, ax))
        x = tuple(part[PRIOR - B :] for part in a)
        q = times(t_py, py) + times(t_x, x)
        n = times(t_y, y) + times(t_rest, rest)
        step = at // DEPTH
        for k in range(DEPTH):
            lanes = slice(k * width, (k + 1) * width)
            qbuf_ref.at[step].reshape(two * DEPTH, width)[pl.ds(k, two, stride=DEPTH), :] = q[
                :, lanes
            ]
            nbuf_ref.at[step].reshape(B * DEPTH, width)[pl.ds(k, B, stride=DEPTH), :] = n[
                :, lanes
            ]
        for j, (src, dst) in enumerate(((qbuf_ref, q_ref), (nbuf_ref, n_ref))):
            copy = pltpu.make_async_copy(
                src.at[step], dst.at[:, pl.ds(at, DEPTH), :], sems.at[j, step]
            )
            copy.start()
            copies.append(copy)
    return copies


def swap(x, axis, mask):
    return lax.ppermute(x, axis, [(i, i ^ mask) for i in range(lax.axis_size(axis))])


def shift(x, axis, step):
    size = lax.axis_size(axis)
    return lax.ppermute(
        x, axis, [(i, i + step) for i in range(size) if 0 <= i + step < size]
    )


def quad_sum(parts):
    return (parts[0] + parts[1]) + (parts[2] + parts[3])


def sum_over_devices(keep, give):
    x = keep + swap(give, "gx", 1)
    me = lax.axis_index("gy")
    quarter = x.shape[0] // 4
    parts = [
        lax.dynamic_slice_in_dim(x, (me ^ m) * quarter, quarter, 0) for m in range(4)
    ]
    x = quad_sum([parts[0]] + [swap(parts[m], "gy", m) for m in (1, 2, 3)])
    mask = 2
    while mask < lax.axis_size("gx"):
        x = x + swap(x, "gx", mask)
        mask *= 2
    x = jnp.concatenate([x, swap(x, "gx", 1)], axis=0)
    return [x] + [swap(x, "gy", m) for m in (1, 2, 3)]


def exchange(top, low, edge, edge_left, works=()):
    sends = [(edge, "gy", 1), (edge_left, "gy", -1), (low, "gx", 1), (top, "gx", -1)]
    got, done = [], []
    for k, (x, axis, step) in enumerate(sends):
        if 0 < k <= len(works):
            *out, x = works[k - 1](x)
            done.append(out)
        got.append(shift(x, axis, step))
    return got[2:] + got[:2], done


def dot(a, b):
    return jnp.dot(a, b, precision=HI, preferred_element_type=F32)


def tdot(a, b):
    return lax.dot_general(
        a, b, (((0,), (0,)), ((), ())), precision=HI, preferred_element_type=F32
    )


def inverse_factor(s):
    n = s.shape[0]
    s = 0.5 * (s + s.T)
    row = lax.broadcasted_iota(jnp.int32, (n, 128), 0)
    lane = lax.broadcasted_iota(jnp.int32, (n, 128), 1)
    eye = jnp.where(row + n == lane, 1.0, 0.0)
    a = jnp.concatenate([s, jnp.zeros((n, 128 - n), F32)], axis=1) + eye
    for j in range(n):
        pivot = a[j : j + 1, :]
        inv = 1.0 / jnp.sqrt(pivot[:, j : j + 1])
        pivot = pivot * inv
        factor = a[:, j : j + 1] * inv
        a = jnp.where(row > j, a - factor * pivot, jnp.where(row == j, pivot, a))
    return a[:, n : 2 * n]


def final_kernel(
    scale, place_ref, b0_ref, b1_ref, b2_ref, b3_ref, p_hbm, y_hbm, a_hbm, ax_hbm,
    q_ref, n_ref, g_out, c_out, b_out, p_ref, y_ref, a_ref, ax_ref, all_ref, qbuf_ref, nbuf_ref,
    g_ref, c_ref, b_ref, load_sems, sems, small_sems,
):
    pairs = ((p_hbm, p_ref), (y_hbm, y_ref), (a_hbm, a_ref), (ax_hbm, ax_ref))
    loads = [
        pltpu.make_async_copy(src, dst, load_sems.at[j]) for j, (src, dst) in enumerate(pairs)
    ]
    for load in loads:
        load.start()
    me, core = place_ref[0], place_ref[1]
    quarter = PACK // 8
    for m, ref in enumerate((b0_ref, b1_ref, b2_ref, b3_ref)):
        for h in (0, 1):
            at = (core ^ h) * 4 + (me ^ m)
            all_ref[pl.ds(pl.multiple_of(at * quarter, 8), quarter), :] = ref[
                h * quarter : (h + 1) * quarter
            ]
    row = lax.broadcasted_iota(jnp.int32, (128, 128), 0)
    col = lax.broadcasted_iota(jnp.int32, (128, 128), 1)

    def pair(at, d):
        m = all_ref[at : at + 128] * scale
        t = m.T
        diag = all_ref[768 + d : 769 + d] * scale
        return (
            jnp.where(row <= col, m, t),
            jnp.where(row > col, m, jnp.where(row < col, t, diag)),
        )

    pp, pcp = pair(0, 0)
    pgp, ygy = pair(128, 1)
    yy, ycy = pair(256, 2)
    py = all_ref[384:512] * scale
    xs = all_ref[512:640] * scale
    px, yx, ygx = xs[:, :32], xs[:, 32:64], xs[:, 64:96]
    xx, xgx = xs[:32, 96:], xs[96:, 96:]
    z = PRIOR - B

    h = py[:, z:]
    c = 2.0 * h - dot(pp, h)
    s = yy[z:, z:] + tdot(c, dot(pp, c) - 2.0 * h)
    inv_t = inverse_factor(s).T
    a, b = -dot(c, inv_t), inv_t

    hp = dot(py, a) + dot(px, b)
    wy = dot(yy, a) + dot(yx, b)
    wx = tdot(yx, a) + dot(xx, b)
    hq = tdot(a, hp) + tdot(b, wy[z:])
    kq = dot(pp, a) + dot(h, b)
    kqq = tdot(a, kq) + tdot(b, tdot(h, a) + dot(yy[z:, z:], b))
    cp = 2.0 * hp - dot(pp, hp) - dot(kq, hq)
    cq = 2.0 * hq - tdot(kq, hp) - dot(kqq, hq)
    s = (
        tdot(a, wy)
        + tdot(b, wx)
        + tdot(cp, dot(pp, cp) + dot(kq, cq) - 2.0 * hp)
        + tdot(cq, tdot(kq, cp) + dot(kqq, cq) - 2.0 * hq)
    )
    inv_t = inverse_factor(s).T
    zero_z = jnp.zeros((z, B), F32)
    u = -dot(cp + dot(a, cq), inv_t)
    v = dot(a - jnp.concatenate([zero_z, dot(b, cq)], axis=0), inv_t)
    x = dot(b, inv_t)

    zero = jnp.zeros((B, B), F32)
    tp = jnp.concatenate([a, u, jnp.zeros((128, B), F32)], axis=1)
    ty = jnp.concatenate([jnp.concatenate([zero_z, b], axis=0), v, a], axis=1)
    tx = jnp.concatenate([zero, x, b], axis=1)
    t = jnp.concatenate([m[:, :64].T for m in (tp, ty, tx)], axis=1)
    for load in loads:
        load.wait()
    copies = combine(t, p_ref, y_ref, a_ref, ax_ref, q_ref, n_ref, qbuf_ref, nbuf_ref, sems)

    pcx, ycx, xcx = ycy[:, z:], ygy[:, z:], ygx[z:]
    cpt = dot(pcp, tp) + dot(pgp, ty) + dot(pcx, tx)
    cyt = dot(pgp, tp) + dot(ycy, ty) + dot(ycx, tx)
    cxt = tdot(pcx, tp) + tdot(ycx, ty) + dot(xcx, tx)
    qp, qy, qx = tp[:, :64], ty[:, :64], tx[:, :64]
    r = tdot(qp, cpt) + tdot(qy, cyt) + tdot(qx, cxt)
    side = cpt[:, :64]
    c_ref[0:128, 0:128] = pcp
    c_ref[0:128, 128:192] = side
    c_ref[128:192, 0:128] = side.T
    c_ref[128:192, 128:192] = r[:, :64]
    gpt = cyt[:, 32:64]
    gyt = dot(ycy, u) + dot(ygy, v) + dot(ygx, x)
    gxt = tdot(ycx, u) + tdot(ygx, v) + dot(xgx, x)
    g_ref[0:128] = jnp.concatenate([cpt[:, 64:96], gpt], axis=1)
    g2 = tdot(qp, gpt) + tdot(qy, gyt) + tdot(qx, gxt)
    g_ref[128:192] = jnp.concatenate([r[:, 64:96], g2], axis=1)
    kp = all_ref[640:768]
    extra = all_ref[512:640][:, 96:]
    kx = jnp.concatenate([extra[32:64], extra[64:96]], axis=1)
    b_ref[0:128] = kp[:, :64]
    b_ref[128:192] = tdot(qp, kp[:, :64]) + tdot(qy, kp[:, 64:]) + tdot(qx, kx)


    for j, (src, dst) in enumerate(((g_ref, g_out), (c_ref, c_out), (b_ref, b_out))):
        copy = pltpu.make_async_copy(src, dst, small_sems.at[j])
        copy.start()
        copies.append(copy)
    for copy in copies:
        copy.wait()


def final(place, pieces, p, y, ay, ax, scale):
    rows, fields, width = p.shape
    steps = rows // DEPTH
    small = ((192, 64), (192, 192), (192, 64))
    return call(
        functools.partial(final_kernel, scale),
        (shape(2 * B, rows, width), shape(B, rows, width)) + tuple(shape(*d) for d in small),
        [SM] + [VM] * 4 + [HBM] * 4,
        (HBM,) * 5,
        scratch=[pltpu.VMEM(p.shape, F32)] * 3
        + [
            pltpu.VMEM(ax.shape, F32),
            pltpu.VMEM((PACK, 128), F32),
            pltpu.VMEM((steps, 2 * B, DEPTH, width), F32),
            pltpu.VMEM((steps, B, DEPTH, width), F32),
        ]
        + [pltpu.VMEM(d, F32) for d in small]
        + [pltpu.SemaphoreType.DMA(d) for d in ((4,), (2, steps), (3,))],
        flops=1 << 30,
        moved=5 * p.size * 4,
        limit=40,
    )(place, *pieces, *(in_hbm(a) for a in (p, y, ay, ax)))


def on_device(prior, cond_x, cond_y, cap_level, decap, via, ports):
    rows_here, cols_here = prior.shape[1:]
    total_cols = cols_here * lax.axis_size("gy")
    scale = 1.0 / (rows_here * lax.axis_size("gx") * total_cols)
    gxe = 0.125 * cond_x.astype(F32)
    gye = 0.125 * cond_y.astype(F32)
    gvia = 0.5 * via.astype(F32)
    cap = 0.25 * cap_level.astype(F32) * (1.0 + 2.0 * decap.astype(F32))

    p, top, low, edge = regroup(prior)
    slot = 2 * jnp.arange(rows_here)[:, None] == jnp.arange(cols_here)[None, :]
    gye_edge = jnp.sum(jnp.where(slot, gye[:, -1:], 0.0), axis=0, keepdims=True)
    spare = jnp.zeros((7, cols_here), F32)
    low = jnp.concatenate([low, gxe[-1:], spare], axis=0)
    edge_more = jnp.concatenate([edge, gye_edge, spare], axis=0)
    (above, below, fl, fr), _ = exchange(top, low, edge_more, edge)
    gxw = jnp.concatenate([above[PRIOR : PRIOR + 1], gxe[:-1]], axis=0)
    gys_first = jnp.sum(jnp.where(slot, fl[PRIOR : PRIOR + 1], 0.0), axis=1, keepdims=True)
    gys = jnp.concatenate([gys_first, gye[:, :-1]], axis=1)
    center = gvia + gxe + gxw + gye + gys
    coef = jnp.stack([center, gxe, gxw, gye, gys, 1.0 / cap])

    port_rows = ports // total_cols - lax.axis_index("gx") * rows_here
    port_cols = ports % total_cols - lax.axis_index("gy") * cols_here
    inside = (
        (port_rows >= 0) & (port_rows < rows_here) & (port_cols >= 0) & (port_cols < cols_here)
    )
    where = jnp.stack(
        [
            jnp.clip(port_rows, 0, rows_here - 1),
            jnp.clip(port_cols, 0, cols_here - 1),
            inside.astype(jnp.int32),
        ]
    )
    y, p_in, top, low, edge = first_stencil(coef, p, above[:PRIOR], below, fl[:PRIOR], fr)
    works = [
        lambda x: gram(gram_p_kernel, cap, [p_in], 2, (256, 512), x),
        lambda x: gram(gram_y_kernel, cap, [p_in, y], 2, (256, 512), x),
        lambda x: gram(gram_y_kernel, cap, [y, y], 2, (256, 512), x),
    ]
    sides, ((pp, pcp), (py, pgp), (yy, ygp)) = exchange(top, low, edge, edge, works)
    ay, top, low, edge = stencil(coef, y, *sides)
    top, low, edge = (a[PRIOR - B :] for a in (top, low, edge))
    works = [
        lambda x: gram(gram_a_kernel, cap, [y, ay], 1, (256, 256), x),
        lambda x: gram(gram_x_kernel, cap, [p_in, y, ay], 1, (832, 64), x),
        lambda x: pick(where, p_in, y, ay, x),
    ]
    sides, ((ygy,), (xs,), (kp, kx)) = exchange(top, low, edge, edge, works)
    core = lax.axis_index("gx") % 2
    ax, keep, give = last(
        core[None], coef, ay, sides, [pp, pcp, py, yy, pgp, ygp, ygy, xs, kp, kx]
    )
    place = jnp.stack([lax.axis_index("gy"), core])
    pieces = sum_over_devices(keep, give)
    return tuple(final(place, pieces, p, y, ay, ax, scale))


def solution(mesh):
    in_specs = (
        P(None, "gx", "gy"),
        P("gx", "gy"),
        P("gx", "gy"),
        P("gx", "gy"),
        P("gx", "gy"),
        P("gx", "gy"),
        P(),
    )
    out_specs = (P(None, "gx", "gy"), P(None, "gx", "gy"), P(), P(), P())
    return jax.shard_map(
        on_device, mesh=mesh, in_specs=in_specs, out_specs=out_specs, check_vma=False
    )
```

```python
import functools

import jax
import jax.numpy as jnp
from jax import lax
from jax.experimental import pallas as pl
from jax.experimental.pallas import tpu as pltpu
from jax.sharding import PartitionSpec as P

B = 32
PRIOR = 128
F32 = jnp.float32
HI = lax.Precision.HIGHEST
MIB = 1024 * 1024
TILE = 32
CHUNK = 16
DEPTH = 8
PACK = 832
VM = pl.BlockSpec(memory_space=pltpu.VMEM)
SM = pl.BlockSpec(memory_space=pltpu.SMEM)
HBM = pl.BlockSpec(memory_space=pltpu.HBM)
ANY = pl.BlockSpec(memory_space=pl.ANY)


def call(kernel, out, in_specs, out_specs, scratch=(), flops=0, moved=0, limit=24, aliases={}):
    return pl.pallas_call(
        kernel,
        out_shape=out,
        in_specs=in_specs,
        out_specs=out_specs,
        scratch_shapes=scratch,
        input_output_aliases=aliases,
        compiler_params=pltpu.CompilerParams(vmem_limit_bytes=limit * MIB),
        cost_estimate=pl.CostEstimate(flops=flops, bytes_accessed=moved, transcendentals=0),
    )


def shape(*dims):
    return jax.ShapeDtypeStruct(dims, F32)


def held(*dims):
    return pltpu.VMEM(dims, F32)


def in_hbm(x):
    return pltpu.with_memory_space_constraint(x, pltpu.HBM)


def lanes_of(dims):
    return lax.broadcasted_iota(jnp.int32, dims, len(dims) - 1)


def pack_edges(v_ref, edge_ref, skip=0):
    rows, fields, width = v_ref.shape
    slot = lanes_of((TILE, width)) >> 1
    for at in range(skip, fields, TILE):
        edge = jnp.zeros((TILE, width), F32)
        for r in range(rows):
            edge = jnp.where(
                slot == r, pltpu.roll(v_ref[r, at : at + TILE, :], 2 * r + 1, 1), edge
            )
        edge_ref[at - skip : at - skip + TILE] = edge


def ends(core, v_ref, mate_ref, cross_ref, first=0):
    top = v_ref[0, first:, :]
    low = v_ref[v_ref.shape[0] - 1, first:, :]
    mate_ref[...] = jnp.where(core == 0, low, top)
    cross_ref[...] = jnp.where(core == 0, top, low)


def regroup_kernel(
    core_ref, p_ref, out_hbm, mate_ref, cross_ref, edge_ref, buf_ref, out_ref, sems
):
    parts, fields, rows, width = buf_ref.shape
    copies = [
        pltpu.make_async_copy(p_ref.at[pl.ds(i * fields, fields)], buf_ref.at[i], sems.at[0, i])
        for i in range(parts)
    ]
    back = []
    for copy in copies:
        copy.start()
    for i in range(parts):
        copies[i].wait()
        cut = slice(i * fields, (i + 1) * fields)
        for at in range(0, rows, DEPTH):
            flat = buf_ref.at[i].reshape(fields * rows, width)
            got = [flat[pl.ds(at + k, fields, stride=rows), :] for k in range(DEPTH)]
            for k in range(DEPTH):
                out_ref[at + k, cut, :] = got[k]
        held_part = (slice(None), pl.ds(i * fields, fields), slice(None))
        back.append(
            pltpu.make_async_copy(out_ref.at[held_part], out_hbm.at[held_part], sems.at[1, i])
        )
        back[-1].start()
    pack_edges(out_ref, edge_ref)
    ends(core_ref[0], out_ref, mate_ref, cross_ref)
    for copy in back:
        copy.wait()


def regroup(core, prior):
    fields, rows, width = prior.shape
    parts = fields // CHUNK
    return call(
        regroup_kernel,
        (pltpu.HBM((rows, fields, width), F32),) + (shape(fields, width),) * 3,
        [SM, HBM],
        (HBM,) + (VM,) * 3,
        scratch=[
            pltpu.VMEM((parts, CHUNK, rows, width), F32),
            pltpu.VMEM((rows, fields, width), F32),
            pltpu.SemaphoreType.DMA((2, parts)),
        ],
        moved=2 * prior.size * 4,
        limit=40,
    )(core, in_hbm(prior))


def stencil_rows(
    core, coef_ref, v_ref, first, mate, cross, from_left, from_right, seam_ref, put, ready=None
):
    rows, width = v_ref.shape[0], v_ref.shape[2]
    fields = seam_ref.shape[0]
    tile = 8
    lane = lanes_of((tile, width))
    odd, start, stop = (lane & 1) == 1, lane == 0, lane == width - 1
    for at in range(0, fields, tile):
        cut = slice(at, at + tile)
        seam_ref[cut] = jnp.where(
            odd, pltpu.roll(from_left(cut), 1, 1), pltpu.roll(from_right(cut), width - 1, 1)
        )
    for r in range(rows):
        if ready is not None:
            ready(r)
        c = [jnp.broadcast_to(coef_ref[k, r : r + 1, :], (tile, width)) for k in range(6)]
        for at in range(0, fields, tile):
            cut = slice(at, at + tile)
            src = slice(first + at, first + at + tile)
            v = v_ref[r, src, :]
            if r == 0:
                up = jnp.where(core == 0, cross(cut), mate(cut))
            else:
                up = v_ref[r - 1, src, :]
            if r == rows - 1:
                down = jnp.where(core == 0, mate(cut), cross(cut))
            else:
                down = v_ref[r + 1, src, :]
            side = pltpu.roll(seam_ref[cut], width - 1 - 2 * r, 1)
            south = jnp.where(start, side, pltpu.roll(v, 1, 1))
            north = jnp.where(stop, side, pltpu.roll(v, width - 1, 1))
            put(r, cut, c[0] * v - c[1] * down - c[2] * up - c[3] * north - c[4] * south, c[5])


def reader(ref, at=0):
    return lambda cut: ref[at + cut.start : at + cut.stop, :]


def stencil_kernel(
    first, core_ref, coef_ref, in_ref, mate_ref, cross_ref, fl_ref, fr_ref, y_ref, y_hbm, *rest
):
    if first:
        v_ref, mate_out, cross_out, edge_ref, seam_ref, out_sems, in_sems = rest
    else:
        mate_out, cross_out, edge_ref, seam_ref, out_sems = rest
        v_ref = in_ref
    rows = v_ref.shape[0]
    parts = [pl.ds(i * CHUNK, CHUNK) for i in range(rows // CHUNK)]
    loads, stores = [], []
    if first:
        for i, part in enumerate(parts):
            loads.append(pltpu.make_async_copy(in_ref.at[part], v_ref.at[part], in_sems.at[i]))
            loads[-1].start()

    def store(i):
        stores.append(
            pltpu.make_async_copy(y_ref.at[parts[i]], y_hbm.at[parts[i]], out_sems.at[i])
        )
        stores[-1].start()

    def ready(r):
        if first and r == 0:
            loads[0].wait()
        if first and r % CHUNK == CHUNK - 1 and r + 1 < rows:
            loads[r // CHUNK + 1].wait()
        if r % CHUNK == 0 and r > 0:
            store(r // CHUNK - 1)

    def put(r, cut, image, inv_cap):
        y_ref[r, cut, :] = image * inv_cap

    stencil_rows(
        core_ref[0], coef_ref, v_ref, 0, reader(mate_ref), reader(cross_ref), reader(fl_ref),
        reader(fr_ref), seam_ref, put, ready,
    )
    store(len(parts) - 1)
    skip = y_ref.shape[1] - edge_ref.shape[0]
    pack_edges(y_ref, edge_ref, skip)
    ends(core_ref[0], y_ref, mate_out, cross_out, skip)
    for copy in stores:
        copy.wait()


def stencil(core, coef, v, mate, cross, from_left, from_right, first):
    rows, fields, width = v.shape
    send = shape(fields if first else B, width)
    field = held(rows, fields, width)
    sems = pltpu.SemaphoreType.DMA((rows // CHUNK,))
    return call(
        functools.partial(stencil_kernel, first),
        (field, pltpu.HBM((rows, fields, width), F32)) + (field,) * first + (send,) * 3,
        [SM, VM, HBM if first else VM] + [VM] * 4,
        (VM, HBM) + (VM,) * first + (VM,) * 3,
        scratch=[pltpu.VMEM((fields, width), F32), sems] + [sems] * first,
        flops=12 * v.size,
        moved=2 * v.size * 4,
    )(core, coef, in_hbm(v) if first else v, mate, cross, from_left, from_right)


def wide(ref, at):
    return jnp.concatenate([ref[at + i] for i in range(CHUNK)], axis=1)


def wide_row(ref, at):
    return jnp.concatenate([ref[pl.ds(at + i, 1), :] for i in range(CHUNK)], axis=1)


def halves(x):
    high = x.astype(jnp.bfloat16)
    low = (x - high.astype(F32)).astype(jnp.bfloat16)
    return jnp.concatenate([high, low], axis=0)


def nt(a, b):
    return lax.dot_general(a, b, (((1,), (1,)), ((), ())), preferred_element_type=F32)


def fold(acc, row, rows, col, cols):
    a = acc[row : row + rows, col : col + cols] + acc[row : row + rows, col + cols : col + 2 * cols]
    row += rows
    b = acc[row : row + rows, col : col + cols] + acc[row : row + rows, col + cols : col + 2 * cols]
    return a + b


def over_chunks(rows, accs, terms):
    def add(i, carry):
        for acc, term in zip(accs, terms(i * CHUNK)):
            acc[...] += term
        return carry

    for acc in accs:
        acc[...] = jnp.zeros_like(acc)
    lax.fori_loop(0, rows // CHUNK, add, 0)


def gram_y_kernel(
    cap_ref, p_ref, y_ref, pp_ref, pcp_ref, py_ref, yy_ref, pgp_ref, ygp_ref, accp_ref, accy_ref
):
    def terms(at):
        p, y, cap = wide(p_ref, at), wide(y_ref, at), wide_row(cap_ref, at)
        hp, hy, hg = halves(p), halves(y), halves(y * cap)
        right = jnp.concatenate([hy, hg], axis=0)
        yield nt(hp, jnp.concatenate([right, hp, halves(p * cap)], axis=0))
        yield nt(hy, right)

    over_chunks(p_ref.shape[0], (accp_ref, accy_ref), terms)
    py_ref[...] = fold(accp_ref, 0, 128, 0, 128)
    pgp_ref[...] = fold(accp_ref, 0, 128, 256, 128)
    pp_ref[...] = fold(accp_ref, 0, 128, 512, 128)
    pcp_ref[...] = fold(accp_ref, 0, 128, 768, 128)
    yy_ref[...] = fold(accy_ref, 0, 128, 0, 128)
    ygp_ref[...] = fold(accy_ref, 0, 128, 256, 128)


def gram_x_kernel(
    where_ref, cap_ref, p_ref, y_ref, a_ref, ygy_ref, x_ref, kp_ref, kx_ref, acc_ref, accx_ref
):
    def terms(at):
        ay = wide(a_ref, at)
        hp, hy = halves(wide(p_ref, at)), halves(wide(y_ref, at))
        hg = halves(ay * wide_row(cap_ref, at))
        hx = halves(ay[PRIOR - B :])
        yield nt(hy, hg)
        yield nt(jnp.concatenate([hp, hy, hg, hx], axis=0), hx)

    over_chunks(p_ref.shape[0], (acc_ref, accx_ref), terms)
    ygy_ref[...] = fold(acc_ref, 0, 128, 0, 128)
    px = fold(accx_ref, 0, 128, 0, B)
    yx = fold(accx_ref, 256, 128, 0, B)
    gx = fold(accx_ref, 512, 128, 0, B)
    xx = fold(accx_ref, 768, B, 0, B)
    rest = jnp.concatenate([xx, jnp.zeros((128 - B, B), F32)], axis=0)
    x_ref[...] = jnp.concatenate([px, yx, gx, rest], axis=1)

    kp_ref[...] = jnp.zeros_like(kp_ref)
    kx_ref[...] = jnp.zeros_like(kx_ref)
    n = where_ref.shape[1]

    def step(k, carry):
        @pl.when(where_ref[2, k] > 0)
        def _():
            r, c = where_ref[0, k], where_ref[1, k]
            for v, spot, out_ref in (
                (p_ref[r], k, kp_ref),
                (y_ref[r], k + n, kp_ref),
                (a_ref[r][PRIOR - B :], k, kx_ref),
            ):
                moved = pltpu.roll(v, lax.rem(spot - c + 128, 128), 1)
                out_ref[...] = jnp.where(lanes_of(v.shape) == spot, moved, out_ref[...])

        return carry

    lax.fori_loop(0, n, step, 0)


def gram_y(cap, p, y):
    return call(
        gram_y_kernel,
        (shape(128, 128),) * 6,
        [VM] * 3,
        (VM,) * 6,
        scratch=[pltpu.VMEM((256, 1024), F32), pltpu.VMEM((256, 512), F32)],
        flops=6 * 2 * 256 * 256 * p.shape[0] * 128,
        moved=2 * p.size * 4,
    )(cap, p, y)


def gram_x(where, cap, p, y, ay):
    return call(
        gram_x_kernel,
        (shape(128, 128),) * 3 + (shape(B, 128),),
        [SM] + [VM] * 4,
        (VM,) * 4,
        scratch=[pltpu.VMEM((256, 256), F32), pltpu.VMEM((832, 64), F32)],
        flops=4 * 2 * 256 * 256 * p.shape[0] * 128,
        moved=3 * p.size * 4,
    )(where, cap, p, y, ay)


def pack_kernel(
    core_ref, pp_ref, pcp_ref, py_ref, yy_ref, pgp_ref, ygp_ref, ygy_ref, x_ref, kp_ref, kx_ref,
    mate_ref, keep_ref, give_ref, pack_ref,
):
    row = lax.broadcasted_iota(jnp.int32, (128, 128), 0)
    col = lax.broadcasted_iota(jnp.int32, (128, 128), 1)

    def diagonal(m):
        return jnp.sum(jnp.where(row == col, m, 0.0), axis=0, keepdims=True)

    pack_ref[0:128] = jnp.where(row <= col, pp_ref[...], pcp_ref[...])
    pack_ref[128:256] = jnp.where(row <= col, pgp_ref[...], ygy_ref[...])
    pack_ref[256:384] = jnp.where(row <= col, yy_ref[...], ygp_ref[...])
    pack_ref[384:512] = py_ref[...]
    kx, zero = kx_ref[...], jnp.zeros((B, B), F32)
    extra = jnp.concatenate([zero, kx[:, :B], kx[:, B : 2 * B], zero], axis=0)
    pack_ref[512:640] = x_ref[...] + jnp.concatenate([jnp.zeros((128, 96), F32), extra], axis=1)
    pack_ref[640:768] = kp_ref[...]
    diag = [diagonal(m[...]) for m in (pcp_ref, ygy_ref, ygp_ref)]
    pack_ref[768:776] = jnp.concatenate(diag + [jnp.zeros((5, 128), F32)], axis=0)
    pack_ref[776:832] = jnp.zeros((56, 128), F32)
    half = PACK // 2
    core = core_ref[0]
    keep_ref[...] = pack_ref[pl.ds(pl.multiple_of(core * half, 8), half), :]
    give_ref[0:half] = pack_ref[pl.ds(pl.multiple_of((1 - core) * half, 8), half), :]
    give_ref[half : half + B] = mate_ref[...]


def pack(core, mats, mate):
    return call(
        pack_kernel,
        (shape(PACK // 2, 128), shape(PACK // 2 + B, 128)),
        [SM] + [VM] * (1 + len(mats)),
        (VM,) * 2,
        scratch=[pltpu.VMEM((PACK, 128), F32)],
        moved=1 << 20,
    )(core, *mats, mate)


def fan_kernel(place_ref, keep_ref, got_ref, edge_ref, own_ref, s1_ref, s2_ref, s3_ref, sum_ref):
    half, quarter = PACK // 2, PACK // 8
    sum_ref[...] = keep_ref[...] + got_ref[0:half]
    for m, ref in enumerate((own_ref, s1_ref, s2_ref, s3_ref)):
        at = pl.multiple_of((place_ref[0] ^ m) * quarter, 8)
        ref[0:quarter] = sum_ref[pl.ds(at, quarter), :]
    s1_ref[quarter:] = edge_ref[...]
    s3_ref[quarter:] = edge_ref[...]


def fan(place, keep, got, edge):
    quarter = PACK // 8
    return call(
        fan_kernel,
        tuple(shape(quarter + extra, 128) for extra in (0, B, 0, B)),
        [SM] + [VM] * 3,
        (VM,) * 4,
        scratch=[pltpu.VMEM((PACK // 2, 128), F32)],
        moved=1 << 20,
    )(place, keep, got, edge)


def last_kernel(
    place_ref, coef_ref, a_ref, mate_ref, cross_ref, own_ref, g1_ref, g2_ref, g3_ref,
    ax_hbm, sum_ref, ax_ref, image_ref, seam_ref, sem,
):
    me, core = place_ref[0], place_ref[1]
    quarter = PACK // 8

    def put(r, cut, image, inv_cap):
        ax_ref[r, cut, :] = image * inv_cap
        image_ref[r, cut, :] = image

    near, far = reader(g1_ref, quarter), reader(g3_ref, quarter)

    def from_left(cut):
        other = jnp.where(me == 2, far(cut), 0.0)
        return jnp.where(me % 2 == 1, near(cut), other)

    def from_right(cut):
        other = jnp.where(me == 1, far(cut), 0.0)
        return jnp.where(me % 2 == 0, near(cut), other)

    stencil_rows(
        core, coef_ref, a_ref, PRIOR - B, reader(mate_ref, PACK // 2), reader(cross_ref),
        from_left, from_right, seam_ref, put,
    )
    copy = pltpu.make_async_copy(ax_ref, ax_hbm, sem)
    copy.start()
    sum_ref[0:quarter] = (own_ref[...] + g1_ref[0:quarter]) + (g2_ref[...] + g3_ref[0:quarter])
    acc = jnp.zeros((2 * B, 2 * B), F32)
    for at in range(0, a_ref.shape[0], CHUNK):
        hx = halves(wide(a_ref, at)[PRIOR - B :])
        acc = acc + nt(hx, halves(wide(image_ref, at)))
    xgx = fold(acc, 0, B, 0, B)
    sum_ref[quarter:] = jnp.concatenate([xgx[8 * k : 8 * k + 8] for k in range(4)], axis=1)
    copy.wait()


def last(place, coef, ay, mate, cross, quads):
    rows, fields, width = ay.shape
    return call(
        last_kernel,
        (pltpu.HBM((rows, B, width), F32), shape(PACK // 8 + 8, 128)),
        [SM] + [VM] * 8,
        (HBM, VM),
        scratch=[
            pltpu.VMEM((rows, B, width), F32),
            pltpu.VMEM((rows, B, width), F32),
            pltpu.VMEM((B, width), F32),
            pltpu.SemaphoreType.DMA,
        ],
        flops=1 << 27,
        moved=2 * rows * B * width * 4,
    )(place, coef, ay, mate, cross, *quads)


def split(x):
    high = x.astype(jnp.bfloat16)
    return high, (x - high.astype(F32)).astype(jnp.bfloat16)


def times(t, pair):
    rows = t.shape[0] // 2
    big = jnp.dot(t, pair[0], preferred_element_type=F32)
    return big[:rows] + big[rows:] + jnp.dot(t[:rows], pair[1], preferred_element_type=F32)


def combine(t, p_ref, y_ref, a_ref, ax_ref, q_ref, n_ref, qbuf_ref, nbuf_ref, sems):
    two = 2 * B
    high, low = split(t)

    def cut(lo, hi, first):
        return jnp.concatenate([high[first:, lo:hi], low[first:, lo:hi]], axis=0)

    t_py, t_x, t_y, t_rest = cut(0, 256, 0), cut(256, 288, 0), cut(0, 128, B), cut(128, 288, B)
    rows, fields, width = p_ref.shape
    copies = []
    for at in range(0, rows, DEPTH):

        def row_block(ref):
            return jnp.concatenate([ref[at + i] for i in range(DEPTH)], axis=1)

        p, y = split(row_block(p_ref)), split(row_block(y_ref))
        a, ax = split(row_block(a_ref)), split(row_block(ax_ref))
        py = tuple(jnp.concatenate(pair, axis=0) for pair in zip(p, y))
        rest = tuple(jnp.concatenate(pair, axis=0) for pair in zip(a, ax))
        x = tuple(part[PRIOR - B :] for part in a)
        q = times(t_py, py) + times(t_x, x)
        n = times(t_y, y) + times(t_rest, rest)
        step = at // DEPTH
        for k in range(DEPTH):
            lanes = slice(k * width, (k + 1) * width)
            qbuf_ref.at[step].reshape(two * DEPTH, width)[pl.ds(k, two, stride=DEPTH), :] = q[
                :, lanes
            ]
            nbuf_ref.at[step].reshape(B * DEPTH, width)[pl.ds(k, B, stride=DEPTH), :] = n[
                :, lanes
            ]
        for j, (src, dst) in enumerate(((qbuf_ref, q_ref), (nbuf_ref, n_ref))):
            copy = pltpu.make_async_copy(
                src.at[step], dst.at[:, pl.ds(at, DEPTH), :], sems.at[j, step]
            )
            copy.start()
            copies.append(copy)
    return copies


def swap(x, axis, mask):
    return lax.ppermute(x, axis, [(i, i ^ mask) for i in range(lax.axis_size(axis))])


def shift(x, axis, step):
    size = lax.axis_size(axis)
    return lax.ppermute(
        x, axis, [(i, i + step) for i in range(size) if 0 <= i + step < size]
    )


def swap_cross(x):
    size = lax.axis_size("gx")
    pairs = [(i, i + 1) for i in range(1, size - 1, 2)]
    return lax.ppermute(x, "gx", pairs + [(j, i) for i, j in pairs])


def sum_over_chips(x):
    mask = 2
    while mask < lax.axis_size("gx"):
        x = x + swap(x, "gx", mask)
        mask *= 2
    x = jnp.concatenate([x, swap(x, "gx", 1)], axis=0)
    return [x] + [swap(x, "gy", m) for m in (1, 2, 3)]


def exchange(mate, cross, edge, edge_left):
    return swap(mate, "gx", 1), swap_cross(cross), shift(edge, "gy", 1), shift(edge_left, "gy", -1)


def dot(a, b):
    return jnp.dot(a, b, precision=HI, preferred_element_type=F32)


def tdot(a, b):
    return lax.dot_general(
        a, b, (((0,), (0,)), ((), ())), precision=HI, preferred_element_type=F32
    )


def inverse_factor(s):
    n = s.shape[0]
    s = 0.5 * (s + s.T)
    row = lax.broadcasted_iota(jnp.int32, (n, 128), 0)
    lane = lax.broadcasted_iota(jnp.int32, (n, 128), 1)
    eye = jnp.where(row + n == lane, 1.0, 0.0)
    a = jnp.concatenate([s, jnp.zeros((n, 128 - n), F32)], axis=1) + eye
    for j in range(n):
        pivot = a[j : j + 1, :]
        inv = 1.0 / jnp.sqrt(pivot[:, j : j + 1])
        pivot = pivot * inv
        factor = a[:, j : j + 1] * inv
        a = jnp.where(row > j, a - factor * pivot, jnp.where(row == j, pivot, a))
    return a[:, n : 2 * n]


def final_kernel(
    scale, place_ref, b0_ref, b1_ref, b2_ref, b3_ref, p_hbm, y_hbm, a_hbm, ax_hbm,
    q_ref, n_ref, g_out, c_out, b_out, p_ref, y_ref, a_ref, ax_ref, all_ref, xgx_ref, qbuf_ref,
    nbuf_ref, g_ref, c_ref, b_ref, load_sems, sems, small_sems,
):
    pairs = ((p_hbm, p_ref), (y_hbm, y_ref), (a_hbm, a_ref), (ax_hbm, ax_ref))
    loads = [
        pltpu.make_async_copy(src, dst, load_sems.at[j]) for j, (src, dst) in enumerate(pairs)
    ]
    for load in loads:
        load.start()
    me, core = place_ref[0], place_ref[1]
    quarter = PACK // 8
    for m, ref in enumerate((b0_ref, b1_ref, b2_ref, b3_ref)):
        for h in (0, 1):
            at = (core ^ h) * 4 + (me ^ m)
            lo = h * (quarter + 8)
            all_ref[pl.ds(pl.multiple_of(at * quarter, 8), quarter), :] = ref[lo : lo + quarter]
            xgx_ref[at] = ref[lo + quarter : lo + quarter + 8]
    row = lax.broadcasted_iota(jnp.int32, (128, 128), 0)
    col = lax.broadcasted_iota(jnp.int32, (128, 128), 1)

    def pair(at, d):
        m = all_ref[at : at + 128] * scale
        t = m.T
        diag = all_ref[768 + d : 769 + d] * scale
        return (
            jnp.where(row <= col, m, t),
            jnp.where(row > col, m, jnp.where(row < col, t, diag)),
        )

    pp, pcp = pair(0, 0)
    pgp, ygy = pair(128, 1)
    yy, ycy = pair(256, 2)
    py = all_ref[384:512] * scale
    xs = all_ref[512:640] * scale
    px, yx, ygx = xs[:, :32], xs[:, 32:64], xs[:, 64:96]
    xx = xs[:32, 96:]
    total = xgx_ref[0]
    for k in range(1, 8):
        total = total + xgx_ref[k]
    total = total * scale
    xgx = jnp.concatenate([total[:, B * k : B * (k + 1)] for k in range(4)], axis=0)
    z = PRIOR - B

    h = py[:, z:]
    c = 2.0 * h - dot(pp, h)
    s = yy[z:, z:] + tdot(c, dot(pp, c) - 2.0 * h)
    inv_t = inverse_factor(s).T
    a, b = -dot(c, inv_t), inv_t

    hp = dot(py, a) + dot(px, b)
    wy = dot(yy, a) + dot(yx, b)
    wx = tdot(yx, a) + dot(xx, b)
    hq = tdot(a, hp) + tdot(b, wy[z:])
    kq = dot(pp, a) + dot(h, b)
    kqq = tdot(a, kq) + tdot(b, tdot(h, a) + dot(yy[z:, z:], b))
    cp = 2.0 * hp - dot(pp, hp) - dot(kq, hq)
    cq = 2.0 * hq - tdot(kq, hp) - dot(kqq, hq)
    s = (
        tdot(a, wy)
        + tdot(b, wx)
        + tdot(cp, dot(pp, cp) + dot(kq, cq) - 2.0 * hp)
        + tdot(cq, tdot(kq, cp) + dot(kqq, cq) - 2.0 * hq)
    )
    inv_t = inverse_factor(s).T
    zero_z = jnp.zeros((z, B), F32)
    u = -dot(cp + dot(a, cq), inv_t)
    v = dot(a - jnp.concatenate([zero_z, dot(b, cq)], axis=0), inv_t)
    x = dot(b, inv_t)

    zero = jnp.zeros((B, B), F32)
    tp = jnp.concatenate([a, u, jnp.zeros((128, B), F32)], axis=1)
    ty = jnp.concatenate([jnp.concatenate([zero_z, b], axis=0), v, a], axis=1)
    tx = jnp.concatenate([zero, x, b], axis=1)
    t = jnp.concatenate([m[:, :64].T for m in (tp, ty, tx)], axis=1)
    for load in loads:
        load.wait()
    copies = combine(t, p_ref, y_ref, a_ref, ax_ref, q_ref, n_ref, qbuf_ref, nbuf_ref, sems)

    pcx, ycx, xcx = ycy[:, z:], ygy[:, z:], ygx[z:]
    cpt = dot(pcp, tp) + dot(pgp, ty) + dot(pcx, tx)
    cyt = dot(pgp, tp) + dot(ycy, ty) + dot(ycx, tx)
    cxt = tdot(pcx, tp) + tdot(ycx, ty) + dot(xcx, tx)
    qp, qy, qx = tp[:, :64], ty[:, :64], tx[:, :64]
    r = tdot(qp, cpt) + tdot(qy, cyt) + tdot(qx, cxt)
    side = cpt[:, :64]
    c_ref[0:128, 0:128] = pcp
    c_ref[0:128, 128:192] = side
    c_ref[128:192, 0:128] = side.T
    c_ref[128:192, 128:192] = r[:, :64]
    gpt = cyt[:, 32:64]
    gyt = dot(ycy, u) + dot(ygy, v) + dot(ygx, x)
    gxt = tdot(ycx, u) + tdot(ygx, v) + dot(xgx, x)
    g_ref[0:128] = jnp.concatenate([cpt[:, 64:96], gpt], axis=1)
    g2 = tdot(qp, gpt) + tdot(qy, gyt) + tdot(qx, gxt)
    g_ref[128:192] = jnp.concatenate([r[:, 64:96], g2], axis=1)
    kp = all_ref[640:768]
    extra = all_ref[512:640][:, 96:]
    kx = jnp.concatenate([extra[32:64], extra[64:96]], axis=1)
    b_ref[0:128] = kp[:, :64]
    b_ref[128:192] = tdot(qp, kp[:, :64]) + tdot(qy, kp[:, 64:]) + tdot(qx, kx)


    for j, (src, dst) in enumerate(((g_ref, g_out), (c_ref, c_out), (b_ref, b_out))):
        copy = pltpu.make_async_copy(src, dst, small_sems.at[j])
        copy.start()
        copies.append(copy)
    for copy in copies:
        copy.wait()


def final(place, pieces, p, y, ay, ax, scale):
    rows, fields, width = p.shape
    steps = rows // DEPTH
    small = ((192, 64), (192, 192), (192, 64))
    return call(
        functools.partial(final_kernel, scale),
        tuple(
            pltpu.HBM(d, F32) for d in ((2 * B, rows, width), (B, rows, width)) + small
        ),
        [SM] + [VM] * 4 + [HBM] * 4,
        (HBM,) * 5,
        scratch=[pltpu.VMEM(p.shape, F32)] * 3
        + [
            pltpu.VMEM(ax.shape, F32),
            pltpu.VMEM((PACK, 128), F32),
            pltpu.VMEM((8, 8, 128), F32),
            pltpu.VMEM((steps, 2 * B, DEPTH, width), F32),
            pltpu.VMEM((steps, B, DEPTH, width), F32),
        ]
        + [pltpu.VMEM(d, F32) for d in small]
        + [pltpu.SemaphoreType.DMA(d) for d in ((4,), (2, steps), (3,))],
        flops=1 << 30,
        moved=5 * p.size * 4,
        limit=40,
    )(place, *pieces, *(in_hbm(a) for a in (p, y, ay, ax)))


def on_device(prior, cond_x, cond_y, cap_level, decap, via, ports):
    rows_here, cols_here = prior.shape[1:]
    total_cols = cols_here * lax.axis_size("gy")
    scale = 1.0 / (rows_here * lax.axis_size("gx") * total_cols)
    gxe = 0.125 * cond_x.astype(F32)
    gye = 0.125 * cond_y.astype(F32)
    gvia = 0.5 * via.astype(F32)
    cap = 0.25 * cap_level.astype(F32) * (1.0 + 2.0 * decap.astype(F32))

    core = (lax.axis_index("gx") % 2)[None]
    me = lax.axis_index("gy")
    p, mate, cross, edge = regroup(core, prior)
    slot = 2 * jnp.arange(rows_here)[:, None] == jnp.arange(cols_here)[None, :]
    gye_edge = jnp.sum(jnp.where(slot, gye[:, -1:], 0.0), axis=0, keepdims=True)
    spare = jnp.zeros((7, cols_here), F32)
    pair_row = jnp.where(core == 0, gxe[-1], 0.0)[None]
    cross_row = jnp.where(core == 0, 0.0, gxe[-1])[None]
    mate = jnp.concatenate([mate, pair_row, spare], axis=0)
    cross = jnp.concatenate([cross, cross_row, spare], axis=0)
    edge_more = jnp.concatenate([edge, gye_edge, spare], axis=0)
    mate, cross, fl, fr = exchange(mate, cross, edge_more, edge)
    gxw_first = mate[PRIOR : PRIOR + 1] + cross[PRIOR : PRIOR + 1]
    gxw = jnp.concatenate([gxw_first, gxe[:-1]], axis=0)
    gys_first = jnp.sum(jnp.where(slot, fl[PRIOR : PRIOR + 1], 0.0), axis=1, keepdims=True)
    gys = jnp.concatenate([gys_first, gye[:, :-1]], axis=1)
    center = gvia + gxe + gxw + gye + gys
    coef = jnp.stack([center, gxe, gxw, gye, gys, 1.0 / cap])

    port_rows = ports // total_cols - lax.axis_index("gx") * rows_here
    port_cols = ports % total_cols - lax.axis_index("gy") * cols_here
    inside = (
        (port_rows >= 0) & (port_rows < rows_here) & (port_cols >= 0) & (port_cols < cols_here)
    )
    where = jnp.stack(
        [
            jnp.clip(port_rows, 0, rows_here - 1),
            jnp.clip(port_cols, 0, cols_here - 1),
            inside.astype(jnp.int32),
        ]
    )
    y, y_far, p_in, *sends = stencil(core, coef, p, mate, cross, fl, fr, True)
    sides = exchange(*sends, sends[2])
    grams_y = gram_y(cap, p_in, y)
    ay, ay_far, mate, cross, edge = stencil(core, coef, y, *sides, False)
    ygy, xs, kp, kx = gram_x(where, cap, p_in, y, ay)
    cross = swap_cross(cross)
    place = jnp.concatenate([me[None], core])
    keep, give = pack(core, [*grams_y, ygy, xs, kp, kx], mate)
    got = swap(give, "gx", 1)
    own, *sends = fan(place, keep, got, edge)
    quads = [own] + [swap(x, "gy", m) for m, x in zip((1, 2, 3), sends)]
    ax, x = last(place, coef, ay, got, cross, quads)
    return tuple(final(place, sum_over_chips(x), p, y_far, ay_far, ax, scale))


def solution(mesh):
    in_specs = (
        P(None, "gx", "gy"),
        P("gx", "gy"),
        P("gx", "gy"),
        P("gx", "gy"),
        P("gx", "gy"),
        P("gx", "gy"),
        P(),
    )
    out_specs = (P(None, "gx", "gy"), P(None, "gx", "gy"), P(), P(), P())
    return jax.shard_map(
        on_device, mesh=mesh, in_specs=in_specs, out_specs=out_specs, check_vma=False
    )
```

```python
import functools

import jax
import jax.numpy as jnp
from jax import lax
from jax.experimental import pallas as pl
from jax.experimental.pallas import tpu as pltpu
from jax.sharding import PartitionSpec as P

B = 32
PRIOR = 128
F32 = jnp.float32
HI = lax.Precision.HIGHEST
MIB = 1024 * 1024
TILE = 32
CHUNK = 16
DEPTH = 8
PACK = 832
VM = pl.BlockSpec(memory_space=pltpu.VMEM)
SM = pl.BlockSpec(memory_space=pltpu.SMEM)
HBM = pl.BlockSpec(memory_space=pltpu.HBM)
ANY = pl.BlockSpec(memory_space=pl.ANY)


def call(kernel, out, in_specs, out_specs, scratch=(), flops=0, moved=0, limit=24, aliases={}):
    return pl.pallas_call(
        kernel,
        out_shape=out,
        in_specs=in_specs,
        out_specs=out_specs,
        scratch_shapes=scratch,
        input_output_aliases=aliases,
        compiler_params=pltpu.CompilerParams(vmem_limit_bytes=limit * MIB),
        cost_estimate=pl.CostEstimate(flops=flops, bytes_accessed=moved, transcendentals=0),
    )


def shape(*dims):
    return jax.ShapeDtypeStruct(dims, F32)


def held(*dims):
    return pltpu.VMEM(dims, F32)


def in_hbm(x):
    return pltpu.with_memory_space_constraint(x, pltpu.HBM)


def lanes_of(dims):
    return lax.broadcasted_iota(jnp.int32, dims, len(dims) - 1)


def pack_edges(v_ref, edge_ref, skip=0):
    rows, fields, width = v_ref.shape
    slot = lanes_of((TILE, width)) >> 1
    for at in range(skip, fields, TILE):
        edge = jnp.zeros((TILE, width), F32)
        for r in range(rows):
            edge = jnp.where(
                slot == r, pltpu.roll(v_ref[r, at : at + TILE, :], 2 * r + 1, 1), edge
            )
        edge_ref[at - skip : at - skip + TILE] = edge


def ends(core, v_ref, mate_ref, cross_ref, first=0):
    top = v_ref[0, first:, :]
    low = v_ref[v_ref.shape[0] - 1, first:, :]
    mate_ref[...] = jnp.where(core == 0, low, top)
    cross_ref[...] = jnp.where(core == 0, top, low)


def regroup_kernel(
    core_ref, p_ref, out_hbm, mate_ref, cross_ref, edge_ref, buf_ref, out_ref, sems
):
    parts, fields, rows, width = buf_ref.shape
    copies = [
        pltpu.make_async_copy(p_ref.at[pl.ds(i * fields, fields)], buf_ref.at[i], sems.at[0, i])
        for i in range(parts)
    ]
    back = []
    for copy in copies:
        copy.start()
    for i in range(parts):
        copies[i].wait()
        cut = slice(i * fields, (i + 1) * fields)
        for at in range(0, rows, DEPTH):
            flat = buf_ref.at[i].reshape(fields * rows, width)
            got = [flat[pl.ds(at + k, fields, stride=rows), :] for k in range(DEPTH)]
            for k in range(DEPTH):
                out_ref[at + k, cut, :] = got[k]
        held_part = (slice(None), pl.ds(i * fields, fields), slice(None))
        back.append(
            pltpu.make_async_copy(out_ref.at[held_part], out_hbm.at[held_part], sems.at[1, i])
        )
        back[-1].start()
    pack_edges(out_ref, edge_ref)
    ends(core_ref[0], out_ref, mate_ref, cross_ref)
    for copy in back:
        copy.wait()


def regroup(core, prior):
    fields, rows, width = prior.shape
    parts = fields // CHUNK
    return call(
        regroup_kernel,
        (pltpu.HBM((rows, fields, width), F32),) + (shape(fields, width),) * 3,
        [SM, HBM],
        (HBM,) + (VM,) * 3,
        scratch=[
            pltpu.VMEM((parts, CHUNK, rows, width), F32),
            pltpu.VMEM((rows, fields, width), F32),
            pltpu.SemaphoreType.DMA((2, parts)),
        ],
        moved=2 * prior.size * 4,
        limit=40,
    )(core, in_hbm(prior))


def stencil_rows(
    core, coef_ref, v_ref, first, mate, cross, from_left, from_right, seam_ref, put, ready=None
):
    rows, width = v_ref.shape[0], v_ref.shape[2]
    fields = seam_ref.shape[0]
    tile = 8
    lane = lanes_of((tile, width))
    odd, start, stop = (lane & 1) == 1, lane == 0, lane == width - 1
    for at in range(0, fields, tile):
        cut = slice(at, at + tile)
        seam_ref[cut] = jnp.where(
            odd, pltpu.roll(from_left(cut), 1, 1), pltpu.roll(from_right(cut), width - 1, 1)
        )
    for r in range(rows):
        if ready is not None:
            ready(r)
        c = [jnp.broadcast_to(coef_ref[k, r : r + 1, :], (tile, width)) for k in range(6)]
        for at in range(0, fields, tile):
            cut = slice(at, at + tile)
            src = slice(first + at, first + at + tile)
            v = v_ref[r, src, :]
            if r == 0:
                up = jnp.where(core == 0, cross(cut), mate(cut))
            else:
                up = v_ref[r - 1, src, :]
            if r == rows - 1:
                down = jnp.where(core == 0, mate(cut), cross(cut))
            else:
                down = v_ref[r + 1, src, :]
            side = pltpu.roll(seam_ref[cut], width - 1 - 2 * r, 1)
            south = jnp.where(start, side, pltpu.roll(v, 1, 1))
            north = jnp.where(stop, side, pltpu.roll(v, width - 1, 1))
            put(r, cut, c[0] * v - c[1] * down - c[2] * up - c[3] * north - c[4] * south, c[5])


def reader(ref, at=0):
    return lambda cut: ref[at + cut.start : at + cut.stop, :]


def stencil_kernel(
    first, core_ref, coef_ref, in_ref, mate_ref, cross_ref, fl_ref, fr_ref, y_ref, y_hbm, *rest
):
    if first:
        v_ref, mate_out, cross_out, edge_ref, seam_ref, out_sems, in_sems = rest
    else:
        mate_out, cross_out, edge_ref, seam_ref, out_sems = rest
        v_ref = in_ref
    rows = v_ref.shape[0]
    parts = [pl.ds(i * CHUNK, CHUNK) for i in range(rows // CHUNK)]
    loads, stores = [], []
    if first:
        for i, part in enumerate(parts):
            loads.append(pltpu.make_async_copy(in_ref.at[part], v_ref.at[part], in_sems.at[i]))
            loads[-1].start()

    def store(i):
        stores.append(
            pltpu.make_async_copy(y_ref.at[parts[i]], y_hbm.at[parts[i]], out_sems.at[i])
        )
        stores[-1].start()

    def ready(r):
        if first and r == 0:
            loads[0].wait()
        if first and r % CHUNK == CHUNK - 1 and r + 1 < rows:
            loads[r // CHUNK + 1].wait()
        if r % CHUNK == 0 and r > 0:
            store(r // CHUNK - 1)

    def put(r, cut, image, inv_cap):
        y_ref[r, cut, :] = image * inv_cap

    stencil_rows(
        core_ref[0], coef_ref, v_ref, 0, reader(mate_ref), reader(cross_ref), reader(fl_ref),
        reader(fr_ref), seam_ref, put, ready,
    )
    store(len(parts) - 1)
    skip = y_ref.shape[1] - edge_ref.shape[0]
    pack_edges(y_ref, edge_ref, skip)
    ends(core_ref[0], y_ref, mate_out, cross_out, skip)
    for copy in stores:
        copy.wait()


def stencil(core, coef, v, mate, cross, from_left, from_right, first):
    rows, fields, width = v.shape
    send = shape(fields if first else B, width)
    field = held(rows, fields, width)
    sems = pltpu.SemaphoreType.DMA((rows // CHUNK,))
    return call(
        functools.partial(stencil_kernel, first),
        (field, pltpu.HBM((rows, fields, width), F32)) + (field,) * first + (send,) * 3,
        [SM, VM, HBM if first else VM] + [VM] * 4,
        (VM, HBM) + (VM,) * first + (VM,) * 3,
        scratch=[pltpu.VMEM((fields, width), F32), sems] + [sems] * first,
        flops=12 * v.size,
        moved=2 * v.size * 4,
    )(core, coef, in_hbm(v) if first else v, mate, cross, from_left, from_right)


def wide(ref, at):
    return jnp.concatenate([ref[at + i] for i in range(CHUNK)], axis=1)


def wide_row(ref, at):
    return jnp.concatenate([ref[pl.ds(at + i, 1), :] for i in range(CHUNK)], axis=1)


def halves(x):
    high = x.astype(jnp.bfloat16)
    low = (x - high.astype(F32)).astype(jnp.bfloat16)
    return jnp.concatenate([high, low], axis=0)


def nt(a, b):
    return lax.dot_general(a, b, (((1,), (1,)), ((), ())), preferred_element_type=F32)


def fold(acc, row, rows, col, cols):
    a = acc[row : row + rows, col : col + cols] + acc[row : row + rows, col + cols : col + 2 * cols]
    row += rows
    b = acc[row : row + rows, col : col + cols] + acc[row : row + rows, col + cols : col + 2 * cols]
    return a + b


def over_chunks(rows, accs, terms):
    def add(i, carry):
        for acc, term in zip(accs, terms(i * CHUNK)):
            acc[...] += term
        return carry

    for acc in accs:
        acc[...] = jnp.zeros_like(acc)
    lax.fori_loop(0, rows // CHUNK, add, 0)


def gram_y_kernel(
    cap_ref, p_ref, y_ref, pp_ref, pcp_ref, py_ref, yy_ref, pgp_ref, ygp_ref, accp_ref, accy_ref
):
    def terms(at):
        p, y, cap = wide(p_ref, at), wide(y_ref, at), wide_row(cap_ref, at)
        hp, hy, hg = halves(p), halves(y), halves(y * cap)
        right = jnp.concatenate([hy, hg], axis=0)
        yield nt(hp, jnp.concatenate([right, hp, halves(p * cap)], axis=0))
        yield nt(hy, right)

    over_chunks(p_ref.shape[0], (accp_ref, accy_ref), terms)
    py_ref[...] = fold(accp_ref, 0, 128, 0, 128)
    pgp_ref[...] = fold(accp_ref, 0, 128, 256, 128)
    pp_ref[...] = fold(accp_ref, 0, 128, 512, 128)
    pcp_ref[...] = fold(accp_ref, 0, 128, 768, 128)
    yy_ref[...] = fold(accy_ref, 0, 128, 0, 128)
    ygp_ref[...] = fold(accy_ref, 0, 128, 256, 128)


def gram_x_kernel(
    where_ref, cap_ref, p_ref, y_ref, a_ref, ygy_ref, x_ref, kp_ref, kx_ref, acc_ref, accx_ref
):
    def terms(at):
        ay = wide(a_ref, at)
        hp, hy = halves(wide(p_ref, at)), halves(wide(y_ref, at))
        hg = halves(ay * wide_row(cap_ref, at))
        hx = halves(ay[PRIOR - B :])
        yield nt(hy, hg)
        yield nt(jnp.concatenate([hp, hy, hg, hx], axis=0), hx)

    over_chunks(p_ref.shape[0], (acc_ref, accx_ref), terms)
    ygy_ref[...] = fold(acc_ref, 0, 128, 0, 128)
    px = fold(accx_ref, 0, 128, 0, B)
    yx = fold(accx_ref, 256, 128, 0, B)
    gx = fold(accx_ref, 512, 128, 0, B)
    xx = fold(accx_ref, 768, B, 0, B)
    rest = jnp.concatenate([xx, jnp.zeros((128 - B, B), F32)], axis=0)
    x_ref[...] = jnp.concatenate([px, yx, gx, rest], axis=1)

    kp_ref[...] = jnp.zeros_like(kp_ref)
    kx_ref[...] = jnp.zeros_like(kx_ref)
    n = where_ref.shape[1]

    def step(k, carry):
        @pl.when(where_ref[2, k] > 0)
        def _():
            r, c = where_ref[0, k], where_ref[1, k]
            for v, spot, out_ref in (
                (p_ref[r], k, kp_ref),
                (y_ref[r], k + n, kp_ref),
                (a_ref[r][PRIOR - B :], k, kx_ref),
            ):
                moved = pltpu.roll(v, lax.rem(spot - c + 128, 128), 1)
                out_ref[...] = jnp.where(lanes_of(v.shape) == spot, moved, out_ref[...])

        return carry

    lax.fori_loop(0, n, step, 0)


def gram_y(cap, p, y):
    return call(
        gram_y_kernel,
        (shape(128, 128),) * 6,
        [VM] * 3,
        (VM,) * 6,
        scratch=[pltpu.VMEM((256, 1024), F32), pltpu.VMEM((256, 512), F32)],
        flops=6 * 2 * 256 * 256 * p.shape[0] * 128,
        moved=2 * p.size * 4,
    )(cap, p, y)


def gram_x(where, cap, p, y, ay):
    return call(
        gram_x_kernel,
        (shape(128, 128),) * 3 + (shape(B, 128),),
        [SM] + [VM] * 4,
        (VM,) * 4,
        scratch=[pltpu.VMEM((256, 256), F32), pltpu.VMEM((832, 64), F32)],
        flops=4 * 2 * 256 * 256 * p.shape[0] * 128,
        moved=3 * p.size * 4,
    )(where, cap, p, y, ay)


def pack_kernel(
    core_ref, pp_ref, pcp_ref, py_ref, yy_ref, pgp_ref, ygp_ref, ygy_ref, x_ref, kp_ref, kx_ref,
    mate_ref, keep_ref, give_ref, pack_ref,
):
    row = lax.broadcasted_iota(jnp.int32, (128, 128), 0)
    col = lax.broadcasted_iota(jnp.int32, (128, 128), 1)

    def diagonal(m):
        return jnp.sum(jnp.where(row == col, m, 0.0), axis=0, keepdims=True)

    pack_ref[0:128] = jnp.where(row <= col, pp_ref[...], pcp_ref[...])
    pack_ref[128:256] = jnp.where(row <= col, pgp_ref[...], ygy_ref[...])
    pack_ref[256:384] = jnp.where(row <= col, yy_ref[...], ygp_ref[...])
    pack_ref[384:512] = py_ref[...]
    kx, zero = kx_ref[...], jnp.zeros((B, B), F32)
    extra = jnp.concatenate([zero, kx[:, :B], kx[:, B : 2 * B], zero], axis=0)
    pack_ref[512:640] = x_ref[...] + jnp.concatenate([jnp.zeros((128, 96), F32), extra], axis=1)
    pack_ref[640:768] = kp_ref[...]
    diag = [diagonal(m[...]) for m in (pcp_ref, ygy_ref, ygp_ref)]
    pack_ref[768:776] = jnp.concatenate(diag + [jnp.zeros((5, 128), F32)], axis=0)
    pack_ref[776:832] = jnp.zeros((56, 128), F32)
    half = PACK // 2
    core = core_ref[0]
    keep_ref[...] = pack_ref[pl.ds(pl.multiple_of(core * half, 8), half), :]
    give_ref[0:half] = pack_ref[pl.ds(pl.multiple_of((1 - core) * half, 8), half), :]
    give_ref[half : half + B] = mate_ref[...]


def pack(core, mats, mate):
    return call(
        pack_kernel,
        (shape(PACK // 2, 128), shape(PACK // 2 + B, 128)),
        [SM] + [VM] * (1 + len(mats)),
        (VM,) * 2,
        scratch=[pltpu.VMEM((PACK, 128), F32)],
        moved=1 << 20,
    )(core, *mats, mate)


def fan_kernel(place_ref, keep_ref, got_ref, edge_ref, own_ref, s1_ref, s2_ref, s3_ref, sum_ref):
    half, quarter = PACK // 2, PACK // 8
    sum_ref[...] = keep_ref[...] + got_ref[0:half]
    for m, ref in enumerate((own_ref, s1_ref, s2_ref, s3_ref)):
        at = pl.multiple_of((place_ref[0] ^ m) * quarter, 8)
        ref[0:quarter] = sum_ref[pl.ds(at, quarter), :]
    s1_ref[quarter:] = edge_ref[...]
    s3_ref[quarter:] = edge_ref[...]


def fan(place, keep, got, edge):
    quarter = PACK // 8
    return call(
        fan_kernel,
        tuple(shape(quarter + extra, 128) for extra in (0, B, 0, B)),
        [SM] + [VM] * 3,
        (VM,) * 4,
        scratch=[pltpu.VMEM((PACK // 2, 128), F32)],
        moved=1 << 20,
    )(place, keep, got, edge)


def last_kernel(
    place_ref, coef_ref, a_ref, mate_ref, cross_ref, own_ref, g1_ref, g2_ref, g3_ref,
    ax_hbm, sum_ref, ax_ref, image_ref, seam_ref, sem,
):
    me, core = place_ref[0], place_ref[1]
    quarter = PACK // 8

    def put(r, cut, image, inv_cap):
        ax_ref[r, cut, :] = image * inv_cap
        image_ref[r, cut, :] = image

    near, far = reader(g1_ref, quarter), reader(g3_ref, quarter)

    def from_left(cut):
        other = jnp.where(me == 2, far(cut), 0.0)
        return jnp.where(me % 2 == 1, near(cut), other)

    def from_right(cut):
        other = jnp.where(me == 1, far(cut), 0.0)
        return jnp.where(me % 2 == 0, near(cut), other)

    stencil_rows(
        core, coef_ref, a_ref, PRIOR - B, reader(mate_ref, PACK // 2), reader(cross_ref),
        from_left, from_right, seam_ref, put,
    )
    copy = pltpu.make_async_copy(ax_ref, ax_hbm, sem)
    copy.start()
    sum_ref[0:quarter] = (own_ref[...] + g1_ref[0:quarter]) + (g2_ref[...] + g3_ref[0:quarter])
    acc = jnp.zeros((2 * B, 2 * B), F32)
    for at in range(0, a_ref.shape[0], CHUNK):
        hx = halves(wide(a_ref, at)[PRIOR - B :])
        acc = acc + nt(hx, halves(wide(image_ref, at)))
    xgx = fold(acc, 0, B, 0, B)
    sum_ref[quarter:] = jnp.concatenate([xgx[8 * k : 8 * k + 8] for k in range(4)], axis=1)
    copy.wait()


def last(place, coef, ay, mate, cross, quads):
    rows, fields, width = ay.shape
    return call(
        last_kernel,
        (pltpu.HBM((rows, B, width), F32), shape(PACK // 8 + 8, 128)),
        [SM] + [VM] * 8,
        (HBM, VM),
        scratch=[
            pltpu.VMEM((rows, B, width), F32),
            pltpu.VMEM((rows, B, width), F32),
            pltpu.VMEM((B, width), F32),
            pltpu.SemaphoreType.DMA,
        ],
        flops=1 << 27,
        moved=2 * rows * B * width * 4,
    )(place, coef, ay, mate, cross, *quads)


def split(x):
    high = x.astype(jnp.bfloat16)
    return high, (x - high.astype(F32)).astype(jnp.bfloat16)


def times(t, pair):
    rows = t.shape[0] // 2
    big = jnp.dot(t, pair[0], preferred_element_type=F32)
    return big[:rows] + big[rows:] + jnp.dot(t[:rows], pair[1], preferred_element_type=F32)


def combine(t, p_ref, y_ref, a_ref, ax_ref, q_ref, n_ref, qbuf_ref, nbuf_ref, sems, ready):
    two = 2 * B
    high, low = split(t)

    def cut(lo, hi, first):
        return jnp.concatenate([high[first:, lo:hi], low[first:, lo:hi]], axis=0)

    t_py, t_x, t_y, t_rest = cut(0, 256, 0), cut(256, 288, 0), cut(0, 128, B), cut(128, 288, B)
    rows, fields, width = p_ref.shape
    copies = []
    for at in range(0, rows, DEPTH):
        ready(at)

        def row_block(ref):
            return jnp.concatenate([ref[at + i] for i in range(DEPTH)], axis=1)

        p, y = split(row_block(p_ref)), split(row_block(y_ref))
        a, ax = split(row_block(a_ref)), split(row_block(ax_ref))
        py = tuple(jnp.concatenate(pair, axis=0) for pair in zip(p, y))
        rest = tuple(jnp.concatenate(pair, axis=0) for pair in zip(a, ax))
        x = tuple(part[PRIOR - B :] for part in a)
        q = times(t_py, py) + times(t_x, x)
        n = times(t_y, y) + times(t_rest, rest)
        step = at // DEPTH
        for k in range(DEPTH):
            lanes = slice(k * width, (k + 1) * width)
            qbuf_ref.at[step].reshape(two * DEPTH, width)[pl.ds(k, two, stride=DEPTH), :] = q[
                :, lanes
            ]
            nbuf_ref.at[step].reshape(B * DEPTH, width)[pl.ds(k, B, stride=DEPTH), :] = n[
                :, lanes
            ]
        for j, (src, dst) in enumerate(((qbuf_ref, q_ref), (nbuf_ref, n_ref))):
            copy = pltpu.make_async_copy(
                src.at[step], dst.at[:, pl.ds(at, DEPTH), :], sems.at[j, step]
            )
            copy.start()
            copies.append(copy)
    return copies


def swap(x, axis, mask):
    return lax.ppermute(x, axis, [(i, i ^ mask) for i in range(lax.axis_size(axis))])


def shift(x, axis, step):
    size = lax.axis_size(axis)
    return lax.ppermute(
        x, axis, [(i, i + step) for i in range(size) if 0 <= i + step < size]
    )


def swap_cross(x):
    size = lax.axis_size("gx")
    pairs = [(i, i + 1) for i in range(1, size - 1, 2)]
    return lax.ppermute(x, "gx", pairs + [(j, i) for i, j in pairs])


def sum_over_chips(x):
    mask = 2
    while mask < lax.axis_size("gx"):
        x = x + swap(x, "gx", mask)
        mask *= 2
    x = jnp.concatenate([x, swap(x, "gx", 1)], axis=0)
    return [x] + [swap(x, "gy", m) for m in (1, 2, 3)]


def exchange(mate, cross, edge, edge_left):
    return swap(mate, "gx", 1), swap_cross(cross), shift(edge, "gy", 1), shift(edge_left, "gy", -1)


def dot(a, b):
    return jnp.dot(a, b, precision=HI, preferred_element_type=F32)


def tdot(a, b):
    return lax.dot_general(
        a, b, (((0,), (0,)), ((), ())), precision=HI, preferred_element_type=F32
    )


def inverse_factor(s):
    n = s.shape[0]
    s = 0.5 * (s + s.T)
    row = lax.broadcasted_iota(jnp.int32, (n, 128), 0)
    lane = lax.broadcasted_iota(jnp.int32, (n, 128), 1)
    eye = jnp.where(row + n == lane, 1.0, 0.0)
    a = jnp.concatenate([s, jnp.zeros((n, 128 - n), F32)], axis=1) + eye
    for j in range(0, n, 2):
        one = jnp.broadcast_to(a[:, j : j + 1], (n, 128))
        two = jnp.broadcast_to(a[:, j + 1 : j + 2], (n, 128))
        inv = 1.0 / one[j : j + 1]
        step = one[j + 1 : j + 2] * inv
        head = a[j : j + 1]
        tail = a[j + 1 : j + 2] - step * head
        left = one * inv
        two = two - left * two[j : j + 1]
        right = two * (1.0 / two[j + 1 : j + 2])
        below = a - left * head - right * tail
        a = jnp.where(row > j + 1, below, jnp.where(row == j + 1, tail, a))
    diag = jnp.sum(jnp.where(row == lane, a, 0.0), axis=1, keepdims=True)
    return (a / jnp.sqrt(diag))[:, n : 2 * n]


def final_kernel(
    scale, place_ref, b0_ref, b1_ref, b2_ref, b3_ref, p_hbm, y_hbm, a_hbm, ax_hbm,
    q_ref, n_ref, g_out, c_out, b_out, p_ref, y_ref, a_ref, ax_ref, all_ref, xgx_ref, qbuf_ref,
    nbuf_ref, g_ref, c_ref, b_ref, load_sems, sems, small_sems,
):
    pairs = ((p_hbm, p_ref), (y_hbm, y_ref), (a_hbm, a_ref), (ax_hbm, ax_ref))
    loads = []
    for i in range(p_ref.shape[0] // CHUNK):
        part = pl.ds(i * CHUNK, CHUNK)
        for j, (src, dst) in enumerate(pairs):
            loads.append(
                pltpu.make_async_copy(src.at[part], dst.at[part], load_sems.at[j, i])
            )
            loads[-1].start()

    def ready(at):
        if at % CHUNK == 0:
            for load in loads[at // CHUNK * 4 : at // CHUNK * 4 + 4]:
                load.wait()

    me, core = place_ref[0], place_ref[1]
    quarter = PACK // 8
    for m, ref in enumerate((b0_ref, b1_ref, b2_ref, b3_ref)):
        for h in (0, 1):
            at = (core ^ h) * 4 + (me ^ m)
            lo = h * (quarter + 8)
            all_ref[pl.ds(pl.multiple_of(at * quarter, 8), quarter), :] = ref[lo : lo + quarter]
            xgx_ref[at] = ref[lo + quarter : lo + quarter + 8]
    row = lax.broadcasted_iota(jnp.int32, (128, 128), 0)
    col = lax.broadcasted_iota(jnp.int32, (128, 128), 1)

    def pair(at, d):
        m = all_ref[at : at + 128] * scale
        t = m.T
        diag = all_ref[768 + d : 769 + d] * scale
        return (
            jnp.where(row <= col, m, t),
            jnp.where(row > col, m, jnp.where(row < col, t, diag)),
        )

    pp, pcp = pair(0, 0)
    pgp, ygy = pair(128, 1)
    yy, ycy = pair(256, 2)
    py = all_ref[384:512] * scale
    xs = all_ref[512:640] * scale
    px, yx, ygx = xs[:, :32], xs[:, 32:64], xs[:, 64:96]
    xx = xs[:32, 96:]
    total = xgx_ref[0]
    for k in range(1, 8):
        total = total + xgx_ref[k]
    total = total * scale
    xgx = jnp.concatenate([total[:, B * k : B * (k + 1)] for k in range(4)], axis=0)
    z = PRIOR - B

    h = py[:, z:]
    c = 2.0 * h - dot(pp, h)
    s = yy[z:, z:] + tdot(c, dot(pp, c) - 2.0 * h)
    inv_t = inverse_factor(s).T
    a, b = -dot(c, inv_t), inv_t

    hp = dot(py, a) + dot(px, b)
    wy = dot(yy, a) + dot(yx, b)
    wx = tdot(yx, a) + dot(xx, b)
    hq = tdot(a, hp) + tdot(b, wy[z:])
    kq = dot(pp, a) + dot(h, b)
    kqq = tdot(a, kq) + tdot(b, tdot(h, a) + dot(yy[z:, z:], b))
    cp = 2.0 * hp - dot(pp, hp) - dot(kq, hq)
    cq = 2.0 * hq - tdot(kq, hp) - dot(kqq, hq)
    s = (
        tdot(a, wy)
        + tdot(b, wx)
        + tdot(cp, dot(pp, cp) + dot(kq, cq) - 2.0 * hp)
        + tdot(cq, tdot(kq, cp) + dot(kqq, cq) - 2.0 * hq)
    )
    inv_t = inverse_factor(s).T
    zero_z = jnp.zeros((z, B), F32)
    u = -dot(cp + dot(a, cq), inv_t)
    v = dot(a - jnp.concatenate([zero_z, dot(b, cq)], axis=0), inv_t)
    x = dot(b, inv_t)

    zero = jnp.zeros((B, B), F32)
    tp = jnp.concatenate([a, u, jnp.zeros((128, B), F32)], axis=1)
    ty = jnp.concatenate([jnp.concatenate([zero_z, b], axis=0), v, a], axis=1)
    tx = jnp.concatenate([zero, x, b], axis=1)
    t = jnp.concatenate([m[:, :64].T for m in (tp, ty, tx)], axis=1)
    copies = combine(
        t, p_ref, y_ref, a_ref, ax_ref, q_ref, n_ref, qbuf_ref, nbuf_ref, sems, ready
    )

    pcx, ycx, xcx = ycy[:, z:], ygy[:, z:], ygx[z:]
    cpt = dot(pcp, tp) + dot(pgp, ty) + dot(pcx, tx)
    cyt = dot(pgp, tp) + dot(ycy, ty) + dot(ycx, tx)
    cxt = tdot(pcx, tp) + tdot(ycx, ty) + dot(xcx, tx)
    qp, qy, qx = tp[:, :64], ty[:, :64], tx[:, :64]
    r = tdot(qp, cpt) + tdot(qy, cyt) + tdot(qx, cxt)
    side = cpt[:, :64]
    c_ref[0:128, 0:128] = pcp
    c_ref[0:128, 128:192] = side
    c_ref[128:192, 0:128] = side.T
    c_ref[128:192, 128:192] = r[:, :64]
    gpt = cyt[:, 32:64]
    gyt = dot(ycy, u) + dot(ygy, v) + dot(ygx, x)
    gxt = tdot(ycx, u) + tdot(ygx, v) + dot(xgx, x)
    g_ref[:, 0:128] = jnp.concatenate([cpt[:, 64:96].T, gpt.T], axis=0)
    g2 = tdot(qp, gpt) + tdot(qy, gyt) + tdot(qx, gxt)
    g_ref[:, 128:192] = jnp.concatenate([r[:, 64:96].T, g2.T], axis=0)
    kp = all_ref[640:768]
    extra = all_ref[512:640][:, 96:]
    kx = jnp.concatenate([extra[32:64], extra[64:96]], axis=1)
    b_ref[:, 0:128] = kp[:, :64].T
    b_ref[:, 128:192] = tdot(kp[:, :64], qp) + tdot(kp[:, 64:], qy) + tdot(kx, qx)


    for j, (src, dst) in enumerate(((g_ref, g_out), (c_ref, c_out), (b_ref, b_out))):
        copy = pltpu.make_async_copy(src, dst, small_sems.at[j])
        copy.start()
        copies.append(copy)
    for copy in copies:
        copy.wait()


def final(place, pieces, p, y, ay, ax, scale):
    rows, fields, width = p.shape
    steps = rows // DEPTH
    small = ((64, 192), (192, 192), (64, 192))
    return call(
        functools.partial(final_kernel, scale),
        tuple(
            pltpu.HBM(d, F32) for d in ((2 * B, rows, width), (B, rows, width)) + small
        ),
        [SM] + [VM] * 4 + [HBM] * 4,
        (HBM,) * 5,
        scratch=[pltpu.VMEM(p.shape, F32)] * 3
        + [
            pltpu.VMEM(ax.shape, F32),
            pltpu.VMEM((PACK, 128), F32),
            pltpu.VMEM((8, 8, 128), F32),
            pltpu.VMEM((steps, 2 * B, DEPTH, width), F32),
            pltpu.VMEM((steps, B, DEPTH, width), F32),
        ]
        + [pltpu.VMEM(d, F32) for d in small]
        + [pltpu.SemaphoreType.DMA(d) for d in ((4, rows // CHUNK), (2, steps), (3,))],
        flops=1 << 30,
        moved=5 * p.size * 4,
        limit=40,
    )(place, *pieces, *(in_hbm(a) for a in (p, y, ay, ax)))


def on_device(prior, cond_x, cond_y, cap_level, decap, via, ports):
    rows_here, cols_here = prior.shape[1:]
    total_cols = cols_here * lax.axis_size("gy")
    scale = 1.0 / (rows_here * lax.axis_size("gx") * total_cols)
    gxe = 0.125 * cond_x.astype(F32)
    gye = 0.125 * cond_y.astype(F32)
    gvia = 0.5 * via.astype(F32)
    cap = 0.25 * cap_level.astype(F32) * (1.0 + 2.0 * decap.astype(F32))

    core = (lax.axis_index("gx") % 2)[None]
    me = lax.axis_index("gy")
    p, mate, cross, edge = regroup(core, prior)
    slot = 2 * jnp.arange(rows_here)[:, None] == jnp.arange(cols_here)[None, :]
    gye_edge = jnp.sum(jnp.where(slot, gye[:, -1:], 0.0), axis=0, keepdims=True)
    spare = jnp.zeros((7, cols_here), F32)
    pair_row = jnp.where(core == 0, gxe[-1], 0.0)[None]
    cross_row = jnp.where(core == 0, 0.0, gxe[-1])[None]
    mate = jnp.concatenate([mate, pair_row, spare], axis=0)
    cross = jnp.concatenate([cross, cross_row, spare], axis=0)
    edge_more = jnp.concatenate([edge, gye_edge, spare], axis=0)
    mate, cross, fl, fr = exchange(mate, cross, edge_more, edge)
    gxw_first = mate[PRIOR : PRIOR + 1] + cross[PRIOR : PRIOR + 1]
    gxw = jnp.concatenate([gxw_first, gxe[:-1]], axis=0)
    gys_first = jnp.sum(jnp.where(slot, fl[PRIOR : PRIOR + 1], 0.0), axis=1, keepdims=True)
    gys = jnp.concatenate([gys_first, gye[:, :-1]], axis=1)
    center = gvia + gxe + gxw + gye + gys
    coef = jnp.stack([center, gxe, gxw, gye, gys, 1.0 / cap])

    port_rows = ports // total_cols - lax.axis_index("gx") * rows_here
    port_cols = ports % total_cols - lax.axis_index("gy") * cols_here
    inside = (
        (port_rows >= 0) & (port_rows < rows_here) & (port_cols >= 0) & (port_cols < cols_here)
    )
    where = jnp.stack(
        [
            jnp.clip(port_rows, 0, rows_here - 1),
            jnp.clip(port_cols, 0, cols_here - 1),
            inside.astype(jnp.int32),
        ]
    )
    y, y_far, p_in, *sends = stencil(core, coef, p, mate, cross, fl, fr, True)
    sides = exchange(*sends, sends[2])
    grams_y = gram_y(cap, p_in, y)
    ay, ay_far, mate, cross, edge = stencil(core, coef, y, *sides, False)
    ygy, xs, kp, kx = gram_x(where, cap, p_in, y, ay)
    cross = swap_cross(cross)
    place = jnp.concatenate([me[None], core])
    keep, give = pack(core, [*grams_y, ygy, xs, kp, kx], mate)
    got = swap(give, "gx", 1)
    own, *sends = fan(place, keep, got, edge)
    quads = [own] + [swap(x, "gy", m) for m, x in zip((1, 2, 3), sends)]
    ax, x = last(place, coef, ay, got, cross, quads)
    pieces = sum_over_chips(x)
    basis, image, g_t, c, b_t = final(place, pieces, p, y_far, ay_far, ax, scale)
    return basis, image, g_t.T, c, b_t.T


def solution(mesh):
    in_specs = (
        P(None, "gx", "gy"),
        P("gx", "gy"),
        P("gx", "gy"),
        P("gx", "gy"),
        P("gx", "gy"),
        P("gx", "gy"),
        P(),
    )
    out_specs = (P(None, "gx", "gy"), P(None, "gx", "gy"), P(), P(), P())
    return jax.shard_map(
        on_device, mesh=mesh, in_specs=in_specs, out_specs=out_specs, check_vma=False
    )
```

```python
import functools

import jax
import jax.numpy as jnp
from jax import lax
from jax.experimental import pallas as pl
from jax.experimental.pallas import tpu as pltpu
from jax.sharding import PartitionSpec as P

B = 32
PRIOR = 128
F32 = jnp.float32
HI = lax.Precision.HIGHEST
MIB = 1024 * 1024
TILE = 32
CHUNK = 16
DEPTH = 8
PACK = 832
VM = pl.BlockSpec(memory_space=pltpu.VMEM)
SM = pl.BlockSpec(memory_space=pltpu.SMEM)
HBM = pl.BlockSpec(memory_space=pltpu.HBM)
ANY = pl.BlockSpec(memory_space=pl.ANY)


def call(kernel, out, in_specs, out_specs, scratch=(), flops=0, moved=0, limit=24, aliases={}):
    return pl.pallas_call(
        kernel,
        out_shape=out,
        in_specs=in_specs,
        out_specs=out_specs,
        scratch_shapes=scratch,
        input_output_aliases=aliases,
        compiler_params=pltpu.CompilerParams(vmem_limit_bytes=limit * MIB),
        cost_estimate=pl.CostEstimate(flops=flops, bytes_accessed=moved, transcendentals=0),
    )


def shape(*dims):
    return jax.ShapeDtypeStruct(dims, F32)


def held(*dims):
    return pltpu.VMEM(dims, F32)


def in_hbm(x):
    return pltpu.with_memory_space_constraint(x, pltpu.HBM)


def lanes_of(dims):
    return lax.broadcasted_iota(jnp.int32, dims, len(dims) - 1)


def pack_edges(v_ref, edge_ref, skip=0):
    rows, fields, width = v_ref.shape
    slot = lanes_of((TILE, width)) >> 1
    for at in range(skip, fields, TILE):
        edge = jnp.zeros((TILE, width), F32)
        for r in range(rows):
            edge = jnp.where(
                slot == r, pltpu.roll(v_ref[r, at : at + TILE, :], 2 * r + 1, 1), edge
            )
        edge_ref[at - skip : at - skip + TILE] = edge


def ends(core, v_ref, mate_ref, cross_ref, first=0):
    top = v_ref[0, first:, :]
    low = v_ref[v_ref.shape[0] - 1, first:, :]
    mate_ref[...] = jnp.where(core == 0, low, top)
    cross_ref[...] = jnp.where(core == 0, top, low)


def regroup_kernel(
    core_ref, p_ref, out_hbm, mate_ref, cross_ref, edge_ref, buf_ref, out_ref, sems
):
    parts, fields, rows, width = buf_ref.shape
    copies = [
        pltpu.make_async_copy(p_ref.at[pl.ds(i * fields, fields)], buf_ref.at[i], sems.at[0, i])
        for i in range(parts)
    ]
    back = []
    for copy in copies:
        copy.start()
    for i in range(parts):
        copies[i].wait()
        cut = slice(i * fields, (i + 1) * fields)
        for at in range(0, rows, DEPTH):
            flat = buf_ref.at[i].reshape(fields * rows, width)
            got = [flat[pl.ds(at + k, fields, stride=rows), :] for k in range(DEPTH)]
            for k in range(DEPTH):
                out_ref[at + k, cut, :] = got[k]
        held_part = (slice(None), pl.ds(i * fields, fields), slice(None))
        back.append(
            pltpu.make_async_copy(out_ref.at[held_part], out_hbm.at[held_part], sems.at[1, i])
        )
        back[-1].start()
    pack_edges(out_ref, edge_ref)
    ends(core_ref[0], out_ref, mate_ref, cross_ref)
    for copy in back:
        copy.wait()


def regroup(core, prior):
    fields, rows, width = prior.shape
    parts = fields // CHUNK
    return call(
        regroup_kernel,
        (pltpu.HBM((rows, fields, width), F32),) + (shape(fields, width),) * 3,
        [SM, HBM],
        (HBM,) + (VM,) * 3,
        scratch=[
            pltpu.VMEM((parts, CHUNK, rows, width), F32),
            pltpu.VMEM((rows, fields, width), F32),
            pltpu.SemaphoreType.DMA((2, parts)),
        ],
        moved=2 * prior.size * 4,
        limit=40,
    )(core, in_hbm(prior))


def stencil_rows(
    core, coef_ref, v_ref, first, mate, cross, from_left, from_right, seam_ref, put, ready=None
):
    rows, width = v_ref.shape[0], v_ref.shape[2]
    fields = seam_ref.shape[0]
    tile = 8
    lane = lanes_of((tile, width))
    odd, start, stop = (lane & 1) == 1, lane == 0, lane == width - 1
    for at in range(0, fields, tile):
        cut = slice(at, at + tile)
        seam_ref[cut] = jnp.where(
            odd, pltpu.roll(from_left(cut), 1, 1), pltpu.roll(from_right(cut), width - 1, 1)
        )
    for r in range(rows):
        if ready is not None:
            ready(r)
        c = [jnp.broadcast_to(coef_ref[k, r : r + 1, :], (tile, width)) for k in range(6)]
        for at in range(0, fields, tile):
            cut = slice(at, at + tile)
            src = slice(first + at, first + at + tile)
            v = v_ref[r, src, :]
            if r == 0:
                up = jnp.where(core == 0, cross(cut), mate(cut))
            else:
                up = v_ref[r - 1, src, :]
            if r == rows - 1:
                down = jnp.where(core == 0, mate(cut), cross(cut))
            else:
                down = v_ref[r + 1, src, :]
            side = pltpu.roll(seam_ref[cut], width - 1 - 2 * r, 1)
            south = jnp.where(start, side, pltpu.roll(v, 1, 1))
            north = jnp.where(stop, side, pltpu.roll(v, width - 1, 1))
            put(r, cut, c[0] * v - c[1] * down - c[2] * up - c[3] * north - c[4] * south, c[5])


def reader(ref, at=0):
    return lambda cut: ref[at + cut.start : at + cut.stop, :]


def stencil_kernel(
    first, core_ref, coef_ref, in_ref, mate_ref, cross_ref, fl_ref, fr_ref, y_ref, y_hbm, *rest
):
    if first:
        v_ref, mate_out, cross_out, edge_ref, seam_ref, out_sems, in_sems = rest
    else:
        mate_out, cross_out, edge_ref, seam_ref, out_sems = rest
        v_ref = in_ref
    rows = v_ref.shape[0]
    parts = [pl.ds(i * CHUNK, CHUNK) for i in range(rows // CHUNK)]
    loads, stores = [], []
    if first:
        for i, part in enumerate(parts):
            loads.append(pltpu.make_async_copy(in_ref.at[part], v_ref.at[part], in_sems.at[i]))
            loads[-1].start()

    def store(i):
        stores.append(
            pltpu.make_async_copy(y_ref.at[parts[i]], y_hbm.at[parts[i]], out_sems.at[i])
        )
        stores[-1].start()

    def ready(r):
        if first and r == 0:
            loads[0].wait()
        if first and r % CHUNK == CHUNK - 1 and r + 1 < rows:
            loads[r // CHUNK + 1].wait()
        if r % CHUNK == 0 and r > 0:
            store(r // CHUNK - 1)

    def put(r, cut, image, inv_cap):
        y_ref[r, cut, :] = image * inv_cap

    stencil_rows(
        core_ref[0], coef_ref, v_ref, 0, reader(mate_ref), reader(cross_ref), reader(fl_ref),
        reader(fr_ref), seam_ref, put, ready,
    )
    store(len(parts) - 1)
    skip = y_ref.shape[1] - edge_ref.shape[0]
    pack_edges(y_ref, edge_ref, skip)
    ends(core_ref[0], y_ref, mate_out, cross_out, skip)
    for copy in stores:
        copy.wait()


def stencil(core, coef, v, mate, cross, from_left, from_right, first):
    rows, fields, width = v.shape
    send = shape(fields if first else B, width)
    field = held(rows, fields, width)
    sems = pltpu.SemaphoreType.DMA((rows // CHUNK,))
    return call(
        functools.partial(stencil_kernel, first),
        (field, pltpu.HBM((rows, fields, width), F32)) + (field,) * first + (send,) * 3,
        [SM, VM, HBM if first else VM] + [VM] * 4,
        (VM, HBM) + (VM,) * first + (VM,) * 3,
        scratch=[pltpu.VMEM((fields, width), F32), sems] + [sems] * first,
        flops=12 * v.size,
        moved=2 * v.size * 4,
    )(core, coef, in_hbm(v) if first else v, mate, cross, from_left, from_right)


def wide(ref, at):
    return jnp.concatenate([ref[at + i] for i in range(CHUNK)], axis=1)


def wide_row(ref, at):
    return jnp.concatenate([ref[pl.ds(at + i, 1), :] for i in range(CHUNK)], axis=1)


def halves(x):
    high = x.astype(jnp.bfloat16)
    low = (x - high.astype(F32)).astype(jnp.bfloat16)
    return jnp.concatenate([high, low], axis=0)


def nt(a, b):
    return lax.dot_general(a, b, (((1,), (1,)), ((), ())), preferred_element_type=F32)


def fold(acc, row, rows, col, cols):
    a = acc[row : row + rows, col : col + cols] + acc[row : row + rows, col + cols : col + 2 * cols]
    row += rows
    b = acc[row : row + rows, col : col + cols] + acc[row : row + rows, col + cols : col + 2 * cols]
    return a + b


def over_chunks(rows, accs, terms):
    def add(i, carry):
        for acc, term in zip(accs, terms(i * CHUNK)):
            acc[...] += term
        return carry

    for acc in accs:
        acc[...] = jnp.zeros_like(acc)
    lax.fori_loop(0, rows // CHUNK, add, 0)


def gram_y_kernel(
    cap_ref, p_ref, y_ref, pp_ref, pcp_ref, py_ref, yy_ref, pgp_ref, ygp_ref, accp_ref, accy_ref
):
    def terms(at):
        p, y, cap = wide(p_ref, at), wide(y_ref, at), wide_row(cap_ref, at)
        hp, hy, hg = halves(p), halves(y), halves(y * cap)
        right = jnp.concatenate([hy, hg], axis=0)
        yield nt(hp, jnp.concatenate([right, hp, halves(p * cap)], axis=0))
        yield nt(hy, right)

    over_chunks(p_ref.shape[0], (accp_ref, accy_ref), terms)
    py_ref[...] = fold(accp_ref, 0, 128, 0, 128)
    pgp_ref[...] = fold(accp_ref, 0, 128, 256, 128)
    pp_ref[...] = fold(accp_ref, 0, 128, 512, 128)
    pcp_ref[...] = fold(accp_ref, 0, 128, 768, 128)
    yy_ref[...] = fold(accy_ref, 0, 128, 0, 128)
    ygp_ref[...] = fold(accy_ref, 0, 128, 256, 128)


def gram_x_kernel(
    where_ref, cap_ref, p_ref, y_ref, a_ref, ygy_ref, x_ref, kp_ref, kx_ref, acc_ref, accx_ref
):
    def terms(at):
        ay = wide(a_ref, at)
        hp, hy = halves(wide(p_ref, at)), halves(wide(y_ref, at))
        hg = halves(ay * wide_row(cap_ref, at))
        hx = halves(ay[PRIOR - B :])
        yield nt(hy, hg)
        yield nt(jnp.concatenate([hp, hy, hg, hx], axis=0), hx)

    over_chunks(p_ref.shape[0], (acc_ref, accx_ref), terms)
    ygy_ref[...] = fold(acc_ref, 0, 128, 0, 128)
    px = fold(accx_ref, 0, 128, 0, B)
    yx = fold(accx_ref, 256, 128, 0, B)
    gx = fold(accx_ref, 512, 128, 0, B)
    xx = fold(accx_ref, 768, B, 0, B)
    rest = jnp.concatenate([xx, jnp.zeros((128 - B, B), F32)], axis=0)
    x_ref[...] = jnp.concatenate([px, yx, gx, rest], axis=1)

    kp_ref[...] = jnp.zeros_like(kp_ref)
    kx_ref[...] = jnp.zeros_like(kx_ref)
    n = where_ref.shape[1]

    def step(k, carry):
        @pl.when(where_ref[2, k] > 0)
        def _():
            r, c = where_ref[0, k], where_ref[1, k]
            for v, spot, out_ref in (
                (p_ref[r], k, kp_ref),
                (y_ref[r], k + n, kp_ref),
                (a_ref[r][PRIOR - B :], k, kx_ref),
            ):
                moved = pltpu.roll(v, lax.rem(spot - c + 128, 128), 1)
                out_ref[...] = jnp.where(lanes_of(v.shape) == spot, moved, out_ref[...])

        return carry

    lax.fori_loop(0, n, step, 0)


def gram_y(cap, p, y):
    return call(
        gram_y_kernel,
        (shape(128, 128),) * 6,
        [VM] * 3,
        (VM,) * 6,
        scratch=[pltpu.VMEM((256, 1024), F32), pltpu.VMEM((256, 512), F32)],
        flops=6 * 2 * 256 * 256 * p.shape[0] * 128,
        moved=2 * p.size * 4,
    )(cap, p, y)


def gram_x(where, cap, p, y, ay):
    return call(
        gram_x_kernel,
        (shape(128, 128),) * 3 + (shape(B, 128),),
        [SM] + [VM] * 4,
        (VM,) * 4,
        scratch=[pltpu.VMEM((256, 256), F32), pltpu.VMEM((832, 64), F32)],
        flops=4 * 2 * 256 * 256 * p.shape[0] * 128,
        moved=3 * p.size * 4,
    )(where, cap, p, y, ay)


def pack_kernel(
    core_ref, pp_ref, pcp_ref, py_ref, yy_ref, pgp_ref, ygp_ref, ygy_ref, x_ref, kp_ref, kx_ref,
    mate_ref, cross_ref, keep_ref, give_ref, pack_ref,
):
    row = lax.broadcasted_iota(jnp.int32, (128, 128), 0)
    col = lax.broadcasted_iota(jnp.int32, (128, 128), 1)

    def diagonal(m):
        return jnp.sum(jnp.where(row == col, m, 0.0), axis=0, keepdims=True)

    pack_ref[0:128] = jnp.where(row <= col, pp_ref[...], pcp_ref[...])
    pack_ref[128:256] = jnp.where(row <= col, pgp_ref[...], ygy_ref[...])
    pack_ref[256:384] = jnp.where(row <= col, yy_ref[...], ygp_ref[...])
    pack_ref[384:512] = py_ref[...]
    kx, zero = kx_ref[...], jnp.zeros((B, B), F32)
    extra = jnp.concatenate([zero, kx[:, :B], kx[:, B : 2 * B], zero], axis=0)
    pack_ref[512:640] = x_ref[...] + jnp.concatenate([jnp.zeros((128, 96), F32), extra], axis=1)
    pack_ref[640:768] = kp_ref[...]
    diag = [diagonal(m[...]) for m in (pcp_ref, ygy_ref, ygp_ref)]
    pack_ref[768:776] = jnp.concatenate(diag + [jnp.zeros((5, 128), F32)], axis=0)
    pack_ref[776:832] = jnp.zeros((56, 128), F32)
    half = PACK // 2
    core = core_ref[0]
    keep_ref[...] = pack_ref[pl.ds(pl.multiple_of(core * half, 8), half), :]
    give_ref[0:half] = pack_ref[pl.ds(pl.multiple_of((1 - core) * half, 8), half), :]
    give_ref[half : half + B] = mate_ref[...]


def pack(core, mats, mate, cross):
    return call(
        pack_kernel,
        (shape(PACK // 2, 128), shape(PACK // 2 + B, 128)),
        [SM] + [VM] * (1 + len(mats)) + [ANY],
        (VM,) * 2,
        scratch=[pltpu.VMEM((PACK, 128), F32)],
        moved=1 << 20,
    )(core, *mats, mate, cross)


def fan_kernel(place_ref, keep_ref, got_ref, edge_ref, own_ref, s1_ref, s2_ref, s3_ref, sum_ref):
    half, quarter = PACK // 2, PACK // 8
    sum_ref[...] = keep_ref[...] + got_ref[0:half]
    for m, ref in enumerate((own_ref, s1_ref, s2_ref, s3_ref)):
        at = pl.multiple_of((place_ref[0] ^ m) * quarter, 8)
        ref[0:quarter] = sum_ref[pl.ds(at, quarter), :]
    s1_ref[quarter:] = edge_ref[...]
    s3_ref[quarter:] = edge_ref[...]


def fan(place, keep, got, edge):
    quarter = PACK // 8
    return call(
        fan_kernel,
        tuple(shape(quarter + extra, 128) for extra in (0, B, 0, B)),
        [SM] + [VM] * 3,
        (VM,) * 4,
        scratch=[pltpu.VMEM((PACK // 2, 128), F32)],
        moved=1 << 20,
    )(place, keep, got, edge)


def last_kernel(
    place_ref, coef_ref, a_ref, mate_ref, cross_ref, own_ref, g1_ref, g2_ref, g3_ref,
    ax_hbm, sum_ref, ax_ref, image_ref, seam_ref, sem,
):
    me, core = place_ref[0], place_ref[1]
    quarter = PACK // 8

    def put(r, cut, image, inv_cap):
        ax_ref[r, cut, :] = image * inv_cap
        image_ref[r, cut, :] = image

    near, far = reader(g1_ref, quarter), reader(g3_ref, quarter)

    def from_left(cut):
        other = jnp.where(me == 2, far(cut), 0.0)
        return jnp.where(me % 2 == 1, near(cut), other)

    def from_right(cut):
        other = jnp.where(me == 1, far(cut), 0.0)
        return jnp.where(me % 2 == 0, near(cut), other)

    stencil_rows(
        core, coef_ref, a_ref, PRIOR - B, reader(mate_ref, PACK // 2), reader(cross_ref),
        from_left, from_right, seam_ref, put,
    )
    copy = pltpu.make_async_copy(ax_ref, ax_hbm, sem)
    copy.start()
    sum_ref[0:quarter] = (own_ref[...] + g1_ref[0:quarter]) + (g2_ref[...] + g3_ref[0:quarter])
    acc = jnp.zeros((2 * B, 2 * B), F32)
    for at in range(0, a_ref.shape[0], CHUNK):
        hx = halves(wide(a_ref, at)[PRIOR - B :])
        acc = acc + nt(hx, halves(wide(image_ref, at)))
    xgx = fold(acc, 0, B, 0, B)
    sum_ref[quarter:] = jnp.concatenate([xgx[8 * k : 8 * k + 8] for k in range(4)], axis=1)
    copy.wait()


def last(place, coef, ay, mate, cross, quads):
    rows, fields, width = ay.shape
    return call(
        last_kernel,
        (pltpu.HBM((rows, B, width), F32), shape(PACK // 8 + 8, 128)),
        [SM] + [VM] * 8,
        (HBM, VM),
        scratch=[
            pltpu.VMEM((rows, B, width), F32),
            pltpu.VMEM((rows, B, width), F32),
            pltpu.VMEM((B, width), F32),
            pltpu.SemaphoreType.DMA,
        ],
        flops=1 << 27,
        moved=2 * rows * B * width * 4,
    )(place, coef, ay, mate, cross, *quads)


def split(x):
    high = x.astype(jnp.bfloat16)
    return high, (x - high.astype(F32)).astype(jnp.bfloat16)


def times(t, pair):
    rows = t.shape[0] // 2
    big = jnp.dot(t, pair[0], preferred_element_type=F32)
    return big[:rows] + big[rows:] + jnp.dot(t[:rows], pair[1], preferred_element_type=F32)


def combine(t, p_ref, y_ref, a_ref, ax_ref, q_ref, n_ref, qbuf_ref, nbuf_ref, sems, ready):
    two = 2 * B
    high, low = split(t)

    def cut(lo, hi, first):
        return jnp.concatenate([high[first:, lo:hi], low[first:, lo:hi]], axis=0)

    t_py, t_x, t_y, t_rest = cut(0, 256, 0), cut(256, 288, 0), cut(0, 128, B), cut(128, 288, B)
    rows, fields, width = p_ref.shape
    copies = []
    for at in range(0, rows, DEPTH):
        ready(at)

        def row_block(ref):
            return jnp.concatenate([ref[at + i] for i in range(DEPTH)], axis=1)

        p, y = split(row_block(p_ref)), split(row_block(y_ref))
        a, ax = split(row_block(a_ref)), split(row_block(ax_ref))
        py = tuple(jnp.concatenate(pair, axis=0) for pair in zip(p, y))
        rest = tuple(jnp.concatenate(pair, axis=0) for pair in zip(a, ax))
        x = tuple(part[PRIOR - B :] for part in a)
        q = times(t_py, py) + times(t_x, x)
        n = times(t_y, y) + times(t_rest, rest)
        step = at // DEPTH
        for k in range(DEPTH):
            lanes = slice(k * width, (k + 1) * width)
            qbuf_ref.at[step].reshape(two * DEPTH, width)[pl.ds(k, two, stride=DEPTH), :] = q[
                :, lanes
            ]
            nbuf_ref.at[step].reshape(B * DEPTH, width)[pl.ds(k, B, stride=DEPTH), :] = n[
                :, lanes
            ]
        for j, (src, dst) in enumerate(((qbuf_ref, q_ref), (nbuf_ref, n_ref))):
            copy = pltpu.make_async_copy(
                src.at[step], dst.at[:, pl.ds(at, DEPTH), :], sems.at[j, step]
            )
            copy.start()
            copies.append(copy)
    return copies


def swap(x, axis, mask):
    return lax.ppermute(x, axis, [(i, i ^ mask) for i in range(lax.axis_size(axis))])


def shift(x, axis, step):
    size = lax.axis_size(axis)
    return lax.ppermute(
        x, axis, [(i, i + step) for i in range(size) if 0 <= i + step < size]
    )


def swap_cross(x):
    size = lax.axis_size("gx")
    pairs = [(i, i + 1) for i in range(1, size - 1, 2)]
    return lax.ppermute(x, "gx", pairs + [(j, i) for i, j in pairs])


def sum_over_chips(x):
    mask = 2
    while mask < lax.axis_size("gx"):
        x = x + swap(x, "gx", mask)
        mask *= 2
    x = jnp.concatenate([x] + [swap(x, "gy", m) for m in (1, 2, 3)], axis=0)
    return x, swap(x, "gx", 1)


def exchange(mate, cross, edge, edge_left):
    return swap(mate, "gx", 1), swap_cross(cross), shift(edge, "gy", 1), shift(edge_left, "gy", -1)


def dot(a, b):
    return jnp.dot(a, b, precision=HI, preferred_element_type=F32)


def tdot(a, b):
    return lax.dot_general(
        a, b, (((0,), (0,)), ((), ())), precision=HI, preferred_element_type=F32
    )


def inverse_factor(s):
    n = s.shape[0]
    s = 0.5 * (s + s.T)
    row = lax.broadcasted_iota(jnp.int32, (n, 128), 0)
    lane = lax.broadcasted_iota(jnp.int32, (n, 128), 1)
    eye = jnp.where(row + n == lane, 1.0, 0.0)
    a = jnp.concatenate([s, jnp.zeros((n, 128 - n), F32)], axis=1) + eye
    for j in range(0, n, 2):
        one = jnp.broadcast_to(a[:, j : j + 1], (n, 128))
        two = jnp.broadcast_to(a[:, j + 1 : j + 2], (n, 128))
        inv = 1.0 / one[j : j + 1]
        step = one[j + 1 : j + 2] * inv
        head = a[j : j + 1]
        tail = a[j + 1 : j + 2] - step * head
        left = one * inv
        two = two - left * two[j : j + 1]
        right = two * (1.0 / two[j + 1 : j + 2])
        below = a - left * head - right * tail
        a = jnp.where(row > j + 1, below, jnp.where(row == j + 1, tail, a))
    diag = jnp.sum(jnp.where(row == lane, a, 0.0), axis=1, keepdims=True)
    return (a / jnp.sqrt(diag))[:, n : 2 * n]


def final_kernel(
    scale, place_ref, own_ref, other_ref, p_hbm, y_hbm, a_hbm, ax_hbm,
    q_ref, n_ref, g_out, c_out, b_out, p_ref, y_ref, a_ref, ax_ref, all_ref, xgx_ref, qbuf_ref,
    nbuf_ref, g_ref, c_ref, b_ref, load_sems, sems, small_sems,
):
    pairs = ((p_hbm, p_ref), (y_hbm, y_ref), (a_hbm, a_ref), (ax_hbm, ax_ref))
    loads = []
    for i in range(p_ref.shape[0] // CHUNK):
        part = pl.ds(i * CHUNK, CHUNK)
        for j, (src, dst) in enumerate(pairs):
            loads.append(
                pltpu.make_async_copy(src.at[part], dst.at[part], load_sems.at[j, i])
            )
            loads[-1].start()

    def ready(at):
        if at % CHUNK == 0:
            for load in loads[at // CHUNK * 4 : at // CHUNK * 4 + 4]:
                load.wait()

    me, core = place_ref[0], place_ref[1]
    quarter = PACK // 8
    for m in range(4):
        for h, ref in enumerate((own_ref, other_ref)):
            at = (core ^ h) * 4 + (me ^ m)
            lo = m * (quarter + 8)
            all_ref[pl.ds(pl.multiple_of(at * quarter, 8), quarter), :] = ref[lo : lo + quarter]
            xgx_ref[at] = ref[lo + quarter : lo + quarter + 8]
    row = lax.broadcasted_iota(jnp.int32, (128, 128), 0)
    col = lax.broadcasted_iota(jnp.int32, (128, 128), 1)

    def pair(at, d):
        m = all_ref[at : at + 128] * scale
        t = m.T
        diag = all_ref[768 + d : 769 + d] * scale
        return (
            jnp.where(row <= col, m, t),
            jnp.where(row > col, m, jnp.where(row < col, t, diag)),
        )

    pp, pcp = pair(0, 0)
    pgp, ygy = pair(128, 1)
    yy, ycy = pair(256, 2)
    py = all_ref[384:512] * scale
    xs = all_ref[512:640] * scale
    px, yx, ygx = xs[:, :32], xs[:, 32:64], xs[:, 64:96]
    xx = xs[:32, 96:]
    total = xgx_ref[0]
    for k in range(1, 8):
        total = total + xgx_ref[k]
    total = total * scale
    xgx = jnp.concatenate([total[:, B * k : B * (k + 1)] for k in range(4)], axis=0)
    z = PRIOR - B

    h = py[:, z:]
    c = 2.0 * h - dot(pp, h)
    s = yy[z:, z:] + tdot(c, dot(pp, c) - 2.0 * h)
    inv_t = inverse_factor(s).T
    a, b = -dot(c, inv_t), inv_t

    hp = dot(py, a) + dot(px, b)
    wy = dot(yy, a) + dot(yx, b)
    wx = tdot(yx, a) + dot(xx, b)
    hq = tdot(a, hp) + tdot(b, wy[z:])
    kq = dot(pp, a) + dot(h, b)
    kqq = tdot(a, kq) + tdot(b, tdot(h, a) + dot(yy[z:, z:], b))
    cp = 2.0 * hp - dot(pp, hp) - dot(kq, hq)
    cq = 2.0 * hq - tdot(kq, hp) - dot(kqq, hq)
    s = (
        tdot(a, wy)
        + tdot(b, wx)
        + tdot(cp, dot(pp, cp) + dot(kq, cq) - 2.0 * hp)
        + tdot(cq, tdot(kq, cp) + dot(kqq, cq) - 2.0 * hq)
    )
    inv_t = inverse_factor(s).T
    zero_z = jnp.zeros((z, B), F32)
    u = -dot(cp + dot(a, cq), inv_t)
    v = dot(a - jnp.concatenate([zero_z, dot(b, cq)], axis=0), inv_t)
    x = dot(b, inv_t)

    zero = jnp.zeros((B, B), F32)
    tp = jnp.concatenate([a, u, jnp.zeros((128, B), F32)], axis=1)
    ty = jnp.concatenate([jnp.concatenate([zero_z, b], axis=0), v, a], axis=1)
    tx = jnp.concatenate([zero, x, b], axis=1)
    t = jnp.concatenate([m[:, :64].T for m in (tp, ty, tx)], axis=1)
    copies = combine(
        t, p_ref, y_ref, a_ref, ax_ref, q_ref, n_ref, qbuf_ref, nbuf_ref, sems, ready
    )

    pcx, ycx, xcx = ycy[:, z:], ygy[:, z:], ygx[z:]
    cpt = dot(pcp, tp) + dot(pgp, ty) + dot(pcx, tx)
    cyt = dot(pgp, tp) + dot(ycy, ty) + dot(ycx, tx)
    cxt = tdot(pcx, tp) + tdot(ycx, ty) + dot(xcx, tx)
    qp, qy, qx = tp[:, :64], ty[:, :64], tx[:, :64]
    r = tdot(qp, cpt) + tdot(qy, cyt) + tdot(qx, cxt)
    side = cpt[:, :64]
    c_ref[0:128, 0:128] = pcp
    c_ref[0:128, 128:192] = side
    c_ref[128:192, 0:128] = side.T
    c_ref[128:192, 128:192] = r[:, :64]
    gpt = cyt[:, 32:64]
    gyt = dot(ycy, u) + dot(ygy, v) + dot(ygx, x)
    gxt = tdot(ycx, u) + tdot(ygx, v) + dot(xgx, x)
    g_ref[:, 0:128] = jnp.concatenate([cpt[:, 64:96].T, gpt.T], axis=0)
    g2 = tdot(qp, gpt) + tdot(qy, gyt) + tdot(qx, gxt)
    g_ref[:, 128:192] = jnp.concatenate([r[:, 64:96].T, g2.T], axis=0)
    kp = all_ref[640:768]
    extra = all_ref[512:640][:, 96:]
    kx = jnp.concatenate([extra[32:64], extra[64:96]], axis=1)
    b_ref[:, 0:128] = kp[:, :64].T
    b_ref[:, 128:192] = tdot(kp[:, :64], qp) + tdot(kp[:, 64:], qy) + tdot(kx, qx)


    for j, (src, dst) in enumerate(((g_ref, g_out), (c_ref, c_out), (b_ref, b_out))):
        copy = pltpu.make_async_copy(src, dst, small_sems.at[j])
        copy.start()
        copies.append(copy)
    for copy in copies:
        copy.wait()


def final(place, pieces, p, y, ay, ax, scale):
    rows, fields, width = p.shape
    steps = rows // DEPTH
    small = ((64, 192), (192, 192), (64, 192))
    return call(
        functools.partial(final_kernel, scale),
        tuple(
            pltpu.HBM(d, F32) for d in ((2 * B, rows, width), (B, rows, width)) + small
        ),
        [SM] + [VM] * 2 + [HBM] * 4,
        (HBM,) * 5,
        scratch=[pltpu.VMEM(p.shape, F32)] * 3
        + [
            pltpu.VMEM(ax.shape, F32),
            pltpu.VMEM((PACK, 128), F32),
            pltpu.VMEM((8, 8, 128), F32),
            pltpu.VMEM((steps, 2 * B, DEPTH, width), F32),
            pltpu.VMEM((steps, B, DEPTH, width), F32),
        ]
        + [pltpu.VMEM(d, F32) for d in small]
        + [pltpu.SemaphoreType.DMA(d) for d in ((4, rows // CHUNK), (2, steps), (3,))],
        flops=1 << 30,
        moved=5 * p.size * 4,
        limit=40,
    )(place, *pieces, *(in_hbm(a) for a in (p, y, ay, ax)))


def on_device(prior, cond_x, cond_y, cap_level, decap, via, ports):
    rows_here, cols_here = prior.shape[1:]
    total_cols = cols_here * lax.axis_size("gy")
    scale = 1.0 / (rows_here * lax.axis_size("gx") * total_cols)
    gxe = 0.125 * cond_x.astype(F32)
    gye = 0.125 * cond_y.astype(F32)
    gvia = 0.5 * via.astype(F32)
    cap = 0.25 * cap_level.astype(F32) * (1.0 + 2.0 * decap.astype(F32))

    core = (lax.axis_index("gx") % 2)[None]
    me = lax.axis_index("gy")
    p, mate, cross, edge = regroup(core, prior)
    slot = 2 * jnp.arange(rows_here)[:, None] == jnp.arange(cols_here)[None, :]
    gye_edge = jnp.sum(jnp.where(slot, gye[:, -1:], 0.0), axis=0, keepdims=True)
    spare = jnp.zeros((7, cols_here), F32)
    pair_row = jnp.where(core == 0, gxe[-1], 0.0)[None]
    cross_row = jnp.where(core == 0, 0.0, gxe[-1])[None]
    mate = jnp.concatenate([mate, pair_row, spare], axis=0)
    cross = jnp.concatenate([cross, cross_row, spare], axis=0)
    edge_more = jnp.concatenate([edge, gye_edge, spare], axis=0)
    mate, cross, fl, fr = exchange(mate, cross, edge_more, edge)
    gxw_first = mate[PRIOR : PRIOR + 1] + cross[PRIOR : PRIOR + 1]
    gxw = jnp.concatenate([gxw_first, gxe[:-1]], axis=0)
    gys_first = jnp.sum(jnp.where(slot, fl[PRIOR : PRIOR + 1], 0.0), axis=1, keepdims=True)
    gys = jnp.concatenate([gys_first, gye[:, :-1]], axis=1)
    center = gvia + gxe + gxw + gye + gys
    coef = jnp.stack([center, gxe, gxw, gye, gys, 1.0 / cap])

    port_rows = ports // total_cols - lax.axis_index("gx") * rows_here
    port_cols = ports % total_cols - lax.axis_index("gy") * cols_here
    inside = (
        (port_rows >= 0) & (port_rows < rows_here) & (port_cols >= 0) & (port_cols < cols_here)
    )
    where = jnp.stack(
        [
            jnp.clip(port_rows, 0, rows_here - 1),
            jnp.clip(port_cols, 0, cols_here - 1),
            inside.astype(jnp.int32),
        ]
    )
    y, y_far, p_in, *sends = stencil(core, coef, p, mate, cross, fl, fr, True)
    sides = exchange(*sends, sends[2])
    grams_y = gram_y(cap, p_in, y)
    ay, ay_far, mate, cross, edge = stencil(core, coef, y, *sides, False)
    ygy, xs, kp, kx = gram_x(where, cap, p_in, y, ay)
    cross = swap_cross(cross)
    place = jnp.concatenate([me[None], core])
    keep, give = pack(core, [*grams_y, ygy, xs, kp, kx], mate, cross)
    got = swap(give, "gx", 1)
    own, *sends = fan(place, keep, got, edge)
    quads = [own] + [swap(x, "gy", m) for m, x in zip((1, 2, 3), sends)]
    ax, x = last(place, coef, ay, got, cross, quads)
    pieces = sum_over_chips(x)
    basis, image, g_t, c, b_t = final(place, pieces, p, y_far, ay_far, ax, scale)
    return basis, image, g_t.T, c, b_t.T


def solution(mesh):
    in_specs = (
        P(None, "gx", "gy"),
        P("gx", "gy"),
        P("gx", "gy"),
        P("gx", "gy"),
        P("gx", "gy"),
        P("gx", "gy"),
        P(),
    )
    out_specs = (P(None, "gx", "gy"), P(None, "gx", "gy"), P(), P(), P())
    return jax.shard_map(
        on_device, mesh=mesh, in_specs=in_specs, out_specs=out_specs, check_vma=False
    )
```

```python
import functools

import jax
import jax.numpy as jnp
from jax import lax
from jax.experimental import pallas as pl
from jax.experimental.pallas import tpu as pltpu
from jax.sharding import PartitionSpec as P

B = 32
PRIOR = 128
F32 = jnp.float32
HI = lax.Precision.HIGHEST
MIB = 1024 * 1024
TILE = 32
CHUNK = 16
DEPTH = 8
PACK = 832
VM = pl.BlockSpec(memory_space=pltpu.VMEM)
SM = pl.BlockSpec(memory_space=pltpu.SMEM)
HBM = pl.BlockSpec(memory_space=pltpu.HBM)
ANY = pl.BlockSpec(memory_space=pl.ANY)


def call(kernel, out, in_specs, out_specs, scratch=(), flops=0, moved=0, limit=24, aliases={}):
    return pl.pallas_call(
        kernel,
        out_shape=out,
        in_specs=in_specs,
        out_specs=out_specs,
        scratch_shapes=scratch,
        input_output_aliases=aliases,
        compiler_params=pltpu.CompilerParams(vmem_limit_bytes=limit * MIB),
        cost_estimate=pl.CostEstimate(flops=flops, bytes_accessed=moved, transcendentals=0),
    )


def shape(*dims):
    return jax.ShapeDtypeStruct(dims, F32)


def held(*dims):
    return pltpu.VMEM(dims, F32)


def in_hbm(x):
    return pltpu.with_memory_space_constraint(x, pltpu.HBM)


def lanes_of(dims):
    return lax.broadcasted_iota(jnp.int32, dims, len(dims) - 1)


def pack_edges(v_ref, edge_ref, skip=0):
    rows, fields, width = v_ref.shape
    slot = lanes_of((TILE, width)) >> 1
    for at in range(skip, fields, TILE):
        edge = jnp.zeros((TILE, width), F32)
        for r in range(rows):
            edge = jnp.where(
                slot == r, pltpu.roll(v_ref[r, at : at + TILE, :], 2 * r + 1, 1), edge
            )
        edge_ref[at - skip : at - skip + TILE] = edge


def ends(core, v_ref, mate_ref, cross_ref, first=0):
    top = v_ref[0, first:, :]
    low = v_ref[v_ref.shape[0] - 1, first:, :]
    mate_ref[...] = jnp.where(core == 0, low, top)
    cross_ref[...] = jnp.where(core == 0, top, low)


def regroup_kernel(
    core_ref, p_ref, out_hbm, mate_ref, cross_ref, edge_ref, buf_ref, out_ref, sems
):
    parts, fields, rows, width = buf_ref.shape
    copies = [
        pltpu.make_async_copy(p_ref.at[pl.ds(i * fields, fields)], buf_ref.at[i], sems.at[0, i])
        for i in range(parts)
    ]
    back = []
    for copy in copies:
        copy.start()
    for i in range(parts):
        copies[i].wait()
        cut = slice(i * fields, (i + 1) * fields)
        for at in range(0, rows, DEPTH):
            flat = buf_ref.at[i].reshape(fields * rows, width)
            got = [flat[pl.ds(at + k, fields, stride=rows), :] for k in range(DEPTH)]
            for k in range(DEPTH):
                out_ref[at + k, cut, :] = got[k]
        held_part = (slice(None), pl.ds(i * fields, fields), slice(None))
        back.append(
            pltpu.make_async_copy(out_ref.at[held_part], out_hbm.at[held_part], sems.at[1, i])
        )
        back[-1].start()
    pack_edges(out_ref, edge_ref)
    ends(core_ref[0], out_ref, mate_ref, cross_ref)
    for copy in back:
        copy.wait()


def regroup(core, prior):
    fields, rows, width = prior.shape
    parts = fields // CHUNK
    return call(
        regroup_kernel,
        (pltpu.HBM((rows, fields, width), F32),) + (shape(fields, width),) * 3,
        [SM, HBM],
        (HBM,) + (VM,) * 3,
        scratch=[
            pltpu.VMEM((parts, CHUNK, rows, width), F32),
            pltpu.VMEM((rows, fields, width), F32),
            pltpu.SemaphoreType.DMA((2, parts)),
        ],
        moved=2 * prior.size * 4,
        limit=40,
    )(core, in_hbm(prior))


def stencil_rows(
    core, coef_ref, v_ref, first, mate, cross, from_left, from_right, seam_ref, put, ready=None
):
    rows, width = v_ref.shape[0], v_ref.shape[2]
    fields = seam_ref.shape[0]
    tile = 8
    lane = lanes_of((tile, width))
    odd, start, stop = (lane & 1) == 1, lane == 0, lane == width - 1
    for at in range(0, fields, tile):
        cut = slice(at, at + tile)
        seam_ref[cut] = jnp.where(
            odd, pltpu.roll(from_left(cut), 1, 1), pltpu.roll(from_right(cut), width - 1, 1)
        )
    for r in range(rows):
        if ready is not None:
            ready(r)
        c = [jnp.broadcast_to(coef_ref[k, r : r + 1, :], (tile, width)) for k in range(6)]
        for at in range(0, fields, tile):
            cut = slice(at, at + tile)
            src = slice(first + at, first + at + tile)
            v = v_ref[r, src, :]
            if r == 0:
                up = jnp.where(core == 0, cross(cut), mate(cut))
            else:
                up = v_ref[r - 1, src, :]
            if r == rows - 1:
                down = jnp.where(core == 0, mate(cut), cross(cut))
            else:
                down = v_ref[r + 1, src, :]
            side = pltpu.roll(seam_ref[cut], width - 1 - 2 * r, 1)
            south = jnp.where(start, side, pltpu.roll(v, 1, 1))
            north = jnp.where(stop, side, pltpu.roll(v, width - 1, 1))
            put(r, cut, c[0] * v - c[1] * down - c[2] * up - c[3] * north - c[4] * south, c[5])


def reader(ref, at=0):
    return lambda cut: ref[at + cut.start : at + cut.stop, :]


def stencil_kernel(
    first, core_ref, coef_ref, in_ref, mate_ref, cross_ref, fl_ref, fr_ref, y_ref, y_hbm, *rest
):
    if first:
        v_ref, mate_out, cross_out, edge_ref, seam_ref, out_sems, in_sems = rest
    else:
        mate_out, cross_out, edge_ref, seam_ref, out_sems = rest
        v_ref = in_ref
    rows = v_ref.shape[0]
    parts = [pl.ds(i * CHUNK, CHUNK) for i in range(rows // CHUNK)]
    loads, stores = [], []
    if first:
        for i, part in enumerate(parts):
            loads.append(pltpu.make_async_copy(in_ref.at[part], v_ref.at[part], in_sems.at[i]))
            loads[-1].start()

    def store(i):
        stores.append(
            pltpu.make_async_copy(y_ref.at[parts[i]], y_hbm.at[parts[i]], out_sems.at[i])
        )
        stores[-1].start()

    def ready(r):
        if first and r == 0:
            loads[0].wait()
        if first and r % CHUNK == CHUNK - 1 and r + 1 < rows:
            loads[r // CHUNK + 1].wait()
        if r % CHUNK == 0 and r > 0:
            store(r // CHUNK - 1)

    def put(r, cut, image, inv_cap):
        y_ref[r, cut, :] = image * inv_cap

    stencil_rows(
        core_ref[0], coef_ref, v_ref, 0, reader(mate_ref), reader(cross_ref), reader(fl_ref),
        reader(fr_ref), seam_ref, put, ready,
    )
    store(len(parts) - 1)
    skip = y_ref.shape[1] - edge_ref.shape[0]
    pack_edges(y_ref, edge_ref, skip)
    ends(core_ref[0], y_ref, mate_out, cross_out, skip)
    for copy in stores:
        copy.wait()


def stencil(core, coef, v, mate, cross, from_left, from_right, first):
    rows, fields, width = v.shape
    send = shape(fields if first else B, width)
    field = held(rows, fields, width)
    sems = pltpu.SemaphoreType.DMA((rows // CHUNK,))
    return call(
        functools.partial(stencil_kernel, first),
        (field, pltpu.HBM((rows, fields, width), F32)) + (field,) * first + (send,) * 3,
        [SM, VM, HBM if first else VM] + [VM] * 4,
        (VM, HBM) + (VM,) * first + (VM,) * 3,
        scratch=[pltpu.VMEM((fields, width), F32), sems] + [sems] * first,
        flops=12 * v.size,
        moved=2 * v.size * 4,
    )(core, coef, in_hbm(v) if first else v, mate, cross, from_left, from_right)


def wide(ref, at):
    return jnp.concatenate([ref[at + i] for i in range(CHUNK)], axis=1)


def wide_row(ref, at):
    return jnp.concatenate([ref[pl.ds(at + i, 1), :] for i in range(CHUNK)], axis=1)


def halves(x):
    high = x.astype(jnp.bfloat16)
    low = (x - high.astype(F32)).astype(jnp.bfloat16)
    return jnp.concatenate([high, low], axis=0)


def nt(a, b):
    return lax.dot_general(a, b, (((1,), (1,)), ((), ())), preferred_element_type=F32)


def fold(acc, row, rows, col, cols):
    a = acc[row : row + rows, col : col + cols] + acc[row : row + rows, col + cols : col + 2 * cols]
    row += rows
    b = acc[row : row + rows, col : col + cols] + acc[row : row + rows, col + cols : col + 2 * cols]
    return a + b


def over_chunks(rows, accs, terms):
    def add(i, carry):
        for acc, term in zip(accs, terms(i * CHUNK)):
            acc[...] += term
        return carry

    for acc in accs:
        acc[...] = jnp.zeros_like(acc)
    lax.fori_loop(0, rows // CHUNK, add, 0)


def gram_y_kernel(
    cap_ref, p_ref, y_ref, pp_ref, pcp_ref, py_ref, yy_ref, pgp_ref, ygp_ref, accp_ref, accy_ref
):
    def terms(at):
        p, y, cap = wide(p_ref, at), wide(y_ref, at), wide_row(cap_ref, at)
        hp, hy, hg = halves(p), halves(y), halves(y * cap)
        right = jnp.concatenate([hy, hg], axis=0)
        yield nt(hp, jnp.concatenate([right, hp, halves(p * cap)], axis=0))
        yield nt(hy, right)

    over_chunks(p_ref.shape[0], (accp_ref, accy_ref), terms)
    py_ref[...] = fold(accp_ref, 0, 128, 0, 128)
    pgp_ref[...] = fold(accp_ref, 0, 128, 256, 128)
    pp_ref[...] = fold(accp_ref, 0, 128, 512, 128)
    pcp_ref[...] = fold(accp_ref, 0, 128, 768, 128)
    yy_ref[...] = fold(accy_ref, 0, 128, 0, 128)
    ygp_ref[...] = fold(accy_ref, 0, 128, 256, 128)


def gram_x_kernel(
    where_ref, cap_ref, p_ref, y_ref, a_ref, ygy_ref, x_ref, kp_ref, kx_ref, acc_ref, accx_ref
):
    def terms(at):
        ay = wide(a_ref, at)
        hp, hy = halves(wide(p_ref, at)), halves(wide(y_ref, at))
        hg = halves(ay * wide_row(cap_ref, at))
        hx = halves(ay[PRIOR - B :])
        yield nt(hy, hg)
        yield nt(jnp.concatenate([hp, hy, hg, hx], axis=0), hx)

    over_chunks(p_ref.shape[0], (acc_ref, accx_ref), terms)
    ygy_ref[...] = fold(acc_ref, 0, 128, 0, 128)
    px = fold(accx_ref, 0, 128, 0, B)
    yx = fold(accx_ref, 256, 128, 0, B)
    gx = fold(accx_ref, 512, 128, 0, B)
    xx = fold(accx_ref, 768, B, 0, B)
    rest = jnp.concatenate([xx, jnp.zeros((128 - B, B), F32)], axis=0)
    x_ref[...] = jnp.concatenate([px, yx, gx, rest], axis=1)

    kp_ref[...] = jnp.zeros_like(kp_ref)
    kx_ref[...] = jnp.zeros_like(kx_ref)
    n = where_ref.shape[1]

    def step(k, carry):
        @pl.when(where_ref[2, k] > 0)
        def _():
            r, c = where_ref[0, k], where_ref[1, k]
            for v, spot, out_ref in (
                (p_ref[r], k, kp_ref),
                (y_ref[r], k + n, kp_ref),
                (a_ref[r][PRIOR - B :], k, kx_ref),
            ):
                moved = pltpu.roll(v, lax.rem(spot - c + 128, 128), 1)
                out_ref[...] = jnp.where(lanes_of(v.shape) == spot, moved, out_ref[...])

        return carry

    lax.fori_loop(0, n, step, 0)


def gram_y(cap, p, y):
    return call(
        gram_y_kernel,
        (shape(128, 128),) * 6,
        [VM] * 3,
        (VM,) * 6,
        scratch=[pltpu.VMEM((256, 1024), F32), pltpu.VMEM((256, 512), F32)],
        flops=6 * 2 * 256 * 256 * p.shape[0] * 128,
        moved=2 * p.size * 4,
    )(cap, p, y)


def gram_x(where, cap, p, y, ay):
    return call(
        gram_x_kernel,
        (shape(128, 128),) * 3 + (shape(B, 128),),
        [SM] + [VM] * 4,
        (VM,) * 4,
        scratch=[pltpu.VMEM((256, 256), F32), pltpu.VMEM((832, 64), F32)],
        flops=4 * 2 * 256 * 256 * p.shape[0] * 128,
        moved=3 * p.size * 4,
    )(where, cap, p, y, ay)


def pack_kernel(
    core_ref, pp_ref, pcp_ref, py_ref, yy_ref, pgp_ref, ygp_ref, ygy_ref, x_ref, kp_ref, kx_ref,
    mate_ref, cross_ref, keep_ref, give_ref, pack_ref,
):
    row = lax.broadcasted_iota(jnp.int32, (128, 128), 0)
    col = lax.broadcasted_iota(jnp.int32, (128, 128), 1)

    def diagonal(m):
        return jnp.sum(jnp.where(row == col, m, 0.0), axis=0, keepdims=True)

    pack_ref[0:128] = jnp.where(row <= col, pp_ref[...], pcp_ref[...])
    pack_ref[128:256] = jnp.where(row <= col, pgp_ref[...], ygy_ref[...])
    pack_ref[256:384] = jnp.where(row <= col, yy_ref[...], ygp_ref[...])
    pack_ref[384:512] = py_ref[...]
    kx, zero = kx_ref[...], jnp.zeros((B, B), F32)
    extra = jnp.concatenate([zero, kx[:, :B], kx[:, B : 2 * B], zero], axis=0)
    pack_ref[512:640] = x_ref[...] + jnp.concatenate([jnp.zeros((128, 96), F32), extra], axis=1)
    pack_ref[640:768] = kp_ref[...]
    diag = [diagonal(m[...]) for m in (pcp_ref, ygy_ref, ygp_ref)]
    pack_ref[768:776] = jnp.concatenate(diag + [jnp.zeros((5, 128), F32)], axis=0)
    pack_ref[776:832] = jnp.zeros((56, 128), F32)
    half = PACK // 2
    core = core_ref[0]
    keep_ref[...] = pack_ref[pl.ds(pl.multiple_of(core * half, 8), half), :]
    give_ref[0:half] = pack_ref[pl.ds(pl.multiple_of((1 - core) * half, 8), half), :]
    give_ref[half : half + B] = mate_ref[...]


def pack(core, mats, mate, cross):
    return call(
        pack_kernel,
        (shape(PACK // 2, 128), shape(PACK // 2 + B, 128)),
        [SM] + [VM] * (1 + len(mats)) + [ANY],
        (VM,) * 2,
        scratch=[pltpu.VMEM((PACK, 128), F32)],
        moved=1 << 20,
    )(core, *mats, mate, cross)


def fan_kernel(place_ref, keep_ref, got_ref, edge_ref, own_ref, s1_ref, s2_ref, s3_ref, sum_ref):
    half, quarter = PACK // 2, PACK // 8
    sum_ref[...] = keep_ref[...] + got_ref[0:half]
    for m, ref in enumerate((own_ref, s1_ref, s2_ref, s3_ref)):
        at = pl.multiple_of((place_ref[0] ^ m) * quarter, 8)
        ref[0:quarter] = sum_ref[pl.ds(at, quarter), :]
    s1_ref[quarter:] = edge_ref[...]
    s3_ref[quarter:] = edge_ref[...]


def fan(place, keep, got, edge):
    quarter = PACK // 8
    return call(
        fan_kernel,
        tuple(shape(quarter + extra, 128) for extra in (0, B, 0, B)),
        [SM] + [VM] * 3,
        (VM,) * 4,
        scratch=[pltpu.VMEM((PACK // 2, 128), F32)],
        moved=1 << 20,
    )(place, keep, got, edge)


def last_kernel(
    place_ref, coef_ref, a_ref, mate_ref, cross_ref, own_ref, g1_ref, g2_ref, g3_ref,
    ax_hbm, sum_ref, ax_ref, image_ref, seam_ref, sem,
):
    me, core = place_ref[0], place_ref[1]
    quarter = PACK // 8

    def put(r, cut, image, inv_cap):
        ax_ref[r, cut, :] = image * inv_cap
        image_ref[r, cut, :] = image

    near, far = reader(g1_ref, quarter), reader(g3_ref, quarter)

    def from_left(cut):
        other = jnp.where(me == 2, far(cut), 0.0)
        return jnp.where(me % 2 == 1, near(cut), other)

    def from_right(cut):
        other = jnp.where(me == 1, far(cut), 0.0)
        return jnp.where(me % 2 == 0, near(cut), other)

    stencil_rows(
        core, coef_ref, a_ref, PRIOR - B, reader(mate_ref, PACK // 2), reader(cross_ref),
        from_left, from_right, seam_ref, put,
    )
    copy = pltpu.make_async_copy(ax_ref, ax_hbm, sem)
    copy.start()
    sum_ref[0:quarter] = (own_ref[...] + g1_ref[0:quarter]) + (g2_ref[...] + g3_ref[0:quarter])
    acc = jnp.zeros((2 * B, 2 * B), F32)
    for at in range(0, a_ref.shape[0], CHUNK):
        hx = halves(wide(a_ref, at)[PRIOR - B :])
        acc = acc + nt(hx, halves(wide(image_ref, at)))
    xgx = fold(acc, 0, B, 0, B)
    sum_ref[quarter:] = jnp.concatenate([xgx[8 * k : 8 * k + 8] for k in range(4)], axis=1)
    copy.wait()


def last(place, coef, ay, mate, cross, quads):
    rows, fields, width = ay.shape
    return call(
        last_kernel,
        (pltpu.HBM((rows, B, width), F32), shape(PACK // 8 + 8, 128)),
        [SM] + [VM] * 8,
        (HBM, VM),
        scratch=[
            pltpu.VMEM((rows, B, width), F32),
            pltpu.VMEM((rows, B, width), F32),
            pltpu.VMEM((B, width), F32),
            pltpu.SemaphoreType.DMA,
        ],
        flops=1 << 27,
        moved=2 * rows * B * width * 4,
    )(place, coef, ay, mate, cross, *quads)


def split(x):
    high = x.astype(jnp.bfloat16)
    return high, (x - high.astype(F32)).astype(jnp.bfloat16)


def times(t, pair):
    rows = t.shape[0] // 2
    big = jnp.dot(t, pair[0], preferred_element_type=F32)
    return big[:rows] + big[rows:] + jnp.dot(t[:rows], pair[1], preferred_element_type=F32)


def combine(t, p_ref, y_ref, a_ref, ax_ref, q_ref, n_ref, qbuf_ref, nbuf_ref, sems, ready):
    two = 2 * B
    high, low = split(t)

    def cut(lo, hi, first):
        return jnp.concatenate([high[first:, lo:hi], low[first:, lo:hi]], axis=0)

    t_py, t_x, t_y, t_rest = cut(0, 256, 0), cut(256, 288, 0), cut(0, 128, B), cut(128, 288, B)
    rows, fields, width = p_ref.shape
    copies = []
    for at in range(0, rows, DEPTH):
        ready(at)

        def row_block(ref):
            return jnp.concatenate([ref[at + i] for i in range(DEPTH)], axis=1)

        p, y = split(row_block(p_ref)), split(row_block(y_ref))
        a, ax = split(row_block(a_ref)), split(row_block(ax_ref))
        py = tuple(jnp.concatenate(pair, axis=0) for pair in zip(p, y))
        rest = tuple(jnp.concatenate(pair, axis=0) for pair in zip(a, ax))
        x = tuple(part[PRIOR - B :] for part in a)
        q = times(t_py, py) + times(t_x, x)
        n = times(t_y, y) + times(t_rest, rest)
        step = at // DEPTH
        for k in range(DEPTH):
            lanes = slice(k * width, (k + 1) * width)
            qbuf_ref.at[step].reshape(two * DEPTH, width)[pl.ds(k, two, stride=DEPTH), :] = q[
                :, lanes
            ]
            nbuf_ref.at[step].reshape(B * DEPTH, width)[pl.ds(k, B, stride=DEPTH), :] = n[
                :, lanes
            ]
        for j, (src, dst) in enumerate(((qbuf_ref, q_ref), (nbuf_ref, n_ref))):
            copy = pltpu.make_async_copy(
                src.at[step], dst.at[:, pl.ds(at, DEPTH), :], sems.at[j, step]
            )
            copy.start()
            copies.append(copy)
    return copies


def swap(x, axis, mask):
    return lax.ppermute(x, axis, [(i, i ^ mask) for i in range(lax.axis_size(axis))])


def shift(x, axis, step):
    size = lax.axis_size(axis)
    return lax.ppermute(
        x, axis, [(i, i + step) for i in range(size) if 0 <= i + step < size]
    )


def swap_cross(x):
    size = lax.axis_size("gx")
    pairs = [(i, i + 1) for i in range(1, size - 1, 2)]
    return lax.ppermute(x, "gx", pairs + [(j, i) for i, j in pairs])


def sum_over_chips(x):
    mask = 2
    while mask < lax.axis_size("gx"):
        x = x + swap(x, "gx", mask)
        mask *= 2
    x = jnp.concatenate([x, swap(x, "gx", 1)], axis=0)
    return [x] + [swap(x, "gy", m) for m in (1, 2, 3)]


def exchange(mate, cross, edge, edge_left):
    return swap(mate, "gx", 1), swap_cross(cross), shift(edge, "gy", 1), shift(edge_left, "gy", -1)


def dot(a, b):
    return jnp.dot(a, b, precision=HI, preferred_element_type=F32)


def tdot(a, b):
    return lax.dot_general(
        a, b, (((0,), (0,)), ((), ())), precision=HI, preferred_element_type=F32
    )


def inverse_factor(s):
    n = s.shape[0]
    s = 0.5 * (s + s.T)
    row = lax.broadcasted_iota(jnp.int32, (n, 128), 0)
    lane = lax.broadcasted_iota(jnp.int32, (n, 128), 1)
    eye = jnp.where(row + n == lane, 1.0, 0.0)
    a = jnp.concatenate([s, jnp.zeros((n, 128 - n), F32)], axis=1) + eye
    for j in range(0, n, 2):
        one = jnp.broadcast_to(a[:, j : j + 1], (n, 128))
        two = jnp.broadcast_to(a[:, j + 1 : j + 2], (n, 128))
        inv = 1.0 / one[j : j + 1]
        step = one[j + 1 : j + 2] * inv
        head = a[j : j + 1]
        tail = a[j + 1 : j + 2] - step * head
        left = one * inv
        two = two - left * two[j : j + 1]
        right = two * (1.0 / two[j + 1 : j + 2])
        below = a - left * head - right * tail
        a = jnp.where(row > j + 1, below, jnp.where(row == j + 1, tail, a))
    diag = jnp.sum(jnp.where(row == lane, a, 0.0), axis=1, keepdims=True)
    return (a / jnp.sqrt(diag))[:, n : 2 * n]


def final_kernel(
    scale, place_ref, b0_ref, b1_ref, b2_ref, b3_ref, p_hbm, y_hbm, a_hbm, ax_hbm,
    q_ref, n_ref, g_out, c_out, b_out, p_ref, y_ref, a_ref, ax_ref, all_ref, xgx_ref, qbuf_ref,
    nbuf_ref, g_ref, c_ref, b_ref, load_sems, sems, small_sems,
):
    pairs = ((p_hbm, p_ref), (y_hbm, y_ref), (a_hbm, a_ref), (ax_hbm, ax_ref))
    loads = []
    for i in range(p_ref.shape[0] // CHUNK):
        part = pl.ds(i * CHUNK, CHUNK)
        for j, (src, dst) in enumerate(pairs):
            loads.append(
                pltpu.make_async_copy(src.at[part], dst.at[part], load_sems.at[j, i])
            )
            loads[-1].start()

    def ready(at):
        if at % CHUNK == 0:
            for load in loads[at // CHUNK * 4 : at // CHUNK * 4 + 4]:
                load.wait()

    me, core = place_ref[0], place_ref[1]
    quarter = PACK // 8
    for m, ref in enumerate((b0_ref, b1_ref, b2_ref, b3_ref)):
        for h in (0, 1):
            at = (core ^ h) * 4 + (me ^ m)
            lo = h * (quarter + 8)
            all_ref[pl.ds(pl.multiple_of(at * quarter, 8), quarter), :] = ref[lo : lo + quarter]
            xgx_ref[at] = ref[lo + quarter : lo + quarter + 8]
    row = lax.broadcasted_iota(jnp.int32, (128, 128), 0)
    col = lax.broadcasted_iota(jnp.int32, (128, 128), 1)

    def pair(at, d):
        m = all_ref[at : at + 128] * scale
        t = m.T
        diag = all_ref[768 + d : 769 + d] * scale
        return (
            jnp.where(row <= col, m, t),
            jnp.where(row > col, m, jnp.where(row < col, t, diag)),
        )

    pp, pcp = pair(0, 0)
    pgp, ygy = pair(128, 1)
    yy, ycy = pair(256, 2)
    py = all_ref[384:512] * scale
    xs = all_ref[512:640] * scale
    px, yx, ygx = xs[:, :32], xs[:, 32:64], xs[:, 64:96]
    xx = xs[:32, 96:]
    total = xgx_ref[0]
    for k in range(1, 8):
        total = total + xgx_ref[k]
    total = total * scale
    xgx = jnp.concatenate([total[:, B * k : B * (k + 1)] for k in range(4)], axis=0)
    z = PRIOR - B

    h = py[:, z:]
    c = 2.0 * h - dot(pp, h)
    s = yy[z:, z:] + tdot(c, dot(pp, c) - 2.0 * h)
    inv_t = inverse_factor(s).T
    a, b = -dot(c, inv_t), inv_t

    hp = dot(py, a) + dot(px, b)
    wy = dot(yy, a) + dot(yx, b)
    wx = tdot(yx, a) + dot(xx, b)
    hq = tdot(a, hp) + tdot(b, wy[z:])
    kq = dot(pp, a) + dot(h, b)
    kqq = tdot(a, kq) + tdot(b, tdot(h, a) + dot(yy[z:, z:], b))
    cp = 2.0 * hp - dot(pp, hp) - dot(kq, hq)
    cq = 2.0 * hq - tdot(kq, hp) - dot(kqq, hq)
    s = (
        tdot(a, wy)
        + tdot(b, wx)
        + tdot(cp, dot(pp, cp) + dot(kq, cq) - 2.0 * hp)
        + tdot(cq, tdot(kq, cp) + dot(kqq, cq) - 2.0 * hq)
    )
    inv_t = inverse_factor(s).T
    zero_z = jnp.zeros((z, B), F32)
    u = -dot(cp + dot(a, cq), inv_t)
    v = dot(a - jnp.concatenate([zero_z, dot(b, cq)], axis=0), inv_t)
    x = dot(b, inv_t)

    zero = jnp.zeros((B, B), F32)
    tp = jnp.concatenate([a, u, jnp.zeros((128, B), F32)], axis=1)
    ty = jnp.concatenate([jnp.concatenate([zero_z, b], axis=0), v, a], axis=1)
    tx = jnp.concatenate([zero, x, b], axis=1)
    t = jnp.concatenate([m[:, :64].T for m in (tp, ty, tx)], axis=1)
    copies = combine(
        t, p_ref, y_ref, a_ref, ax_ref, q_ref, n_ref, qbuf_ref, nbuf_ref, sems, ready
    )

    pcx, ycx, xcx = ycy[:, z:], ygy[:, z:], ygx[z:]
    cpt = dot(pcp, tp) + dot(pgp, ty) + dot(pcx, tx)
    cyt = dot(pgp, tp) + dot(ycy, ty) + dot(ycx, tx)
    cxt = tdot(pcx, tp) + tdot(ycx, ty) + dot(xcx, tx)
    qp, qy, qx = tp[:, :64], ty[:, :64], tx[:, :64]
    r = tdot(qp, cpt) + tdot(qy, cyt) + tdot(qx, cxt)
    side = cpt[:, :64]
    c_ref[0:128, 0:128] = pcp
    c_ref[0:128, 128:192] = side
    c_ref[128:192, 0:128] = side.T
    c_ref[128:192, 128:192] = r[:, :64]
    gpt = cyt[:, 32:64]
    gyt = dot(ycy, u) + dot(ygy, v) + dot(ygx, x)
    gxt = tdot(ycx, u) + tdot(ygx, v) + dot(xgx, x)
    g_ref[:, 0:128] = jnp.concatenate([cpt[:, 64:96].T, gpt.T], axis=0)
    g2 = tdot(qp, gpt) + tdot(qy, gyt) + tdot(qx, gxt)
    g_ref[:, 128:192] = jnp.concatenate([r[:, 64:96].T, g2.T], axis=0)
    kp = all_ref[640:768]
    extra = all_ref[512:640][:, 96:]
    kx = jnp.concatenate([extra[32:64], extra[64:96]], axis=1)
    b_ref[:, 0:128] = kp[:, :64].T
    b_ref[:, 128:192] = tdot(kp[:, :64], qp) + tdot(kp[:, 64:], qy) + tdot(kx, qx)


    for j, (src, dst) in enumerate(((g_ref, g_out), (c_ref, c_out), (b_ref, b_out))):
        copy = pltpu.make_async_copy(src, dst, small_sems.at[j])
        copy.start()
        copies.append(copy)
    for copy in copies:
        copy.wait()


def final(place, pieces, p, y, ay, ax, scale):
    rows, fields, width = p.shape
    steps = rows // DEPTH
    small = ((64, 192), (192, 192), (64, 192))
    return call(
        functools.partial(final_kernel, scale),
        tuple(
            pltpu.HBM(d, F32) for d in ((2 * B, rows, width), (B, rows, width)) + small
        ),
        [SM] + [VM] * 4 + [HBM] * 4,
        (HBM,) * 5,
        scratch=[pltpu.VMEM(p.shape, F32)] * 3
        + [
            pltpu.VMEM(ax.shape, F32),
            pltpu.VMEM((PACK, 128), F32),
            pltpu.VMEM((8, 8, 128), F32),
            pltpu.VMEM((steps, 2 * B, DEPTH, width), F32),
            pltpu.VMEM((steps, B, DEPTH, width), F32),
        ]
        + [pltpu.VMEM(d, F32) for d in small]
        + [pltpu.SemaphoreType.DMA(d) for d in ((4, rows // CHUNK), (2, steps), (3,))],
        flops=1 << 30,
        moved=5 * p.size * 4,
        limit=40,
    )(place, *pieces, *(in_hbm(a) for a in (p, y, ay, ax)))


def on_device(prior, cond_x, cond_y, cap_level, decap, via, ports):
    rows_here, cols_here = prior.shape[1:]
    total_cols = cols_here * lax.axis_size("gy")
    scale = 1.0 / (rows_here * lax.axis_size("gx") * total_cols)
    gxe = 0.125 * cond_x.astype(F32)
    gye = 0.125 * cond_y.astype(F32)
    gvia = 0.5 * via.astype(F32)
    cap = 0.25 * cap_level.astype(F32) * (1.0 + 2.0 * decap.astype(F32))

    core = (lax.axis_index("gx") % 2)[None]
    me = lax.axis_index("gy")
    p, mate, cross, edge = regroup(core, prior)
    slot = 2 * jnp.arange(rows_here)[:, None] == jnp.arange(cols_here)[None, :]
    gye_edge = jnp.sum(jnp.where(slot, gye[:, -1:], 0.0), axis=0, keepdims=True)
    spare = jnp.zeros((7, cols_here), F32)
    pair_row = jnp.where(core == 0, gxe[-1], 0.0)[None]
    cross_row = jnp.where(core == 0, 0.0, gxe[-1])[None]
    mate = jnp.concatenate([mate, pair_row, spare], axis=0)
    cross = jnp.concatenate([cross, cross_row, spare], axis=0)
    edge_more = jnp.concatenate([edge, gye_edge, spare], axis=0)
    mate, cross, fl, fr = exchange(mate, cross, edge_more, edge)
    gxw_first = mate[PRIOR : PRIOR + 1] + cross[PRIOR : PRIOR + 1]
    gxw = jnp.concatenate([gxw_first, gxe[:-1]], axis=0)
    gys_first = jnp.sum(jnp.where(slot, fl[PRIOR : PRIOR + 1], 0.0), axis=1, keepdims=True)
    gys = jnp.concatenate([gys_first, gye[:, :-1]], axis=1)
    center = gvia + gxe + gxw + gye + gys
    coef = jnp.stack([center, gxe, gxw, gye, gys, 1.0 / cap])

    port_rows = ports // total_cols - lax.axis_index("gx") * rows_here
    port_cols = ports % total_cols - lax.axis_index("gy") * cols_here
    inside = (
        (port_rows >= 0) & (port_rows < rows_here) & (port_cols >= 0) & (port_cols < cols_here)
    )
    where = jnp.stack(
        [
            jnp.clip(port_rows, 0, rows_here - 1),
            jnp.clip(port_cols, 0, cols_here - 1),
            inside.astype(jnp.int32),
        ]
    )
    y, y_far, p_in, *sends = stencil(core, coef, p, mate, cross, fl, fr, True)
    sides = exchange(*sends, sends[2])
    grams_y = gram_y(cap, p_in, y)
    ay, ay_far, mate, cross, edge = stencil(core, coef, y, *sides, False)
    ygy, xs, kp, kx = gram_x(where, cap, p_in, y, ay)
    cross = swap_cross(cross)
    place = jnp.concatenate([me[None], core])
    keep, give = pack(core, [*grams_y, ygy, xs, kp, kx], mate, cross)
    got = swap(give, "gx", 1)
    own, *sends = fan(place, keep, got, edge)
    quads = [own] + [swap(x, "gy", m) for m, x in zip((1, 2, 3), sends)]
    ax, x = last(place, coef, ay, got, cross, quads)
    pieces = sum_over_chips(x)
    basis, image, g_t, c, b_t = final(place, pieces, p, y_far, ay_far, ax, scale)
    return basis, image, g_t.T, c, b_t.T


def solution(mesh):
    in_specs = (
        P(None, "gx", "gy"),
        P("gx", "gy"),
        P("gx", "gy"),
        P("gx", "gy"),
        P("gx", "gy"),
        P("gx", "gy"),
        P(),
    )
    out_specs = (P(None, "gx", "gy"), P(None, "gx", "gy"), P(), P(), P())
    return jax.shard_map(
        on_device, mesh=mesh, in_specs=in_specs, out_specs=out_specs, check_vma=False
    )
```
